32 devices in a mesh: pipe: 2 (over x), expert: 16 (over z, y, core).
Axes of the slice: x: 2, y: 2, z: 4, core: 2. Of those that a mesh axis runs over, the one named last changes fastest.
Arguments:
- hidden_a: bfloat16 [16, 768, 2048], P('expert'), may hold values from -6 to 6
- expert_weights: bfloat16 [16, 2048, 7168], P('expert', None, 'pipe'), may hold values from -0.125 to 0.125
- routes_a: int32 [1024, 8], P('expert'), may hold values from 0 to 15, all different within a row; in each aligned block of 64 rows (0 to 63, 64 to 127, ...) at most 48 rows name the same one
- gates_a: float32 [1024, 8], P('expert'), may hold values from 0.05 to 0.6
- cotangent_b: bfloat16 [1024, 7168], P('expert', 'pipe'), may hold values from -6 to 6
- routes_b: int32 [1024, 8], P('expert'), may hold values from 0 to 15, all different within a row; in each aligned block of 64 rows (0 to 63, 64 to 127, ...) at most 48 rows name the same one
- gates_b: float32 [1024, 8], P('expert'), may hold values from 0.05 to 0.6
Outputs:
- mixed_a: bfloat16 [1024, 7168], P('expert', 'pipe')
- grad_hidden_b: bfloat16 [16, 768, 2048], P('expert', None, 'pipe')
The draws below stay inside these ranges and needn't reach their ends.
Inputs may be any that keep to these rules, and one draw needn't show every extreme that they name: `routes_a`: among the tokens of one index of expert (aligned blocks of 64 rows), no expert is chosen more than 48 times, a bound that some block reaches; the 8 experts of a token differ. `routes_b`: among the tokens of one index of expert (aligned blocks of 64 rows), no expert is chosen more than 48 times, a bound that some block reaches; the 8 experts of a token differ.
All inputs are finite; a program needn't handle non-finite values.
Results may differ from the reference program's by a relative error of at most 0.019.
Values may be sent and summed in bfloat16 or wider, within the bound.
No kernel may reach another device: no remote copies, remote signals or barrier semaphores. Data moves between devices by JAX's collectives and lax.ppermute only.
A program may use at most 128 MiB of HBM per device.

```python
import math
import jax
import jax.numpy as jnp
import numpy as np
from jax import lax

D = 7168
FF = 2048
TOP = 8
TOK_DEV = 64
EXPERTS = 16
CAP = 48
SLOTS = 768
TOKENS = 1024
N_PIPE = 2
N_EXPERT = 16


def levels(key, dims, pieces, least, largest):
    factor_of = 1.0
    for dim, parts in pieces:
        steps = jax.random.uniform(jax.random.fold_in(jax.random.fold_in(key, 6), dim), (parts,), jnp.float32, least / len(pieces), largest / len(pieces))
        factor_of = factor_of * jnp.repeat(jnp.exp(steps), dims[dim] // parts).reshape((-1,) + (1,) * (len(dims) - 1 - dim))
    return factor_of


def routed_block(key, own, number, rows, number_of, top, most, lean):
    sequence = jax.random.permutation(key, number_of)
    crowded, common = load_shares(number_of, rows * top, most, lean, True), load_shares(number_of, rows * top, most, lean, False)
    places = jnp.arange(number_of)

    def named(lengths, rotation):
        used = int((lengths > 0).sum())
        fixed = max(1, used // 4)
        moved = fixed + (places - fixed + rotation * (used - fixed)) % max(1, number_of - fixed)
        return jnp.zeros((number_of,), jnp.int32).at[sequence[jnp.where(places < fixed, places, moved)]].set(jnp.asarray(lengths, jnp.int32))

    lengths = jnp.where(number % 4 == 0, named(crowded, number // 4), named(common, number - number // 4 - 1))
    mixed = jax.random.permutation(jax.random.fold_in(own, 3), number_of)
    source_of, taker = mixed[0:number_of // 2 * 2:2], mixed[1:number_of // 2 * 2:2]
    margin = jnp.minimum(lengths[source_of] - 1, most - lengths[taker]) // 2
    margin = jnp.where((source_of == sequence[0]) | (taker == sequence[0]) | (lengths[taker] == 0), 0, jnp.maximum(margin, 0))
    moved = jax.random.randint(jax.random.fold_in(own, 4), (number_of // 2,), 0, 1 << 20) % (margin + 1)
    lengths = lengths.at[source_of].add(-moved).at[taker].add(moved)
    members = jnp.searchsorted(jnp.cumsum(lengths), jnp.arange(rows * top), side="right").astype(jnp.int32)
    listing = members.reshape(top, rows).T
    listing = listing[jax.random.permutation(jax.random.fold_in(own, 1), rows)]
    rotation = jax.random.randint(jax.random.fold_in(own, 2), (rows, 1), 0, top)
    return jnp.take_along_axis(listing, (jnp.arange(top)[None, :] + rotation) % top, axis=1)


def load_shares(number_of, total, limit, lean, full):
    portions = [(1 << 20) // math.isqrt(standing ** lean) + 1 for standing in range(1, number_of + 1)]
    largest = limit if full else min(limit, max(-(-total // number_of), total * portions[0] // sum(portions)))
    least = 1 if total - largest >= number_of - 1 else 0
    holding, surplus = [largest] + [least] * (number_of - 1), total - largest - least * (number_of - 1)
    while surplus > 0:
        candidates = [i for i in range(1, number_of) if holding[i] < largest] or [i for i in range(1, number_of) if holding[i] < limit]
        mass, budget = sum([portions[i] for i in candidates]), surplus
        for i in candidates:
            extra = min(limit - holding[i], max(1, budget * portions[i] // mass), surplus)
            holding[i] = holding[i] + extra
            surplus = surplus - extra
    return np.array(holding)


def noise(own_key, extent, width, bound, split=(), kind=jnp.bfloat16):
    values = width * jax.random.normal(own_key, extent, jnp.float32)
    if split:
        values = values * levels(own_key, extent, split, -0.22, 0.18)
    return jnp.clip(values, -bound, bound).astype(kind)


def setup_inputs(seed: int = 0) -> dict:
    keys = jax.random.split(jax.random.key(seed), 8)
    hidden_a = noise(keys[0], (EXPERTS, SLOTS, FF), 1.0, 6.0, ((0, 16),))
    expert_weights = noise(keys[1], (EXPERTS, FF, D), FF ** -0.5, 0.125, ((0, 16), (2, 2)))
    routes_a_keys = jax.random.split(jax.random.fold_in(keys[2], 1), TOKENS // TOK_DEV)
    routes_a_turns = jax.random.permutation(jax.random.fold_in(keys[2], 3), TOKENS // TOK_DEV)
    routes_a = jax.vmap(lambda own, number: routed_block(jax.random.fold_in(keys[2], 2), own, number, TOK_DEV, EXPERTS, TOP, CAP, 2))(routes_a_keys, routes_a_turns).reshape((TOKENS, TOP))
    gates_a = jnp.clip(jnp.exp(math.log(0.6) - 2.4849067 * jax.random.uniform(keys[3], (TOKENS, TOP), jnp.float32) ** levels(keys[3], (TOKENS, TOP), ((0, 16),), -0.2, 0.2)), 0.05, 0.6)
    cotangent_b = noise(keys[4], (TOKENS, D), 1.0, 6.0, ((0, 16), (1, 2)))
    routes_b_keys = jax.random.split(jax.random.fold_in(keys[5], 1), TOKENS // TOK_DEV)
    routes_b_turns = jax.random.permutation(jax.random.fold_in(keys[5], 3), TOKENS // TOK_DEV)
    routes_b = jax.vmap(lambda own, number: routed_block(jax.random.fold_in(keys[5], 2), own, number, TOK_DEV, EXPERTS, TOP, CAP, 2))(routes_b_keys, routes_b_turns).reshape((TOKENS, TOP))
    gates_b = jnp.clip(jnp.exp(math.log(0.6) - 2.4849067 * jax.random.uniform(keys[6], (TOKENS, TOP), jnp.float32) ** levels(keys[6], (TOKENS, TOP), ((0, 16),), -0.2, 0.2)), 0.05, 0.6)
    return dict(hidden_a=hidden_a, expert_weights=expert_weights, routes_a=routes_a, gates_a=gates_a, cotangent_b=cotangent_b, routes_b=routes_b, gates_b=gates_b)


def slot_rows(routes):
    blocks = routes.reshape(N_EXPERT, TOK_DEV * TOP)
    onehot = (blocks[:, :, None] == jnp.arange(EXPERTS, dtype=jnp.int32)[None, None, :]).astype(jnp.int32)
    ranks = jnp.cumsum(onehot, axis=1) - onehot
    slots = jnp.sum(ranks * onehot, axis=2).reshape(N_EXPERT * TOK_DEV, TOP)
    source = (jnp.arange(N_EXPERT * TOK_DEV, dtype=jnp.int32) // TOK_DEV)[:, None]
    return routes * (N_EXPERT * CAP) + source * CAP + slots


def reference(hidden_a, expert_weights, routes_a, gates_a, cotangent_b, routes_b, gates_b):
    def forward_one(pair):
        return jnp.dot(pair[0], pair[1], preferred_element_type=jnp.float32).astype(jnp.bfloat16)

    expert_out = lax.map(forward_one, (hidden_a, expert_weights))
    index_a = slot_rows(routes_a)
    picked = expert_out.reshape(-1, D)[index_a]
    mixed_a = jnp.einsum('tk,tkd->td', gates_a.astype(jnp.float32), picked.astype(jnp.float32)).astype(jnp.bfloat16)
    index_b = slot_rows(routes_b)
    values = (gates_b[:, :, None] * cotangent_b[:, None, :].astype(jnp.float32)).astype(jnp.bfloat16)
    slot_grad = jnp.zeros((EXPERTS * N_EXPERT * CAP, D), jnp.bfloat16)
    slot_grad = slot_grad.at[index_b.reshape(-1)].set(values.reshape(-1, D))
    slot_grad = slot_grad.reshape(EXPERTS, N_EXPERT * CAP, D)

    def backward_one(pair):
        blocks_g = pair[0].reshape(N_EXPERT * CAP, N_PIPE, D // N_PIPE).astype(jnp.float32)
        blocks_w = pair[1].reshape(FF, N_PIPE, D // N_PIPE).astype(jnp.float32)
        partial_value = jnp.einsum('rpd,fpd->prf', blocks_g, blocks_w).astype(jnp.bfloat16)
        partial_value = lax.optimization_barrier(partial_value)
        return jnp.sum(partial_value.astype(jnp.float32), axis=0).astype(jnp.bfloat16)

    grad_hidden_b = lax.map(backward_one, (slot_grad, expert_weights))
    return mixed_a, grad_hidden_b
```

```python
import functools

import jax
import jax.numpy as jnp
from jax import lax
from jax.experimental import pallas as pl
from jax.experimental.pallas import tpu as pltpu
from jax.sharding import PartitionSpec as P

BF16, F32 = jnp.bfloat16, jnp.float32
TILE = 512
LANES = 128


def dense_gates(routes, gates, total):
    experts = jnp.arange(total, dtype=jnp.int32)[:, None, None]
    return jnp.sum(jnp.where(routes[None] == experts, gates[None], 0.0), axis=2)


def ranks_of(gate):
    tokens = gate.shape[-1]
    earlier = jnp.triu(jnp.ones((tokens, tokens), BF16), 1)
    counts = jnp.dot((gate > 0.0).astype(BF16), earlier, preferred_element_type=F32)
    return counts.astype(jnp.int32)


def add(*terms):
    total = terms[0].astype(F32)
    for term in terms[1:]:
        total = total + term.astype(F32)
    return total.astype(BF16)


def on_device_any(hidden_a, expert_weights, routes_a, gates_a, cotangent_b, routes_b, gates_b):
    groups = lax.axis_size("expert")
    me = lax.axis_index("expert")
    total = expert_weights.shape[0] * groups
    rows = hidden_a.shape[1]
    cap = rows // groups
    tokens, width = cotangent_b.shape
    weights = expert_weights[0]

    both = jnp.stack(
        [dense_gates(routes_a, gates_a, total), dense_gates(routes_b, gates_b, total)], axis=1
    )
    every = lax.all_gather(both, "expert", axis=0, tiled=False)
    own = lax.dynamic_index_in_dim(every, me, axis=1, keepdims=False)
    gathered = lax.all_gather(cotangent_b, "expert", axis=0, tiled=True)

    def placement(gate):
        slots = jnp.arange(cap, dtype=jnp.int32)[None, :, None]
        hit = (gate > 0.0)[:, None, :] & (ranks_of(gate)[:, None, :] == slots)
        return hit.astype(BF16), jnp.sum(jnp.where(hit, gate[:, None, :], 0.0), axis=2)

    hit_a, slot_gate_a = placement(own[:, 0])
    hit_b, slot_gate_b = placement(own[:, 1])

    outputs = jnp.einsum("rf,fd->rd", hidden_a[0], weights, preferred_element_type=F32)
    scaled = (outputs * slot_gate_a.reshape(rows, 1)).astype(BF16)
    spread = jnp.einsum(
        "sct,scd->std", hit_a, scaled.reshape(groups, cap, width), preferred_element_type=F32
    ).astype(BF16)
    mixed_a = lax.psum_scatter(
        spread.reshape(groups * tokens, width), "expert", scatter_dimension=0, tiled=True
    )
    picked = jnp.einsum(
        "sct,std->scd",
        hit_b,
        gathered.reshape(groups, tokens, width),
        preferred_element_type=F32,
    ).astype(BF16)
    partial_value = jnp.einsum(
        "rd,fd->rf", picked.reshape(rows, width), weights, preferred_element_type=F32
    )
    partial_value = (partial_value * slot_gate_b.reshape(rows, 1)).astype(BF16)
    grad = lax.psum_scatter(partial_value, "pipe", scatter_dimension=1, tiled=True)
    return (mixed_a, grad[None])


RING = [(0, 0), (1, 0), (2, 0), (3, 0), (3, 1), (2, 1), (1, 1), (0, 1)]


def step_ring(value, way):
    pairs = []
    for place, (z, y) in enumerate(RING):
        to_z, to_y = RING[(place + way) % 8]
        pairs += [(z * 4 + y * 2 + c, to_z * 4 + to_y * 2 + c) for c in range(2)]
    return lax.ppermute(value, "expert", pairs)


def xor(value, bits):
    return lax.ppermute(value, "expert", [(i, i ^ bits) for i in range(16)])


def core(value):
    return xor(value, 1)


def across(value):
    return lax.ppermute(value, "pipe", [(0, 1), (1, 0)])


def pin(value):
    return pltpu.with_memory_space_constraint(value, pltpu.HBM)


def tie(*values):
    return lax.optimization_barrier(values)


SMEM = pl.BlockSpec(memory_space=pltpu.SMEM)
VMEM = pl.BlockSpec(memory_space=pltpu.VMEM)
HBM = pl.BlockSpec(memory_space=pltpu.HBM)
ANY = pl.BlockSpec(memory_space=pl.ANY)


def kernel_call(kernel, name, inputs, out_shape, scratch, flops, moved):
    in_specs, arrays = zip(*inputs)
    return pl.pallas_call(
        kernel,
        in_specs=in_specs,
        out_specs=[VMEM] * len(out_shape),
        out_shape=out_shape,
        scratch_shapes=scratch,
        compiler_params=pltpu.CompilerParams(vmem_limit_bytes=20 * 2**20),
        cost_estimate=pl.CostEstimate(flops=flops, bytes_accessed=moved, transcendentals=0),
        name=name,
    )(*arrays)


def gates_kernel(*refs):
    sources, out, held, sems = refs[:4], refs[4], refs[5:9], refs[9]
    copies = [pltpu.make_async_copy(x, y, sems.at[i]) for i, (x, y) in enumerate(zip(sources, held))]
    for copy in copies:
        copy.start()
    for copy in copies:
        copy.wait()
    top, tokens = held[0].shape
    experts = lax.broadcasted_iota(jnp.int32, (out.shape[0], tokens), 0)
    for i in range(2):
        routes, gates = held[2 * i : 2 * i + 2]
        total = jnp.zeros(experts.shape, F32)
        for k in range(top):
            total += jnp.where(routes[k : k + 1, :] == experts, gates[k : k + 1, :], 0.0)
        out[:, pl.ds(i * tokens, tokens)] = total


def gates_of(*arrays):
    tokens, top = arrays[0].shape
    arrays = [pin(x.T) for x in arrays]
    return kernel_call(
        gates_kernel,
        "gates",
        [(HBM, x) for x in arrays],
        [jax.ShapeDtypeStruct((16, 2 * tokens), F32)],
        [pltpu.VMEM((top, tokens), x.dtype) for x in arrays] + [pltpu.SemaphoreType.DMA((4,))],
        flops=2**20,
        moved=2**17,
    )[0]


def place_slots(distances, where, gates, cap, target, place, slot_gates):
    gate = gates[...]
    tokens = gate.shape[1] // 2
    row = lax.broadcasted_iota(jnp.int32, (2 * tokens, 2 * tokens), 0)
    col = lax.broadcasted_iota(jnp.int32, (2 * tokens, 2 * tokens), 1)
    earlier = ((row < col) & (row // tokens == col // tokens)).astype(F32).astype(BF16)
    chosen = (gate > 0.0).astype(F32).astype(BF16)
    rank = jnp.dot(chosen, earlier, preferred_element_type=F32)
    second = (lax.broadcasted_iota(jnp.int32, gate.shape, 1) // tokens) ^ where[8]
    target[...] = jnp.where(gate > 0.0, rank + (second * cap).astype(F32), -1.0)
    slots = lax.broadcasted_iota(jnp.int32, (2 * cap, 2 * tokens), 0).astype(F32)
    for i, d in enumerate(distances):
        block = pl.ds(where[9 + d % 8], 1)
        hit = target[block, :] == slots
        place[i] = hit.astype(F32).astype(BF16)
        total = jnp.sum(jnp.where(hit, gates[block, :], 0.0), axis=1, keepdims=True)
        slot_gates[pl.ds(i * 2 * cap, 2 * cap), :] = jnp.broadcast_to(total, (2 * cap, LANES))


def place_scratch(count, gates, cap):
    return [
        pltpu.VMEM(gates.shape, F32),
        pltpu.VMEM((count, 2 * cap, gates.shape[1]), BF16),
        pltpu.VMEM((count * 2 * cap, LANES), F32),
    ]


def gated(value, slot_gates):
    factor = jnp.concatenate([slot_gates] * (value.shape[1] // LANES), axis=1)
    return (value * factor).astype(BF16)


class Stream:
    def __init__(self, tile, buffer, sems):
        self.tile, self.buffer, self.sems = tile, buffer, sems
        self.slots, self.parts = sems.shape

    def copies(self, n):
        slot = n % self.slots
        rows = self.buffer.shape[1] // self.parts
        source = self.tile(n)
        for part in range(self.parts):
            at = pl.ds(part * rows, rows)
            yield pltpu.make_async_copy(
                source.at[at, :], self.buffer.at[slot, at, :], self.sems.at[slot, part]
            )

    def start(self, n):
        for copy in self.copies(n):
            copy.start()

    def wait(self, n):
        for copy in self.copies(n):
            copy.wait()


def raw_kernel(first, hidden, weights, out, buffer, sems, staged, out_sems):
    tile, tiles = buffer.shape[2], out.shape[1] // buffer.shape[2]
    stream = Stream(
        lambda n: weights.at[:, pl.ds(pl.multiple_of(first + n * tile, tile), tile)], buffer, sems
    )
    for n in range(stream.slots):
        stream.start(n)

    def put(n):
        cols = pl.ds(pl.multiple_of(n * tile, tile), tile)
        return pltpu.make_async_copy(staged.at[n % 2], out.at[:, cols], out_sems.at[n % 2])

    @pl.loop(0, tiles)
    def _(n):
        stream.wait(n)

        @pl.when(n >= 2)
        def _():
            put(n - 2).wait()

        value = jnp.dot(hidden[...], buffer[n % stream.slots], preferred_element_type=F32)
        staged[n % 2] = value.astype(BF16)
        put(n).start()

        @pl.when(n + stream.slots < tiles)
        def _():
            stream.start(n + stream.slots)

    put(tiles - 2).wait()
    put(tiles - 1).wait()


def raw_forward(first, width, hidden, weights):
    rows, depth = hidden.shape
    return pl.pallas_call(
        functools.partial(raw_kernel, first),
        in_specs=[VMEM, HBM],
        out_specs=HBM,
        out_shape=pltpu.HBM((rows, width), BF16),
        scratch_shapes=[
            pltpu.VMEM((3, depth, 256), BF16),
            pltpu.SemaphoreType.DMA((3, 4)),
            pltpu.VMEM((2, rows, 256), BF16),
            pltpu.SemaphoreType.DMA((2,)),
        ],
        compiler_params=pltpu.CompilerParams(vmem_limit_bytes=20 * 2**20),
        cost_estimate=pl.CostEstimate(
            flops=2 * rows * depth * width,
            bytes_accessed=2 * (depth * width + rows * (depth + width)),
            transcendentals=0,
        ),
        name="raw_forward",
    )(hidden, weights)


def spread_kernel(distances, split, cap, where, gates, *refs):
    count = len(distances)
    raws, (keep, *others), scratch = refs[:2], refs[2:-6], refs[-6:]
    target, place, slot_gates, to_tokens, held, sems = scratch
    rows, half = 2 * cap, gates.shape[1] // 2
    width = raws[0].shape[1]
    fetch = []
    for i, d in enumerate(distances):
        start = pl.multiple_of(where[d % 8] * rows, rows)
        for j, raw in enumerate(raws):
            source = raw.at[pl.ds(start, rows), :]
            fetch.append(
                pltpu.make_async_copy(source, held.at[i, :, pl.ds(j * width, width)], sems.at[i, j])
            )
            fetch[-1].start()
    place_slots(distances, where, gates, cap, target, place, slot_gates)
    tokens = 2 * half
    same = lax.broadcasted_iota(jnp.int32, (tokens, tokens), 0) == lax.broadcasted_iota(
        jnp.int32, (tokens, tokens), 1
    )
    same = same.astype(F32).astype(BF16)
    for i in range(count):
        to_tokens[i] = lax.dot_general(
            same, place[i], (((1,), (1,)), ((), ())), preferred_element_type=F32
        ).astype(BF16)
    for copy in fetch:
        copy.wait()
    for g, other in enumerate(others):

        @pl.loop(0, split)
        def _(j):
            i = g * split + j
            for n in range(2 * width // TILE):
                cols = pl.ds(n * TILE, TILE)
                part = held[i, :, cols].astype(F32)
                part = gated(part, slot_gates[pl.ds(pl.multiple_of(i * rows, rows), rows), :])
                part = jnp.dot(to_tokens[i], part, preferred_element_type=F32).astype(BF16)
                keep[pl.ds(pl.multiple_of(i * half, half), half), cols] = part[:half]
                other[pl.ds(pl.multiple_of(j * half, half), half), cols] = part[half:]


def spread_tokens(distances, split, cap, where, gates, raws):
    count, half, width = len(distances), gates.shape[1] // 2, 2 * raws[0].shape[1]
    return kernel_call(
        functools.partial(spread_kernel, distances, split, cap),
        "spread_tokens",
        [(SMEM, where), (VMEM, gates), (HBM, raws[0]), (HBM, raws[1])],
        [jax.ShapeDtypeStruct((count * half, width), BF16)]
        + [jax.ShapeDtypeStruct((split * half, width), BF16)] * (count // split),
        [
            *place_scratch(count, gates, cap),
            pltpu.VMEM((count, 2 * half, 2 * cap), BF16),
            pltpu.VMEM((count, 2 * cap, width), BF16),
            pltpu.SemaphoreType.DMA((count, 2)),
        ],
        flops=count * 2**28,
        moved=count * 6 * half * width,
    )


def backward_kernel(distances, cap, sides, where, pipe, gates, weights, *refs):
    count, rows = len(distances), 2 * cap
    tokens, outs = refs[: 2 * count], refs[2 * count : 2 * count + len(sides)]
    block, block_sems, picked, target, place, slot_gates, buffer, sems = refs[
        2 * count + len(sides) :
    ]
    half, tile = tokens[0].shape[0], buffer.shape[1]
    tiles = 4 * len(sides)
    first = (1 - pipe[0] + sides[0]) * 4

    def weight_tile(n):
        return weights.at[pl.ds(pl.multiple_of((first + n) % 8 * tile, tile), tile), :]

    fetch = []
    for i, token in enumerate(tokens):
        to = block.at[i // 2, pl.ds(i % 2 * half, half), :]
        fetch.append(pltpu.make_async_copy(token, to, block_sems.at[i]))
        fetch[-1].start()
    stream = Stream(weight_tile, buffer, sems)
    for n in range(stream.slots):
        stream.start(n)
    place_slots(distances, where, gates, cap, target, place, slot_gates)
    for copy in fetch:
        copy.wait()

    @pl.loop(0, count)
    def _(i):
        for n in range(block.shape[2] // TILE):
            cols = pl.ds(n * TILE, TILE)
            picked[pl.ds(pl.multiple_of(i * rows, rows), rows), cols] = jnp.dot(
                place[i], block[i, :, cols], preferred_element_type=F32
            ).astype(BF16)

    @pl.loop(0, tiles)
    def _(n):
        stream.wait(n)
        value = lax.dot_general(
            picked[...],
            buffer[n % stream.slots],
            (((1,), (1,)), ((), ())),
            preferred_element_type=F32,
        )
        value = gated(value, slot_gates[...])
        cols = pl.ds(pl.multiple_of(n % 4 * tile, tile), tile)
        for i, out in enumerate(outs):

            @pl.when(n // 4 == i)
            def _():
                out[:, cols] = value

        @pl.when(n + stream.slots < tiles)
        def _():
            stream.start(n + stream.slots)


def backward(distances, cap, sides, where, pipe, tokens, gates, weights, share):
    count, rows = len(distances), 2 * cap
    depth, width = weights.shape
    return kernel_call(
        functools.partial(backward_kernel, distances, cap, sides),
        "backward",
        [(SMEM, where), (SMEM, pipe), (VMEM, gates), (HBM, weights)] + [(ANY, x) for x in tokens],
        [jax.ShapeDtypeStruct((count * rows, depth // 2), BF16)] * len(sides),
        [
            pltpu.VMEM((count, gates.shape[1], width), BF16),
            pltpu.SemaphoreType.DMA((2 * count,)),
            pltpu.VMEM((count * rows, width), BF16),
            *place_scratch(count, gates, cap),
            pltpu.VMEM((4, depth // 8, width), BF16),
            pltpu.SemaphoreType.DMA((4, 4)),
        ],
        flops=len(sides) * count * rows * depth * width // share,
        moved=2 * (depth * width + count * rows * (depth + 2 * width)) // share,
    )


def collect_kernel(groups, where, *refs):
    out, held, sems = refs[-3:]
    copies = []
    for g, distances in enumerate(groups):
        hold, recv = refs[2 * g], refs[2 * g + 1]
        rows = hold.shape[0] // len(distances)
        for i, d in enumerate(distances):
            at, n = pl.ds(i * rows, rows), len(copies)
            held[n] = (hold[at, :].astype(F32) + recv[at, :].astype(F32)).astype(BF16)
            to = pl.ds(pl.multiple_of(where[d % 8] * rows, rows), rows)
            copies.append(pltpu.make_async_copy(held.at[n], out.at[to, :], sems.at[n]))
            copies[-1].start()
    for copy in copies:
        copy.wait()


def collect(groups, where, arrays, rows, into=None):
    count = sum(len(distances) for distances in groups)
    out = jax.ShapeDtypeStruct((rows, arrays[0].shape[1]), BF16)
    inputs = [(SMEM, where)] + [(VMEM, x) for x in arrays]
    if into is not None:
        inputs.append((HBM, into))
    in_specs, arrays = zip(*inputs)
    return pl.pallas_call(
        functools.partial(collect_kernel, groups),
        in_specs=in_specs,
        out_specs=HBM,
        out_shape=out,
        scratch_shapes=[
            pltpu.VMEM((count, rows // 8, out.shape[1]), BF16),
            pltpu.SemaphoreType.DMA((count,)),
        ],
        input_output_aliases={} if into is None else {len(inputs) - 1: 0},
        compiler_params=pltpu.CompilerParams(vmem_limit_bytes=20 * 2**20),
        cost_estimate=pl.CostEstimate(
            flops=2**20, bytes_accessed=6 * count * rows * 128, transcendentals=0
        ),
        name="collect",
    )(*arrays)


def on_device_16(hidden_a, expert_weights, routes_a, gates_a, cotangent_b, routes_b, gates_b):
    me = lax.axis_index("expert").astype(jnp.int32)
    z, y, c = me // 4, me // 2 % 2, me % 2
    pipe = lax.axis_index("pipe").astype(jnp.int32).reshape(1)
    rows = hidden_a.shape[1] // 8
    cap = rows // 2
    tokens, width = cotangent_b.shape
    weights, hidden = expert_weights[0], hidden_a[0]

    ring = (jnp.where(y == 0, z, 7 - z) + jnp.arange(8, dtype=jnp.int32)) % 8
    to_z, to_y = jnp.minimum(ring, 7 - ring), (ring > 3).astype(jnp.int32)
    chips = to_z * 2 + to_y
    where = jnp.concatenate([chips, c.reshape(1), (to_z ^ z) * 2 + (to_y ^ y)])

    got, pair = {0: cotangent_b}, {}
    got[-1], got[1] = step_ring(cotangent_b, 1), step_ring(cotangent_b, -1)

    both = gates_of(routes_a, gates_a, routes_b, gates_b)
    four = jnp.stack([both] + [xor(both, j) for j in (1, 2, 3)])
    four = lax.dynamic_index_in_dim(four.reshape(4, 4, 4, 2 * tokens), me % 4, 2, False)
    weights, four = tie(weights, four)
    raw1 = raw_forward(0, width // 2, hidden, pin(weights))
    every = jnp.stack([four] + [xor(four, 4 * k) for k in (1, 2, 3)])
    raw1, weights, every, got[-1], got[1] = tie(raw1, weights, every, got[-1], got[1])
    weights = pin(weights)
    every = lax.dynamic_index_in_dim(every, z, 2, False)
    gate = jnp.moveaxis(every.reshape(8, 2, 2, tokens), 2, 0).reshape(2, 8, 2 * tokens)
    gate_a, gate_b = gate[0], gate[1]

    def spread(distances, split, gates):
        return spread_tokens(distances, split, cap, where, gates, (pin(raw1), pin(raw2)))

    def bwd(distances, sides=(0, 1), share=1):
        values = [x for d in distances for x in (got[d], pair[d])]
        return backward(distances, cap, sides, where, pipe, values, gate_b, weights, share)

    got[-2], got[2] = step_ring(got[-1], 1), step_ring(got[1], -1)
    pair[0] = core(got[0])
    raw2 = raw_forward(width // 2, width // 2, hidden, weights)
    raw2, got[-2], got[2], pair[0] = tie(raw2, got[-2], got[2], pair[0])

    got[-3], got[3] = step_ring(got[-2], 1), step_ring(got[2], -1)
    keep1, other1, other2 = spread((3, -4, 2, -3), 2, gate_a)
    other1, other2 = core(other1), core(other2)
    pair[-1], pair[1] = core(got[-1]), core(got[1])
    up = step_ring(add(keep1[:tokens], other1[:tokens]), 1)
    down = step_ring(add(keep1[tokens : 2 * tokens], other1[tokens:]), -1)
    gate_a, pair[-1], pair[1], other2 = tie(gate_a, pair[-1], pair[1], other2)
    keep2, other3, other4 = spread((1, -2, -1, 0), 2, gate_a)
    keep2, gate_b = tie(keep2, gate_b)
    send1, hold1 = bwd((0, -1, 1), share=64)

    def mine(i, other, *more):
        at = slice(i * tokens, (i + 1) * tokens)
        other_at = slice(i % 2 * tokens, (i % 2 + 1) * tokens)
        return add(keep2[at], other[other_at], *more)

    send1, got[-3], got[3], up, down, other3, other4 = tie(
        send1, got[-3], got[3], up, down, other3, other4
    )
    got[-4] = step_ring(got[-3], 1)
    up = step_ring(add(keep1[2 * tokens : 3 * tokens], other2[:tokens], up), 1)
    down = step_ring(add(keep1[3 * tokens :], other2[tokens:], down), -1)
    recv1 = across(send1)
    pair[-2], pair[2], other3 = core(got[-2]), core(got[2]), core(other3)
    pair[-3], pair[3], other4 = core(got[-3]), core(got[3]), core(other4)
    gate_b, other3, other4, pair[-3], pair[3] = tie(gate_b, other3, other4, pair[-3], pair[3])
    send2, hold2 = bwd((-2, 2))

    hold2, send2, down, gate_b = tie(hold2, send2, down, gate_b)
    recv2 = across(send2)
    down = step_ring(mine(1, other3, down), -1)
    send3, hold3 = bwd((-3, 3), share=64)

    hold3, send3, up, got[-4], down, recv1, recv2 = tie(
        hold3, send3, up, got[-4], down, recv1, recv2
    )
    recv3 = across(send3)
    pair[-4] = core(got[-4])
    up, down = step_ring(mine(0, other3, up), 1), step_ring(mine(2, other4, down), -1)
    (send4,) = bwd((-4,), (0,))
    recv4 = across(send4)
    send4, gate_b = tie(send4, gate_b)
    (hold4,) = bwd((-4,), (1,), 64)
    hold4, up, down, recv3 = tie(hold4, up, down, recv3)
    mixed_a = mine(3, other4, up, down)
    grad = collect(
        ((0, -1, 1), (-2, 2), (-3, 3)), where, (hold1, recv1, hold2, recv2, hold3, recv3), 8 * rows
    )
    grad, mixed_a, recv4 = tie(grad, mixed_a, recv4)
    grad = collect(((-4,),), where, (hold4, recv4), 8 * rows, grad)
    return (mixed_a, grad[None])


def solution(mesh):
    in_specs = (
        P("expert", None, None),
        P("expert", None, "pipe"),
        P("expert", None),
        P("expert", None),
        P("expert", "pipe"),
        P("expert", None),
        P("expert", None),
    )
    out_specs = (P("expert", "pipe"), P("expert", None, "pipe"))
    tailored = mesh.shape["expert"] == 16 and mesh.shape["pipe"] == 2
    return jax.shard_map(
        on_device_16 if tailored else on_device_any,
        mesh=mesh,
        in_specs=in_specs,
        out_specs=out_specs,
        check_vma=False,
    )
```

```python
import functools

import jax
import jax.numpy as jnp
from jax import lax
from jax.experimental import pallas as pl
from jax.experimental.pallas import tpu as pltpu
from jax.sharding import PartitionSpec as P

BF16, F32 = jnp.bfloat16, jnp.float32
TILE = 512
LANES = 128
RAW_TILE = 256


def dense_gates(routes, gates, total):
    experts = jnp.arange(total, dtype=jnp.int32)[:, None, None]
    return jnp.sum(jnp.where(routes[None] == experts, gates[None], 0.0), axis=2)


def ranks_of(gate):
    tokens = gate.shape[-1]
    earlier = jnp.triu(jnp.ones((tokens, tokens), BF16), 1)
    counts = jnp.dot((gate > 0.0).astype(BF16), earlier, preferred_element_type=F32)
    return counts.astype(jnp.int32)


def add(*terms):
    total = terms[0].astype(F32)
    for term in terms[1:]:
        total = total + term.astype(F32)
    return total.astype(BF16)


def on_device_any(hidden_a, expert_weights, routes_a, gates_a, cotangent_b, routes_b, gates_b):
    groups = lax.axis_size("expert")
    me = lax.axis_index("expert")
    total = expert_weights.shape[0] * groups
    rows = hidden_a.shape[1]
    cap = rows // groups
    tokens, width = cotangent_b.shape
    weights = expert_weights[0]

    both = jnp.stack(
        [dense_gates(routes_a, gates_a, total), dense_gates(routes_b, gates_b, total)], axis=1
    )
    every = lax.all_gather(both, "expert", axis=0, tiled=False)
    own = lax.dynamic_index_in_dim(every, me, axis=1, keepdims=False)
    gathered = lax.all_gather(cotangent_b, "expert", axis=0, tiled=True)

    def placement(gate):
        slots = jnp.arange(cap, dtype=jnp.int32)[None, :, None]
        hit = (gate > 0.0)[:, None, :] & (ranks_of(gate)[:, None, :] == slots)
        return hit.astype(BF16), jnp.sum(jnp.where(hit, gate[:, None, :], 0.0), axis=2)

    hit_a, slot_gate_a = placement(own[:, 0])
    hit_b, slot_gate_b = placement(own[:, 1])

    outputs = jnp.einsum("rf,fd->rd", hidden_a[0], weights, preferred_element_type=F32)
    scaled = (outputs * slot_gate_a.reshape(rows, 1)).astype(BF16)
    spread = jnp.einsum(
        "sct,scd->std", hit_a, scaled.reshape(groups, cap, width), preferred_element_type=F32
    ).astype(BF16)
    mixed_a = lax.psum_scatter(
        spread.reshape(groups * tokens, width), "expert", scatter_dimension=0, tiled=True
    )
    picked = jnp.einsum(
        "sct,std->scd",
        hit_b,
        gathered.reshape(groups, tokens, width),
        preferred_element_type=F32,
    ).astype(BF16)
    partial_value = jnp.einsum(
        "rd,fd->rf", picked.reshape(rows, width), weights, preferred_element_type=F32
    )
    partial_value = (partial_value * slot_gate_b.reshape(rows, 1)).astype(BF16)
    grad = lax.psum_scatter(partial_value, "pipe", scatter_dimension=1, tiled=True)
    return (mixed_a, grad[None])


RING = [(0, 0), (1, 0), (2, 0), (3, 0), (3, 1), (2, 1), (1, 1), (0, 1)]


def step_ring(value, way):
    pairs = []
    for place, (z, y) in enumerate(RING):
        to_z, to_y = RING[(place + way) % 8]
        pairs += [(z * 4 + y * 2 + c, to_z * 4 + to_y * 2 + c) for c in range(2)]
    return lax.ppermute(value, "expert", pairs)


def xor(value, bits):
    return lax.ppermute(value, "expert", [(i, i ^ bits) for i in range(16)])


def core(value):
    return xor(value, 1)


def across(value):
    return lax.ppermute(value, "pipe", [(0, 1), (1, 0)])


def pin(value):
    return pltpu.with_memory_space_constraint(value, pltpu.HBM)


def tie(*values):
    return lax.optimization_barrier(values)


SMEM = pl.BlockSpec(memory_space=pltpu.SMEM)
VMEM = pl.BlockSpec(memory_space=pltpu.VMEM)
HBM = pl.BlockSpec(memory_space=pltpu.HBM)
ANY = pl.BlockSpec(memory_space=pl.ANY)


def kernel_call(kernel, name, inputs, out_shape, scratch, flops, moved):
    in_specs, arrays = zip(*inputs)
    return pl.pallas_call(
        kernel,
        in_specs=in_specs,
        out_specs=[VMEM] * len(out_shape),
        out_shape=out_shape,
        scratch_shapes=scratch,
        compiler_params=pltpu.CompilerParams(vmem_limit_bytes=20 * 2**20),
        cost_estimate=pl.CostEstimate(flops=flops, bytes_accessed=moved, transcendentals=0),
        name=name,
    )(*arrays)


def gates_kernel(*refs):
    sources, out, held, sems = refs[:4], refs[4], refs[5:9], refs[9]
    copies = [pltpu.make_async_copy(x, y, sems.at[i]) for i, (x, y) in enumerate(zip(sources, held))]
    for copy in copies:
        copy.start()
    for copy in copies:
        copy.wait()
    top, tokens = held[0].shape
    experts = lax.broadcasted_iota(jnp.int32, (out.shape[0], tokens), 0)
    for i in range(2):
        routes, gates = held[2 * i : 2 * i + 2]
        total = jnp.zeros(experts.shape, F32)
        for k in range(top):
            total += jnp.where(routes[k : k + 1, :] == experts, gates[k : k + 1, :], 0.0)
        out[:, pl.ds(i * tokens, tokens)] = total


def gates_of(*arrays):
    tokens, top = arrays[0].shape
    arrays = [pin(x.T) for x in arrays]
    return kernel_call(
        gates_kernel,
        "gates",
        [(HBM, x) for x in arrays],
        [jax.ShapeDtypeStruct((16, 2 * tokens), F32)],
        [pltpu.VMEM((top, tokens), x.dtype) for x in arrays] + [pltpu.SemaphoreType.DMA((4,))],
        flops=2**20,
        moved=2**17,
    )[0]


def place_slots(distances, where, gates, cap, target, place, slot_gates):
    gate = gates[...]
    tokens = gate.shape[1] // 2
    row = lax.broadcasted_iota(jnp.int32, (2 * tokens, 2 * tokens), 0)
    col = lax.broadcasted_iota(jnp.int32, (2 * tokens, 2 * tokens), 1)
    earlier = ((row < col) & (row // tokens == col // tokens)).astype(F32).astype(BF16)
    chosen = (gate > 0.0).astype(F32).astype(BF16)
    rank = jnp.dot(chosen, earlier, preferred_element_type=F32)
    second = (lax.broadcasted_iota(jnp.int32, gate.shape, 1) // tokens) ^ where[8]
    target[...] = jnp.where(gate > 0.0, rank + (second * cap).astype(F32), -1.0)
    slots = lax.broadcasted_iota(jnp.int32, (2 * cap, 2 * tokens), 0).astype(F32)
    for i, d in enumerate(distances):
        block = pl.ds(where[9 + d % 8], 1)
        hit = target[block, :] == slots
        place[i] = hit.astype(F32).astype(BF16)
        total = jnp.sum(jnp.where(hit, gates[block, :], 0.0), axis=1, keepdims=True)
        slot_gates[pl.ds(i * 2 * cap, 2 * cap), :] = jnp.broadcast_to(total, (2 * cap, LANES))


def place_scratch(count, gates, cap):
    return [
        pltpu.VMEM(gates.shape, F32),
        pltpu.VMEM((count, 2 * cap, gates.shape[1]), BF16),
        pltpu.VMEM((count * 2 * cap, LANES), F32),
    ]


def gated(value, slot_gates):
    factor = jnp.concatenate([slot_gates] * (value.shape[1] // LANES), axis=1)
    return (value * factor).astype(BF16)


class Stream:
    def __init__(self, tile, buffer, sems):
        self.tile, self.buffer, self.sems = tile, buffer, sems
        self.slots, self.parts = sems.shape

    def copies(self, n):
        slot = n % self.slots
        rows = self.buffer.shape[1] // self.parts
        source = self.tile(n)
        for part in range(self.parts):
            at = pl.ds(part * rows, rows)
            yield pltpu.make_async_copy(
                source.at[at, :], self.buffer.at[slot, at, :], self.sems.at[slot, part]
            )

    def start(self, n):
        for copy in self.copies(n):
            copy.start()

    def wait(self, n):
        for copy in self.copies(n):
            copy.wait()


def raw_kernel(first, hidden, weights, out, held, held_sems, buffer, sems, staged, out_sems):
    tiles = out.shape[1] // RAW_TILE
    stream = Stream(
        lambda n: weights.at[:, pl.ds(pl.multiple_of(first + n * RAW_TILE, RAW_TILE), RAW_TILE)], buffer, sems
    )
    rows = held.shape[0] // held_sems.shape[0]
    fetch = []
    for i in range(held_sems.shape[0]):
        at = pl.ds(i * rows, rows)
        fetch.append(pltpu.make_async_copy(hidden.at[at, :], held.at[at, :], held_sems.at[i]))
        fetch[-1].start()
    stream.start(0)

    def put(n):
        cols = pl.ds(pl.multiple_of(n * RAW_TILE, RAW_TILE), RAW_TILE)
        return pltpu.make_async_copy(staged.at[n % 2], out.at[:, cols], out_sems.at[n % 2])

    for copy in fetch:
        copy.wait()
    for n in range(1, stream.slots):
        stream.start(n)

    @pl.loop(0, tiles)
    def _(n):
        stream.wait(n)

        @pl.when(n >= 2)
        def _():
            put(n - 2).wait()

        value = jnp.dot(held[...], buffer[n % stream.slots], preferred_element_type=F32)
        staged[n % 2] = value.astype(BF16)
        put(n).start()

        @pl.when(n + stream.slots < tiles)
        def _():
            stream.start(n + stream.slots)

    put(tiles - 2).wait()
    put(tiles - 1).wait()


def raw_forward(first, width, hidden, weights):
    rows, depth = hidden.shape
    return pl.pallas_call(
        functools.partial(raw_kernel, first),
        in_specs=[HBM, HBM],
        out_specs=HBM,
        out_shape=pltpu.HBM((rows, width), BF16),
        scratch_shapes=[
            pltpu.VMEM(hidden.shape, BF16),
            pltpu.SemaphoreType.DMA((4,)),
            pltpu.VMEM((3, depth, RAW_TILE), BF16),
            pltpu.SemaphoreType.DMA((3, 4)),
            pltpu.VMEM((2, rows, RAW_TILE), BF16),
            pltpu.SemaphoreType.DMA((2,)),
        ],
        compiler_params=pltpu.CompilerParams(vmem_limit_bytes=20 * 2**20),
        cost_estimate=pl.CostEstimate(
            flops=2 * rows * depth * width,
            bytes_accessed=2 * (depth * width + rows * (depth + width)),
            transcendentals=0,
        ),
        name="raw_forward",
    )(hidden, weights)


def spread_kernel(distances, split, cap, where, gates, *refs):
    count = len(distances)
    raws, (keep, *others), scratch = refs[:2], refs[2:-6], refs[-6:]
    target, place, slot_gates, to_tokens, held, sems = scratch
    rows, half = 2 * cap, gates.shape[1] // 2
    width = raws[0].shape[1]

    def fetch(i, start):
        return [
            pltpu.make_async_copy(
                raw.at[pl.ds(start, rows), :],
                held.at[i, :, pl.ds(j * width, width)],
                sems.at[i, j],
            )
            for j, raw in enumerate(raws)
        ]

    for i, d in enumerate(distances):
        for copy in fetch(i, pl.multiple_of(where[d % 8] * rows, rows)):
            copy.start()
    place_slots(distances, where, gates, cap, target, place, slot_gates)
    tokens = 2 * half
    same = lax.broadcasted_iota(jnp.int32, (tokens, tokens), 0) == lax.broadcasted_iota(
        jnp.int32, (tokens, tokens), 1
    )
    same = same.astype(F32).astype(BF16)
    for i in range(count):
        to_tokens[i] = lax.dot_general(
            same, place[i], (((1,), (1,)), ((), ())), preferred_element_type=F32
        ).astype(BF16)
    for g, other in enumerate(others):

        @pl.loop(0, split)
        def _(j):
            i = g * split + j
            for copy in fetch(i, 0):
                copy.wait()
            for n in range(2 * width // TILE):
                cols = pl.ds(n * TILE, TILE)
                part = held[i, :, cols].astype(F32)
                part = gated(part, slot_gates[pl.ds(pl.multiple_of(i * rows, rows), rows), :])
                part = jnp.dot(to_tokens[i], part, preferred_element_type=F32).astype(BF16)
                keep[pl.ds(pl.multiple_of(i * half, half), half), cols] = part[:half]
                other[pl.ds(pl.multiple_of(j * half, half), half), cols] = part[half:]


def spread_tokens(distances, split, cap, where, gates, raws):
    count, half, width = len(distances), gates.shape[1] // 2, 2 * raws[0].shape[1]
    return kernel_call(
        functools.partial(spread_kernel, distances, split, cap),
        "spread_tokens",
        [(SMEM, where), (VMEM, gates), (HBM, raws[0]), (HBM, raws[1])],
        [jax.ShapeDtypeStruct((count * half, width), BF16)]
        + [jax.ShapeDtypeStruct((split * half, width), BF16)] * (count // split),
        [
            *place_scratch(count, gates, cap),
            pltpu.VMEM((count, 2 * half, 2 * cap), BF16),
            pltpu.VMEM((count, 2 * cap, width), BF16),
            pltpu.SemaphoreType.DMA((count, 2)),
        ],
        flops=count * 2**28,
        moved=count * 6 * half * width,
    )


def backward_kernel(distances, cap, sides, where, pipe, gates, weights, *refs):
    count, rows = len(distances), 2 * cap
    tokens, outs = refs[: 2 * count], refs[2 * count : 2 * count + len(sides)]
    block, block_sems, picked, target, place, slot_gates, buffer, sems = refs[
        2 * count + len(sides) :
    ]
    half, tile = tokens[0].shape[0], buffer.shape[1]
    tiles = 4 * len(sides)
    first = (1 - pipe[0] + sides[0]) * 4

    def weight_tile(n):
        return weights.at[pl.ds(pl.multiple_of((first + n) % 8 * tile, tile), tile), :]

    fetch = []
    for i, token in enumerate(tokens):
        to = block.at[i // 2, pl.ds(i % 2 * half, half), :]
        fetch.append(pltpu.make_async_copy(token, to, block_sems.at[i]))
        fetch[-1].start()
    stream = Stream(weight_tile, buffer, sems)
    for n in range(stream.slots):
        stream.start(n)
    place_slots(distances, where, gates, cap, target, place, slot_gates)
    for copy in fetch:
        copy.wait()

    @pl.loop(0, count)
    def _(i):
        for n in range(block.shape[2] // TILE):
            cols = pl.ds(n * TILE, TILE)
            picked[pl.ds(pl.multiple_of(i * rows, rows), rows), cols] = jnp.dot(
                place[i], block[i, :, cols], preferred_element_type=F32
            ).astype(BF16)

    @pl.loop(0, tiles)
    def _(n):
        stream.wait(n)
        value = lax.dot_general(
            picked[...],
            buffer[n % stream.slots],
            (((1,), (1,)), ((), ())),
            preferred_element_type=F32,
        )
        value = gated(value, slot_gates[...])
        cols = pl.ds(pl.multiple_of(n % 4 * tile, tile), tile)
        for i, out in enumerate(outs):

            @pl.when(n // 4 == i)
            def _():
                out[:, cols] = value

        @pl.when(n + stream.slots < tiles)
        def _():
            stream.start(n + stream.slots)


def backward(distances, cap, sides, where, pipe, tokens, gates, weights, share):
    count, rows = len(distances), 2 * cap
    depth, width = weights.shape
    return kernel_call(
        functools.partial(backward_kernel, distances, cap, sides),
        "backward",
        [(SMEM, where), (SMEM, pipe), (VMEM, gates), (HBM, weights)] + [(ANY, x) for x in tokens],
        [jax.ShapeDtypeStruct((count * rows, depth // 2), BF16)] * len(sides),
        [
            pltpu.VMEM((count, gates.shape[1], width), BF16),
            pltpu.SemaphoreType.DMA((2 * count,)),
            pltpu.VMEM((count * rows, width), BF16),
            *place_scratch(count, gates, cap),
            pltpu.VMEM((4, depth // 8, width), BF16),
            pltpu.SemaphoreType.DMA((4, 4)),
        ],
        flops=len(sides) * count * rows * depth * width // share,
        moved=2 * (depth * width + count * rows * (depth + 2 * width)) // share,
    )


def collect_kernel(groups, where, *refs):
    out, held, sems = refs[-3:]
    copies = []
    for g, distances in enumerate(groups):
        hold, recv = refs[2 * g], refs[2 * g + 1]
        rows = hold.shape[0] // len(distances)
        for i, d in enumerate(distances):
            at, n = pl.ds(i * rows, rows), len(copies)
            held[n] = (hold[at, :].astype(F32) + recv[at, :].astype(F32)).astype(BF16)
            to = pl.ds(pl.multiple_of(where[d % 8] * rows, rows), rows)
            copies.append(pltpu.make_async_copy(held.at[n], out.at[to, :], sems.at[n]))
            copies[-1].start()
    for copy in copies:
        copy.wait()


def collect(groups, where, arrays, rows, into=None):
    count = sum(len(distances) for distances in groups)
    out = jax.ShapeDtypeStruct((rows, arrays[0].shape[1]), BF16)
    inputs = [(SMEM, where)] + [(VMEM, x) for x in arrays]
    if into is not None:
        inputs.append((HBM, into))
    in_specs, arrays = zip(*inputs)
    return pl.pallas_call(
        functools.partial(collect_kernel, groups),
        in_specs=in_specs,
        out_specs=HBM,
        out_shape=out,
        scratch_shapes=[
            pltpu.VMEM((count, rows // 8, out.shape[1]), BF16),
            pltpu.SemaphoreType.DMA((count,)),
        ],
        input_output_aliases={} if into is None else {len(inputs) - 1: 0},
        compiler_params=pltpu.CompilerParams(vmem_limit_bytes=20 * 2**20),
        cost_estimate=pl.CostEstimate(
            flops=2**20, bytes_accessed=6 * count * rows * 128, transcendentals=0
        ),
        name="collect",
    )(*arrays)


def on_device_16(hidden_a, expert_weights, routes_a, gates_a, cotangent_b, routes_b, gates_b):
    me = lax.axis_index("expert").astype(jnp.int32)
    z, y, c = me // 4, me // 2 % 2, me % 2
    pipe = lax.axis_index("pipe").astype(jnp.int32).reshape(1)
    rows = hidden_a.shape[1] // 8
    cap = rows // 2
    tokens, width = cotangent_b.shape
    weights, hidden = expert_weights[0], hidden_a[0]

    ring = (jnp.where(y == 0, z, 7 - z) + jnp.arange(8, dtype=jnp.int32)) % 8
    to_z, to_y = jnp.minimum(ring, 7 - ring), (ring > 3).astype(jnp.int32)
    chips = to_z * 2 + to_y
    where = jnp.concatenate([chips, c.reshape(1), (to_z ^ z) * 2 + (to_y ^ y)])

    got, pair = {0: cotangent_b}, {}
    got[-1], got[1] = step_ring(cotangent_b, 1), step_ring(cotangent_b, -1)

    both = gates_of(routes_a, gates_a, routes_b, gates_b)
    four = jnp.stack([both] + [xor(both, j) for j in (1, 2, 3)])
    four = lax.dynamic_index_in_dim(four.reshape(4, 4, 4, 2 * tokens), me % 4, 2, False)
    weights, four = tie(weights, four)
    raw1 = raw_forward(0, width // 2, pin(hidden), pin(weights))
    every = jnp.stack([four] + [xor(four, 4 * k) for k in (1, 2, 3)])
    raw1, weights, every, got[-1], got[1] = tie(raw1, weights, every, got[-1], got[1])
    weights = pin(weights)
    every = lax.dynamic_index_in_dim(every, z, 2, False)
    gate = jnp.moveaxis(every.reshape(8, 2, 2, tokens), 2, 0).reshape(2, 8, 2 * tokens)
    gate_a, gate_b = gate[0], gate[1]

    def spread(distances, split, gates):
        return spread_tokens(distances, split, cap, where, gates, (pin(raw1), pin(raw2)))

    def bwd(distances, sides=(0, 1), share=1):
        values = [x for d in distances for x in (got[d], pair[d])]
        return backward(distances, cap, sides, where, pipe, values, gate_b, weights, share)

    got[-2], got[2] = step_ring(got[-1], 1), step_ring(got[1], -1)
    pair[0] = core(got[0])
    raw2 = raw_forward(width // 2, width // 2, pin(hidden), weights)
    raw2, got[-2], got[2], pair[0] = tie(raw2, got[-2], got[2], pair[0])

    got[-3], got[3] = step_ring(got[-2], 1), step_ring(got[2], -1)
    keep1, other1, other2 = spread((3, -4, 2, -3), 2, gate_a)
    other1, other2 = core(other1), core(other2)
    for d in (-1, 1, -2):
        pair[d] = core(got[d])
    up = step_ring(add(keep1[:tokens], other1[:tokens]), 1)
    down = step_ring(add(keep1[tokens : 2 * tokens], other1[tokens:]), -1)
    gate_a, pair[-1], pair[1], pair[-2], other2 = tie(
        gate_a, pair[-1], pair[1], pair[-2], other2
    )
    keep2, other3, other4 = spread((1, -2, -1, 0), 2, gate_a)
    keep2, gate_b = tie(keep2, gate_b)
    groups = (0, -1, 1, -2), (2, -3, 3), (-4,)
    send1, hold1 = bwd(groups[0], share=64)

    def mine(i, other, *more):
        at = slice(i * tokens, (i + 1) * tokens)
        other_at = slice(i % 2 * tokens, (i % 2 + 1) * tokens)
        return add(keep2[at], other[other_at], *more)

    send1, got[-3], got[3], up, down, other3, other4 = tie(
        send1, got[-3], got[3], up, down, other3, other4
    )
    got[-4] = step_ring(got[-3], 1)
    up = step_ring(add(keep1[2 * tokens : 3 * tokens], other2[:tokens], up), 1)
    down = step_ring(add(keep1[3 * tokens :], other2[tokens:], down), -1)
    recv1 = across(send1)
    pair[2], pair[-3], pair[3] = core(got[2]), core(got[-3]), core(got[3])
    other3, other4 = core(other3), core(other4)
    gate_b, other3, other4 = tie(gate_b, other3, other4)
    send2, hold2 = bwd(groups[1], share=64)

    hold2, send2, down = tie(hold2, send2, down)
    recv2 = across(send2)
    down = step_ring(mine(1, other3, down), -1)
    up, got[-4], down, recv1 = tie(up, got[-4], down, recv1)

    pair[-4] = core(got[-4])
    up, down = step_ring(mine(0, other3, up), 1), step_ring(mine(2, other4, down), -1)
    send3, hold3 = bwd(groups[2], share=64)
    recv3 = across(send3)
    hold3, recv2 = tie(hold3, recv2)
    grad = collect(groups[:2], where, (hold1, recv1, hold2, recv2), 8 * rows)
    grad, up, down, recv3 = tie(grad, up, down, recv3)
    mixed_a = mine(3, other4, up, down)
    grad = collect(groups[2:], where, (hold3, recv3), 8 * rows, grad)
    return (mixed_a, grad[None])


def solution(mesh):
    in_specs = (
        P("expert", None, None),
        P("expert", None, "pipe"),
        P("expert", None),
        P("expert", None),
        P("expert", "pipe"),
        P("expert", None),
        P("expert", None),
    )
    out_specs = (P("expert", "pipe"), P("expert", None, "pipe"))
    tailored = mesh.shape["expert"] == 16 and mesh.shape["pipe"] == 2
    return jax.shard_map(
        on_device_16 if tailored else on_device_any,
        mesh=mesh,
        in_specs=in_specs,
        out_specs=out_specs,
        check_vma=False,
    )
```

```python
import functools

import jax
import jax.numpy as jnp
from jax import lax
from jax.experimental import pallas as pl
from jax.experimental.pallas import tpu as pltpu
from jax.sharding import PartitionSpec as P

BF16, F32 = jnp.bfloat16, jnp.float32
TILE = 512
LANES = 128
RAW_TILE = 256


def dense_gates(routes, gates, total):
    experts = jnp.arange(total, dtype=jnp.int32)[:, None, None]
    return jnp.sum(jnp.where(routes[None] == experts, gates[None], 0.0), axis=2)


def ranks_of(gate):
    tokens = gate.shape[-1]
    earlier = jnp.triu(jnp.ones((tokens, tokens), BF16), 1)
    counts = jnp.dot((gate > 0.0).astype(BF16), earlier, preferred_element_type=F32)
    return counts.astype(jnp.int32)


def add(*terms):
    total = terms[0].astype(F32)
    for term in terms[1:]:
        total = total + term.astype(F32)
    return total.astype(BF16)


def on_device_any(hidden_a, expert_weights, routes_a, gates_a, cotangent_b, routes_b, gates_b):
    groups = lax.axis_size("expert")
    me = lax.axis_index("expert")
    total = expert_weights.shape[0] * groups
    rows = hidden_a.shape[1]
    cap = rows // groups
    tokens, width = cotangent_b.shape
    weights = expert_weights[0]

    both = jnp.stack(
        [dense_gates(routes_a, gates_a, total), dense_gates(routes_b, gates_b, total)], axis=1
    )
    every = lax.all_gather(both, "expert", axis=0, tiled=False)
    own = lax.dynamic_index_in_dim(every, me, axis=1, keepdims=False)
    gathered = lax.all_gather(cotangent_b, "expert", axis=0, tiled=True)

    def placement(gate):
        slots = jnp.arange(cap, dtype=jnp.int32)[None, :, None]
        hit = (gate > 0.0)[:, None, :] & (ranks_of(gate)[:, None, :] == slots)
        return hit.astype(BF16), jnp.sum(jnp.where(hit, gate[:, None, :], 0.0), axis=2)

    hit_a, slot_gate_a = placement(own[:, 0])
    hit_b, slot_gate_b = placement(own[:, 1])

    outputs = jnp.einsum("rf,fd->rd", hidden_a[0], weights, preferred_element_type=F32)
    scaled = (outputs * slot_gate_a.reshape(rows, 1)).astype(BF16)
    spread = jnp.einsum(
        "sct,scd->std", hit_a, scaled.reshape(groups, cap, width), preferred_element_type=F32
    ).astype(BF16)
    mixed_a = lax.psum_scatter(
        spread.reshape(groups * tokens, width), "expert", scatter_dimension=0, tiled=True
    )
    picked = jnp.einsum(
        "sct,std->scd",
        hit_b,
        gathered.reshape(groups, tokens, width),
        preferred_element_type=F32,
    ).astype(BF16)
    partial_value = jnp.einsum(
        "rd,fd->rf", picked.reshape(rows, width), weights, preferred_element_type=F32
    )
    partial_value = (partial_value * slot_gate_b.reshape(rows, 1)).astype(BF16)
    grad = lax.psum_scatter(partial_value, "pipe", scatter_dimension=1, tiled=True)
    return (mixed_a, grad[None])


RING = [(0, 0), (1, 0), (2, 0), (3, 0), (3, 1), (2, 1), (1, 1), (0, 1)]


def step_ring(value, way):
    pairs = []
    for place, (z, y) in enumerate(RING):
        to_z, to_y = RING[(place + way) % 8]
        pairs += [(z * 4 + y * 2 + c, to_z * 4 + to_y * 2 + c) for c in range(2)]
    return lax.ppermute(value, "expert", pairs)


def xor(value, bits):
    return lax.ppermute(value, "expert", [(i, i ^ bits) for i in range(16)])


def core(value):
    return xor(value, 1)


def across(value):
    return lax.ppermute(value, "pipe", [(0, 1), (1, 0)])


def pin(value):
    return pltpu.with_memory_space_constraint(value, pltpu.HBM)


def tie(*values):
    return lax.optimization_barrier(values)


SMEM = pl.BlockSpec(memory_space=pltpu.SMEM)
VMEM = pl.BlockSpec(memory_space=pltpu.VMEM)
HBM = pl.BlockSpec(memory_space=pltpu.HBM)
ANY = pl.BlockSpec(memory_space=pl.ANY)


def kernel_call(kernel, name, inputs, out_shape, scratch, flops, moved):
    in_specs, arrays = zip(*inputs)
    return pl.pallas_call(
        kernel,
        in_specs=in_specs,
        out_specs=[VMEM] * len(out_shape),
        out_shape=out_shape,
        scratch_shapes=scratch,
        compiler_params=pltpu.CompilerParams(vmem_limit_bytes=20 * 2**20),
        cost_estimate=pl.CostEstimate(flops=flops, bytes_accessed=moved, transcendentals=0),
        name=name,
    )(*arrays)


def gates_kernel(*refs):
    sources, out, held, sems = refs[:4], refs[4], refs[5:9], refs[9]
    copies = [pltpu.make_async_copy(x, y, sems.at[i]) for i, (x, y) in enumerate(zip(sources, held))]
    for copy in copies:
        copy.start()
    for copy in copies:
        copy.wait()
    top, tokens = held[0].shape
    experts = lax.broadcasted_iota(jnp.int32, (out.shape[0], tokens), 0)
    for i in range(2):
        routes, gates = held[2 * i : 2 * i + 2]
        total = jnp.zeros(experts.shape, F32)
        for k in range(top):
            total += jnp.where(routes[k : k + 1, :] == experts, gates[k : k + 1, :], 0.0)
        out[:, pl.ds(i * tokens, tokens)] = total


def gates_of(*arrays):
    tokens, top = arrays[0].shape
    arrays = [pin(x.T) for x in arrays]
    return kernel_call(
        gates_kernel,
        "gates",
        [(HBM, x) for x in arrays],
        [jax.ShapeDtypeStruct((16, 2 * tokens), F32)],
        [pltpu.VMEM((top, tokens), x.dtype) for x in arrays] + [pltpu.SemaphoreType.DMA((4,))],
        flops=2**20,
        moved=2**17,
    )[0]


def place_slots(distances, where, gates, cap, target, place, slot_gates):
    gate = gates[...]
    tokens = gate.shape[1] // 2
    row = lax.broadcasted_iota(jnp.int32, (2 * tokens, 2 * tokens), 0)
    col = lax.broadcasted_iota(jnp.int32, (2 * tokens, 2 * tokens), 1)
    earlier = ((row < col) & (row // tokens == col // tokens)).astype(F32).astype(BF16)
    chosen = (gate > 0.0).astype(F32).astype(BF16)
    rank = jnp.dot(chosen, earlier, preferred_element_type=F32)
    second = (lax.broadcasted_iota(jnp.int32, gate.shape, 1) // tokens) ^ where[8]
    target[...] = jnp.where(gate > 0.0, rank + (second * cap).astype(F32), -1.0)
    slots = lax.broadcasted_iota(jnp.int32, (2 * cap, 2 * tokens), 0).astype(F32)
    for i, d in enumerate(distances):
        block = pl.ds(where[9 + d % 8], 1)
        hit = target[block, :] == slots
        place[i] = hit.astype(F32).astype(BF16)
        total = jnp.sum(jnp.where(hit, gates[block, :], 0.0), axis=1, keepdims=True)
        slot_gates[pl.ds(i * 2 * cap, 2 * cap), :] = jnp.broadcast_to(total, (2 * cap, LANES))


def place_scratch(count, gates, cap):
    return [
        pltpu.VMEM(gates.shape, F32),
        pltpu.VMEM((count, 2 * cap, gates.shape[1]), BF16),
        pltpu.VMEM((count * 2 * cap, LANES), F32),
    ]


def gated(value, slot_gates):
    factor = jnp.concatenate([slot_gates] * (value.shape[1] // LANES), axis=1)
    return (value * factor).astype(BF16)


class Stream:
    def __init__(self, tile, buffer, sems):
        self.tile, self.buffer, self.sems = tile, buffer, sems
        self.slots, self.parts = sems.shape

    def copies(self, n):
        slot = n % self.slots
        rows = self.buffer.shape[1] // self.parts
        source = self.tile(n)
        for part in range(self.parts):
            at = pl.ds(part * rows, rows)
            yield pltpu.make_async_copy(
                source.at[at, :], self.buffer.at[slot, at, :], self.sems.at[slot, part]
            )

    def start(self, n):
        for copy in self.copies(n):
            copy.start()

    def wait(self, n):
        for copy in self.copies(n):
            copy.wait()


def raw_kernel(first, hidden, weights, out, held, held_sems, buffer, sems, staged, out_sems):
    tiles = out.shape[1] // RAW_TILE
    stream = Stream(
        lambda n: weights.at[:, pl.ds(pl.multiple_of(first + n * RAW_TILE, RAW_TILE), RAW_TILE)], buffer, sems
    )
    rows = held.shape[0] // held_sems.shape[0]
    fetch = []
    for i in range(held_sems.shape[0]):
        at = pl.ds(i * rows, rows)
        fetch.append(pltpu.make_async_copy(hidden.at[at, :], held.at[at, :], held_sems.at[i]))
        fetch[-1].start()
    stream.start(0)

    def put(n):
        cols = pl.ds(pl.multiple_of(n * RAW_TILE, RAW_TILE), RAW_TILE)
        return pltpu.make_async_copy(staged.at[n % 2], out.at[:, cols], out_sems.at[n % 2])

    for copy in fetch:
        copy.wait()
    for n in range(1, stream.slots):
        stream.start(n)

    @pl.loop(0, tiles)
    def _(n):
        stream.wait(n)

        @pl.when(n >= 2)
        def _():
            put(n - 2).wait()

        value = jnp.dot(held[...], buffer[n % stream.slots], preferred_element_type=F32)
        staged[n % 2] = value.astype(BF16)
        put(n).start()

        @pl.when(n + stream.slots < tiles)
        def _():
            stream.start(n + stream.slots)

    put(tiles - 2).wait()
    put(tiles - 1).wait()


def raw_forward(first, width, hidden, weights):
    rows, depth = hidden.shape
    return pl.pallas_call(
        functools.partial(raw_kernel, first),
        in_specs=[HBM, HBM],
        out_specs=HBM,
        out_shape=pltpu.HBM((rows, width), BF16),
        scratch_shapes=[
            pltpu.VMEM(hidden.shape, BF16),
            pltpu.SemaphoreType.DMA((4,)),
            pltpu.VMEM((3, depth, RAW_TILE), BF16),
            pltpu.SemaphoreType.DMA((3, 4)),
            pltpu.VMEM((2, rows, RAW_TILE), BF16),
            pltpu.SemaphoreType.DMA((2,)),
        ],
        compiler_params=pltpu.CompilerParams(vmem_limit_bytes=20 * 2**20),
        cost_estimate=pl.CostEstimate(
            flops=2 * rows * depth * width,
            bytes_accessed=2 * (depth * width + rows * (depth + width)),
            transcendentals=0,
        ),
        name="raw_forward",
    )(hidden, weights)


def spread_kernel(distances, split, cap, where, gates, *refs):
    count = len(distances)
    raws, (keep, *others), scratch = refs[:2], refs[2:-6], refs[-6:]
    target, place, slot_gates, to_tokens, held, sems = scratch
    rows, half = 2 * cap, gates.shape[1] // 2
    width = raws[0].shape[1]

    def fetch(i, start):
        return [
            pltpu.make_async_copy(
                raw.at[pl.ds(start, rows), :],
                held.at[i, :, pl.ds(j * width, width)],
                sems.at[i, j],
            )
            for j, raw in enumerate(raws)
        ]

    for i, d in enumerate(distances):
        for copy in fetch(i, pl.multiple_of(where[d % 8] * rows, rows)):
            copy.start()
    place_slots(distances, where, gates, cap, target, place, slot_gates)
    tokens = 2 * half
    same = lax.broadcasted_iota(jnp.int32, (tokens, tokens), 0) == lax.broadcasted_iota(
        jnp.int32, (tokens, tokens), 1
    )
    same = same.astype(F32).astype(BF16)
    for i in range(count):
        to_tokens[i] = lax.dot_general(
            same, place[i], (((1,), (1,)), ((), ())), preferred_element_type=F32
        ).astype(BF16)
    for g, other in enumerate(others):

        @pl.loop(0, split)
        def _(j):
            i = g * split + j
            for copy in fetch(i, 0):
                copy.wait()
            for n in range(2 * width // TILE):
                cols = pl.ds(n * TILE, TILE)
                part = held[i, :, cols].astype(F32)
                part = gated(part, slot_gates[pl.ds(pl.multiple_of(i * rows, rows), rows), :])
                part = jnp.dot(to_tokens[i], part, preferred_element_type=F32).astype(BF16)
                keep[pl.ds(pl.multiple_of(i * half, half), half), cols] = part[:half]
                other[pl.ds(pl.multiple_of(j * half, half), half), cols] = part[half:]


def spread_tokens(distances, split, cap, where, gates, raws):
    count, half, width = len(distances), gates.shape[1] // 2, 2 * raws[0].shape[1]
    return kernel_call(
        functools.partial(spread_kernel, distances, split, cap),
        "spread_tokens",
        [(SMEM, where), (VMEM, gates), (HBM, raws[0]), (HBM, raws[1])],
        [jax.ShapeDtypeStruct((count * half, width), BF16)]
        + [jax.ShapeDtypeStruct((split * half, width), BF16)] * (count // split),
        [
            *place_scratch(count, gates, cap),
            pltpu.VMEM((count, 2 * half, 2 * cap), BF16),
            pltpu.VMEM((count, 2 * cap, width), BF16),
            pltpu.SemaphoreType.DMA((count, 2)),
        ],
        flops=count * 2**28,
        moved=count * 6 * half * width,
    )


def backward_kernel(distances, cap, sides, where, pipe, gates, weights, *refs):
    count, rows = len(distances), 2 * cap
    tokens, outs = refs[: -8 - len(sides)], refs[-8 - len(sides) : -8]
    block, block_sems, picked, target, place, slot_gates, buffer, sems = refs[-8:]
    tile = buffer.shape[1]
    tiles = 4 * len(sides)
    first = (1 - pipe[0] + sides[0]) * 4

    def weight_tile(n):
        return weights.at[pl.ds(pl.multiple_of((first + n) % 8 * tile, tile), tile), :]

    fetch = []
    at = 0
    for i, token in enumerate(tokens):
        chip, row = divmod(at, block.shape[1])
        to = block.at[chip, pl.ds(row, token.shape[0]), :]
        fetch.append(pltpu.make_async_copy(token, to, block_sems.at[i]))
        fetch[-1].start()
        at += token.shape[0]
    stream = Stream(weight_tile, buffer, sems)
    for n in range(stream.slots):
        stream.start(n)
    place_slots(distances, where, gates, cap, target, place, slot_gates)
    for copy in fetch:
        copy.wait()

    @pl.loop(0, count)
    def _(i):
        for n in range(block.shape[2] // TILE):
            cols = pl.ds(n * TILE, TILE)
            picked[pl.ds(pl.multiple_of(i * rows, rows), rows), cols] = jnp.dot(
                place[i], block[i, :, cols], preferred_element_type=F32
            ).astype(BF16)

    @pl.loop(0, tiles)
    def _(n):
        stream.wait(n)
        value = lax.dot_general(
            picked[...],
            buffer[n % stream.slots],
            (((1,), (1,)), ((), ())),
            preferred_element_type=F32,
        )
        value = gated(value, slot_gates[...])
        cols = pl.ds(pl.multiple_of(n % 4 * tile, tile), tile)
        for i, out in enumerate(outs):

            @pl.when(n // 4 == i)
            def _():
                out[:, cols] = value

        @pl.when(n + stream.slots < tiles)
        def _():
            stream.start(n + stream.slots)


def backward(distances, cap, sides, where, pipe, tokens, gates, weights, share):
    count, rows = len(distances), 2 * cap
    depth, width = weights.shape
    return kernel_call(
        functools.partial(backward_kernel, distances, cap, sides),
        "backward",
        [(SMEM, where), (SMEM, pipe), (VMEM, gates), (HBM, weights)] + [(ANY, x) for x in tokens],
        [jax.ShapeDtypeStruct((count * rows, depth // 2), BF16)] * len(sides),
        [
            pltpu.VMEM((count, gates.shape[1], width), BF16),
            pltpu.SemaphoreType.DMA((len(tokens),)),
            pltpu.VMEM((count * rows, width), BF16),
            *place_scratch(count, gates, cap),
            pltpu.VMEM((4, depth // 8, width), BF16),
            pltpu.SemaphoreType.DMA((4, 4)),
        ],
        flops=len(sides) * count * rows * depth * width // share,
        moved=2 * (depth * width + count * rows * (depth + 2 * width)) // share,
    )


def collect_kernel(groups, where, *refs):
    out, held, sems = refs[-3:]
    copies = []
    for g, distances in enumerate(groups):
        hold, recv = refs[2 * g], refs[2 * g + 1]
        rows = hold.shape[0] // len(distances)
        for i, d in enumerate(distances):
            at, n = pl.ds(i * rows, rows), len(copies)
            held[n] = (hold[at, :].astype(F32) + recv[at, :].astype(F32)).astype(BF16)
            to = pl.ds(pl.multiple_of(where[d % 8] * rows, rows), rows)
            copies.append(pltpu.make_async_copy(held.at[n], out.at[to, :], sems.at[n]))
            copies[-1].start()
    for copy in copies:
        copy.wait()


def collect(groups, where, arrays, rows, into=None):
    count = sum(len(distances) for distances in groups)
    out = jax.ShapeDtypeStruct((rows, arrays[0].shape[1]), BF16)
    inputs = [(SMEM, where)] + [(VMEM, x) for x in arrays]
    if into is not None:
        inputs.append((HBM, into))
    in_specs, arrays = zip(*inputs)
    return pl.pallas_call(
        functools.partial(collect_kernel, groups),
        in_specs=in_specs,
        out_specs=HBM,
        out_shape=out,
        scratch_shapes=[
            pltpu.VMEM((count, rows // 8, out.shape[1]), BF16),
            pltpu.SemaphoreType.DMA((count,)),
        ],
        input_output_aliases={} if into is None else {len(inputs) - 1: 0},
        compiler_params=pltpu.CompilerParams(vmem_limit_bytes=20 * 2**20),
        cost_estimate=pl.CostEstimate(
            flops=2**20, bytes_accessed=6 * count * rows * 128, transcendentals=0
        ),
        name="collect",
    )(*arrays)


def on_device_16(hidden_a, expert_weights, routes_a, gates_a, cotangent_b, routes_b, gates_b):
    me = lax.axis_index("expert").astype(jnp.int32)
    z, y, c = me // 4, me // 2 % 2, me % 2
    pipe = lax.axis_index("pipe").astype(jnp.int32).reshape(1)
    rows = hidden_a.shape[1] // 8
    cap = rows // 2
    tokens, width = cotangent_b.shape
    weights, hidden = expert_weights[0], hidden_a[0]

    ring = (jnp.where(y == 0, z, 7 - z) + jnp.arange(8, dtype=jnp.int32)) % 8
    to_z, to_y = jnp.minimum(ring, 7 - ring), (ring > 3).astype(jnp.int32)
    chips = to_z * 2 + to_y
    where = jnp.concatenate([chips, c.reshape(1), (to_z ^ z) * 2 + (to_y ^ y)])

    got, pair = {0: [cotangent_b]}, {}

    def hop(d, way):
        return [step_ring(x, way) for x in got[d]]

    def swap(d):
        return [core(x) for x in got[d]]

    got[-1], got[1] = hop(0, 1), hop(0, -1)

    both = gates_of(routes_a, gates_a, routes_b, gates_b)
    four = jnp.stack([both] + [xor(both, j) for j in (1, 2, 3)])
    four = lax.dynamic_index_in_dim(four.reshape(4, 4, 4, 2 * tokens), me % 4, 2, False)
    weights, four = tie(weights, four)
    raw1 = raw_forward(0, width // 2, pin(hidden), pin(weights))
    every = jnp.stack([four] + [xor(four, 4 * k) for k in (1, 2, 3)])
    raw1, weights, every, got[-1], got[1] = tie(raw1, weights, every, got[-1], got[1])
    weights = pin(weights)
    every = lax.dynamic_index_in_dim(every, z, 2, False)
    gate = jnp.moveaxis(every.reshape(8, 2, 2, tokens), 2, 0).reshape(2, 8, 2 * tokens)
    gate_a, gate_b = gate[0], gate[1]

    def spread(distances, split, gates):
        return spread_tokens(distances, split, cap, where, gates, (pin(raw1), pin(raw2)))

    def bwd(distances, sides=(0, 1), share=1):
        values = [x for d in distances for x in (*got[d], *pair[d])]
        return backward(distances, cap, sides, where, pipe, values, gate_b, weights, share)

    got[-2], got[2] = hop(-1, 1), hop(1, -1)
    pair[0] = swap(0)
    raw2 = raw_forward(width // 2, width // 2, pin(hidden), weights)
    raw2, got[-2], got[2], pair[0] = tie(raw2, got[-2], got[2], pair[0])

    got[-3], got[3] = hop(-2, 1), hop(2, -1)
    keep1, other1, other2 = spread((3, -4, 2, -3), 2, gate_a)
    other1, other2 = core(other1), core(other2)
    for d in (-1, 1, -2):
        pair[d] = swap(d)
    up = step_ring(add(keep1[:tokens], other1[:tokens]), 1)
    down = step_ring(add(keep1[tokens : 2 * tokens], other1[tokens:]), -1)
    gate_a, pair[-1], pair[1], pair[-2], other2 = tie(
        gate_a, pair[-1], pair[1], pair[-2], other2
    )
    keep2, other3, other4 = spread((1, -2, -1, 0), 2, gate_a)
    keep2, gate_b = tie(keep2, gate_b)
    groups = (0, -1, 1, -2), (2, -3, 3), (-4,)
    send1, hold1 = bwd(groups[0], share=64)

    def mine(i, other, *more):
        at = slice(i * tokens, (i + 1) * tokens)
        other_at = slice(i % 2 * tokens, (i % 2 + 1) * tokens)
        return add(keep2[at], other[other_at], *more)

    send1, got[-3], got[3], up, down, other3, other4 = tie(
        send1, got[-3], got[3], up, down, other3, other4
    )
    middle = tokens // 2
    got[-4] = [step_ring(got[-3][0][:middle], 1), step_ring(got[3][0][middle:], -1)]
    up = step_ring(add(keep1[2 * tokens : 3 * tokens], other2[:tokens], up), 1)
    down = step_ring(add(keep1[3 * tokens :], other2[tokens:], down), -1)
    recv1 = across(send1)
    pair[2], pair[-3], pair[3] = swap(2), swap(-3), swap(3)
    other3, other4 = core(other3), core(other4)
    gate_b, other3, other4 = tie(gate_b, other3, other4)
    send2, hold2 = bwd(groups[1], share=64)

    hold2, send2, up, down, got[-4] = tie(hold2, send2, up, down, got[-4])
    up, down = tie(mine(0, other3, up), mine(1, other3, down))
    up, down = step_ring(up, 1), step_ring(down, -1)
    recv2 = across(send2)
    pair[-4] = swap(-4)
    send3, hold3 = bwd(groups[2], share=64)

    hold3, send3, up, down, recv1 = tie(hold3, send3, up, down, recv1)
    down = step_ring(mine(2, other4, down), -1)
    recv3 = across(send3)
    grad = collect(groups[:2], where, (hold1, recv1, hold2, recv2), 8 * rows)
    grad, down = tie(grad, down)
    mixed_a = mine(3, other4, up, down)
    mixed_a, recv3 = tie(mixed_a, recv3)
    grad = collect(groups[2:], where, (hold3, recv3), 8 * rows, grad)
    return (mixed_a, grad[None])


def solution(mesh):
    in_specs = (
        P("expert", None, None),
        P("expert", None, "pipe"),
        P("expert", None),
        P("expert", None),
        P("expert", "pipe"),
        P("expert", None),
        P("expert", None),
    )
    out_specs = (P("expert", "pipe"), P("expert", None, "pipe"))
    tailored = mesh.shape["expert"] == 16 and mesh.shape["pipe"] == 2
    return jax.shard_map(
        on_device_16 if tailored else on_device_any,
        mesh=mesh,
        in_specs=in_specs,
        out_specs=out_specs,
        check_vma=False,
    )
```

```python
import functools

import jax
import jax.numpy as jnp
from jax import lax
from jax.experimental import pallas as pl
from jax.experimental.pallas import tpu as pltpu
from jax.sharding import PartitionSpec as P

BF16, F32 = jnp.bfloat16, jnp.float32
TILE = 512
LANES = 128
RAW_TILE = 256


def dense_gates(routes, gates, total):
    experts = jnp.arange(total, dtype=jnp.int32)[:, None, None]
    return jnp.sum(jnp.where(routes[None] == experts, gates[None], 0.0), axis=2)


def ranks_of(gate):
    tokens = gate.shape[-1]
    earlier = jnp.triu(jnp.ones((tokens, tokens), BF16), 1)
    counts = jnp.dot((gate > 0.0).astype(BF16), earlier, preferred_element_type=F32)
    return counts.astype(jnp.int32)


def add(*terms):
    total = terms[0].astype(F32)
    for term in terms[1:]:
        total = total + term.astype(F32)
    return total.astype(BF16)


def on_device_any(hidden_a, expert_weights, routes_a, gates_a, cotangent_b, routes_b, gates_b):
    groups = lax.axis_size("expert")
    me = lax.axis_index("expert")
    total = expert_weights.shape[0] * groups
    rows = hidden_a.shape[1]
    cap = rows // groups
    tokens, width = cotangent_b.shape
    weights = expert_weights[0]

    both = jnp.stack(
        [dense_gates(routes_a, gates_a, total), dense_gates(routes_b, gates_b, total)], axis=1
    )
    every = lax.all_gather(both, "expert", axis=0, tiled=False)
    own = lax.dynamic_index_in_dim(every, me, axis=1, keepdims=False)
    gathered = lax.all_gather(cotangent_b, "expert", axis=0, tiled=True)

    def placement(gate):
        slots = jnp.arange(cap, dtype=jnp.int32)[None, :, None]
        hit = (gate > 0.0)[:, None, :] & (ranks_of(gate)[:, None, :] == slots)
        return hit.astype(BF16), jnp.sum(jnp.where(hit, gate[:, None, :], 0.0), axis=2)

    hit_a, slot_gate_a = placement(own[:, 0])
    hit_b, slot_gate_b = placement(own[:, 1])

    outputs = jnp.einsum("rf,fd->rd", hidden_a[0], weights, preferred_element_type=F32)
    scaled = (outputs * slot_gate_a.reshape(rows, 1)).astype(BF16)
    spread = jnp.einsum(
        "sct,scd->std", hit_a, scaled.reshape(groups, cap, width), preferred_element_type=F32
    ).astype(BF16)
    mixed_a = lax.psum_scatter(
        spread.reshape(groups * tokens, width), "expert", scatter_dimension=0, tiled=True
    )
    picked = jnp.einsum(
        "sct,std->scd",
        hit_b,
        gathered.reshape(groups, tokens, width),
        preferred_element_type=F32,
    ).astype(BF16)
    partial_value = jnp.einsum(
        "rd,fd->rf", picked.reshape(rows, width), weights, preferred_element_type=F32
    )
    partial_value = (partial_value * slot_gate_b.reshape(rows, 1)).astype(BF16)
    grad = lax.psum_scatter(partial_value, "pipe", scatter_dimension=1, tiled=True)
    return (mixed_a, grad[None])


RING = [(0, 0), (1, 0), (2, 0), (3, 0), (3, 1), (2, 1), (1, 1), (0, 1)]


def step_ring(value, way):
    pairs = []
    for place, (z, y) in enumerate(RING):
        to_z, to_y = RING[(place + way) % 8]
        pairs += [(z * 4 + y * 2 + c, to_z * 4 + to_y * 2 + c) for c in range(2)]
    return lax.ppermute(value, "expert", pairs)


def xor(value, bits):
    return lax.ppermute(value, "expert", [(i, i ^ bits) for i in range(16)])


def core(value):
    return xor(value, 1)


def across(value):
    return lax.ppermute(value, "pipe", [(0, 1), (1, 0)])


def pin(value):
    return pltpu.with_memory_space_constraint(value, pltpu.HBM)


def tie(*values):
    return lax.optimization_barrier(values)


SMEM = pl.BlockSpec(memory_space=pltpu.SMEM)
VMEM = pl.BlockSpec(memory_space=pltpu.VMEM)
HBM = pl.BlockSpec(memory_space=pltpu.HBM)
ANY = pl.BlockSpec(memory_space=pl.ANY)


def kernel_call(kernel, name, inputs, out_shape, scratch, flops, moved):
    in_specs, arrays = zip(*inputs)
    return pl.pallas_call(
        kernel,
        in_specs=in_specs,
        out_specs=[VMEM] * len(out_shape),
        out_shape=out_shape,
        scratch_shapes=scratch,
        compiler_params=pltpu.CompilerParams(vmem_limit_bytes=20 * 2**20),
        cost_estimate=pl.CostEstimate(flops=flops, bytes_accessed=moved, transcendentals=0),
        name=name,
    )(*arrays)


def gates_kernel(*refs):
    sources, out, held, sems = refs[:4], refs[4], refs[5:9], refs[9]
    copies = [pltpu.make_async_copy(x, y, sems.at[i]) for i, (x, y) in enumerate(zip(sources, held))]
    for copy in copies:
        copy.start()
    for copy in copies:
        copy.wait()
    top, tokens = held[0].shape
    experts = lax.broadcasted_iota(jnp.int32, (out.shape[0], tokens), 0)
    for i in range(2):
        routes, gates = held[2 * i : 2 * i + 2]
        total = jnp.zeros(experts.shape, F32)
        for k in range(top):
            total += jnp.where(routes[k : k + 1, :] == experts, gates[k : k + 1, :], 0.0)
        out[:, pl.ds(i * tokens, tokens)] = total


def gates_of(*arrays):
    tokens, top = arrays[0].shape
    arrays = [pin(x.T) for x in arrays]
    return kernel_call(
        gates_kernel,
        "gates",
        [(HBM, x) for x in arrays],
        [jax.ShapeDtypeStruct((16, 2 * tokens), F32)],
        [pltpu.VMEM((top, tokens), x.dtype) for x in arrays] + [pltpu.SemaphoreType.DMA((4,))],
        flops=2**20,
        moved=2**17,
    )[0]


def place_slots(distances, where, gates, cap, target, place, slot_gates):
    gate = gates[...]
    tokens = gate.shape[1] // 2
    row = lax.broadcasted_iota(jnp.int32, (2 * tokens, 2 * tokens), 0)
    col = lax.broadcasted_iota(jnp.int32, (2 * tokens, 2 * tokens), 1)
    earlier = ((row < col) & (row // tokens == col // tokens)).astype(F32).astype(BF16)
    chosen = (gate > 0.0).astype(F32).astype(BF16)
    rank = jnp.dot(chosen, earlier, preferred_element_type=F32)
    second = (lax.broadcasted_iota(jnp.int32, gate.shape, 1) // tokens) ^ where[8]
    target[...] = jnp.where(gate > 0.0, rank + (second * cap).astype(F32), -1.0)
    slots = lax.broadcasted_iota(jnp.int32, (2 * cap, 2 * tokens), 0).astype(F32)
    for i, d in enumerate(distances):
        block = pl.ds(where[9 + d % 8], 1)
        hit = target[block, :] == slots
        place[i] = hit.astype(F32).astype(BF16)
        total = jnp.sum(jnp.where(hit, gates[block, :], 0.0), axis=1, keepdims=True)
        slot_gates[pl.ds(i * 2 * cap, 2 * cap), :] = jnp.broadcast_to(total, (2 * cap, LANES))


def place_scratch(count, gates, cap):
    return [
        pltpu.VMEM(gates.shape, F32),
        pltpu.VMEM((count, 2 * cap, gates.shape[1]), BF16),
        pltpu.VMEM((count * 2 * cap, LANES), F32),
    ]


def gated(value, slot_gates):
    factor = jnp.concatenate([slot_gates] * (value.shape[1] // LANES), axis=1)
    return (value * factor).astype(BF16)


class Stream:
    def __init__(self, tile, buffer, sems):
        self.tile, self.buffer, self.sems = tile, buffer, sems
        self.slots, self.parts = sems.shape

    def copies(self, n):
        slot = n % self.slots
        rows = self.buffer.shape[1] // self.parts
        source = self.tile(n)
        for part in range(self.parts):
            at = pl.ds(part * rows, rows)
            yield pltpu.make_async_copy(
                source.at[at, :], self.buffer.at[slot, at, :], self.sems.at[slot, part]
            )

    def start(self, n):
        for copy in self.copies(n):
            copy.start()

    def wait(self, n):
        for copy in self.copies(n):
            copy.wait()


def raw_kernel(first, hidden, weights, out, held, held_sems, buffer, sems, staged, out_sems):
    tiles = out.shape[1] // RAW_TILE
    stream = Stream(
        lambda n: weights.at[:, pl.ds(pl.multiple_of(first + n * RAW_TILE, RAW_TILE), RAW_TILE)], buffer, sems
    )
    rows = held.shape[0] // held_sems.shape[0]
    fetch = []
    for i in range(held_sems.shape[0]):
        at = pl.ds(i * rows, rows)
        fetch.append(pltpu.make_async_copy(hidden.at[at, :], held.at[at, :], held_sems.at[i]))
        fetch[-1].start()
    stream.start(0)

    def put(n):
        cols = pl.ds(pl.multiple_of(n * RAW_TILE, RAW_TILE), RAW_TILE)
        return pltpu.make_async_copy(staged.at[n % 2], out.at[:, cols], out_sems.at[n % 2])

    for copy in fetch:
        copy.wait()
    for n in range(1, stream.slots):
        stream.start(n)

    @pl.loop(0, tiles)
    def _(n):
        stream.wait(n)

        @pl.when(n >= 2)
        def _():
            put(n - 2).wait()

        value = jnp.dot(held[...], buffer[n % stream.slots], preferred_element_type=F32)
        staged[n % 2] = value.astype(BF16)
        put(n).start()

        @pl.when(n + stream.slots < tiles)
        def _():
            stream.start(n + stream.slots)

    put(tiles - 2).wait()
    put(tiles - 1).wait()


def raw_forward(first, width, hidden, weights):
    rows, depth = hidden.shape
    return pl.pallas_call(
        functools.partial(raw_kernel, first),
        in_specs=[HBM, HBM],
        out_specs=HBM,
        out_shape=pltpu.HBM((rows, width), BF16),
        scratch_shapes=[
            pltpu.VMEM(hidden.shape, BF16),
            pltpu.SemaphoreType.DMA((4,)),
            pltpu.VMEM((3, depth, RAW_TILE), BF16),
            pltpu.SemaphoreType.DMA((3, 4)),
            pltpu.VMEM((2, rows, RAW_TILE), BF16),
            pltpu.SemaphoreType.DMA((2,)),
        ],
        compiler_params=pltpu.CompilerParams(vmem_limit_bytes=20 * 2**20),
        cost_estimate=pl.CostEstimate(
            flops=2 * rows * depth * width,
            bytes_accessed=2 * (depth * width + rows * (depth + width)),
            transcendentals=0,
        ),
        name="raw_forward",
    )(hidden, weights)


def spread_kernel(distances, split, cap, where, gates, *refs):
    count = len(distances)
    raws, (keep, *others), scratch = refs[:2], refs[2:-6], refs[-6:]
    target, place, slot_gates, to_tokens, held, sems = scratch
    rows, half = 2 * cap, gates.shape[1] // 2
    width = raws[0].shape[1]

    def fetch(i, start):
        return [
            pltpu.make_async_copy(
                raw.at[pl.ds(start, rows), :],
                held.at[i, :, pl.ds(j * width, width)],
                sems.at[i, j],
            )
            for j, raw in enumerate(raws)
        ]

    for i, d in enumerate(distances):
        for copy in fetch(i, pl.multiple_of(where[d % 8] * rows, rows)):
            copy.start()
    place_slots(distances, where, gates, cap, target, place, slot_gates)
    tokens = 2 * half
    same = lax.broadcasted_iota(jnp.int32, (tokens, tokens), 0) == lax.broadcasted_iota(
        jnp.int32, (tokens, tokens), 1
    )
    same = same.astype(F32).astype(BF16)
    for i in range(count):
        to_tokens[i] = lax.dot_general(
            same, place[i], (((1,), (1,)), ((), ())), preferred_element_type=F32
        ).astype(BF16)
    for g, other in enumerate(others):

        @pl.loop(0, split)
        def _(j):
            i = g * split + j
            for copy in fetch(i, 0):
                copy.wait()
            for n in range(2 * width // TILE):
                cols = pl.ds(n * TILE, TILE)
                part = held[i, :, cols].astype(F32)
                part = gated(part, slot_gates[pl.ds(pl.multiple_of(i * rows, rows), rows), :])
                part = jnp.dot(to_tokens[i], part, preferred_element_type=F32).astype(BF16)
                keep[pl.ds(pl.multiple_of(i * half, half), half), cols] = part[:half]
                other[pl.ds(pl.multiple_of(j * half, half), half), cols] = part[half:]


def spread_tokens(distances, split, cap, where, gates, raws):
    count, half, width = len(distances), gates.shape[1] // 2, 2 * raws[0].shape[1]
    return kernel_call(
        functools.partial(spread_kernel, distances, split, cap),
        "spread_tokens",
        [(SMEM, where), (VMEM, gates), (HBM, raws[0]), (HBM, raws[1])],
        [jax.ShapeDtypeStruct((count * half, width), BF16)]
        + [jax.ShapeDtypeStruct((split * half, width), BF16)] * (count // split),
        [
            *place_scratch(count, gates, cap),
            pltpu.VMEM((count, 2 * half, 2 * cap), BF16),
            pltpu.VMEM((count, 2 * cap, width), BF16),
            pltpu.SemaphoreType.DMA((count, 2)),
        ],
        flops=2**20,
        moved=2**14,
    )


def backward_kernel(distances, cap, sides, where, pipe, gates, weights, *refs):
    count, rows = len(distances), 2 * cap
    tokens, outs = refs[: 2 * count], refs[2 * count : 2 * count + len(sides)]
    block, block_sems, picked, target, place, slot_gates, buffer, sems = refs[
        2 * count + len(sides) :
    ]
    half, tile = tokens[0].shape[0], buffer.shape[1]
    tiles = 4 * len(sides)
    first = (1 - pipe[0] + sides[0]) * 4

    def weight_tile(n):
        return weights.at[pl.ds(pl.multiple_of((first + n) % 8 * tile, tile), tile), :]

    fetch = []
    for i, token in enumerate(tokens):
        to = block.at[i // 2, pl.ds(i % 2 * half, half), :]
        fetch.append(pltpu.make_async_copy(token, to, block_sems.at[i]))
        fetch[-1].start()
    stream = Stream(weight_tile, buffer, sems)
    for n in range(stream.slots):
        stream.start(n)
    place_slots(distances, where, gates, cap, target, place, slot_gates)
    for copy in fetch:
        copy.wait()

    @pl.loop(0, count)
    def _(i):
        for n in range(block.shape[2] // TILE):
            cols = pl.ds(n * TILE, TILE)
            picked[pl.ds(pl.multiple_of(i * rows, rows), rows), cols] = jnp.dot(
                place[i], block[i, :, cols], preferred_element_type=F32
            ).astype(BF16)

    @pl.loop(0, tiles)
    def _(n):
        stream.wait(n)
        value = lax.dot_general(
            picked[...],
            buffer[n % stream.slots],
            (((1,), (1,)), ((), ())),
            preferred_element_type=F32,
        )
        value = gated(value, slot_gates[...])
        cols = pl.ds(pl.multiple_of(n % 4 * tile, tile), tile)
        for i, out in enumerate(outs):

            @pl.when(n // 4 == i)
            def _():
                out[:, cols] = value

        @pl.when(n + stream.slots < tiles)
        def _():
            stream.start(n + stream.slots)


def backward(distances, cap, sides, where, pipe, tokens, gates, weights, share):
    count, rows = len(distances), 2 * cap
    depth, width = weights.shape
    return kernel_call(
        functools.partial(backward_kernel, distances, cap, sides),
        "backward",
        [(SMEM, where), (SMEM, pipe), (VMEM, gates), (HBM, weights)] + [(ANY, x) for x in tokens],
        [jax.ShapeDtypeStruct((count * rows, depth // 2), BF16)] * len(sides),
        [
            pltpu.VMEM((count, gates.shape[1], width), BF16),
            pltpu.SemaphoreType.DMA((2 * count,)),
            pltpu.VMEM((count * rows, width), BF16),
            *place_scratch(count, gates, cap),
            pltpu.VMEM((4, depth // 8, width), BF16),
            pltpu.SemaphoreType.DMA((4, 4)),
        ],
        flops=len(sides) * count * rows * depth * width // share,
        moved=2 * (depth * width + count * rows * (depth + 2 * width)) // share,
    )


def collect_kernel(groups, where, *refs):
    out, held, sems = refs[-3:]
    copies = []
    for g, distances in enumerate(groups):
        hold, recv = refs[2 * g], refs[2 * g + 1]
        rows = hold.shape[0] // len(distances)
        for i, d in enumerate(distances):
            at, n = pl.ds(i * rows, rows), len(copies)
            held[n] = (hold[at, :].astype(F32) + recv[at, :].astype(F32)).astype(BF16)
            to = pl.ds(pl.multiple_of(where[d % 8] * rows, rows), rows)
            copies.append(pltpu.make_async_copy(held.at[n], out.at[to, :], sems.at[n]))
            copies[-1].start()
    for copy in copies:
        copy.wait()


def collect(groups, where, arrays, rows, into=None):
    count = sum(len(distances) for distances in groups)
    out = jax.ShapeDtypeStruct((rows, arrays[0].shape[1]), BF16)
    inputs = [(SMEM, where)] + [(VMEM, x) for x in arrays]
    if into is not None:
        inputs.append((HBM, into))
    in_specs, arrays = zip(*inputs)
    return pl.pallas_call(
        functools.partial(collect_kernel, groups),
        in_specs=in_specs,
        out_specs=HBM,
        out_shape=out,
        scratch_shapes=[
            pltpu.VMEM((count, rows // 8, out.shape[1]), BF16),
            pltpu.SemaphoreType.DMA((count,)),
        ],
        input_output_aliases={} if into is None else {len(inputs) - 1: 0},
        compiler_params=pltpu.CompilerParams(vmem_limit_bytes=20 * 2**20),
        cost_estimate=pl.CostEstimate(
            flops=2**20, bytes_accessed=6 * count * rows * 128, transcendentals=0
        ),
        name="collect",
    )(*arrays)


def on_device_16(hidden_a, expert_weights, routes_a, gates_a, cotangent_b, routes_b, gates_b):
    me = lax.axis_index("expert").astype(jnp.int32)
    z, y, c = me // 4, me // 2 % 2, me % 2
    pipe = lax.axis_index("pipe").astype(jnp.int32).reshape(1)
    rows = hidden_a.shape[1] // 8
    cap = rows // 2
    tokens, width = cotangent_b.shape
    weights, hidden = expert_weights[0], hidden_a[0]

    ring = (jnp.where(y == 0, z, 7 - z) + jnp.arange(8, dtype=jnp.int32)) % 8
    to_z, to_y = jnp.minimum(ring, 7 - ring), (ring > 3).astype(jnp.int32)
    chips = to_z * 2 + to_y
    where = jnp.concatenate([chips, c.reshape(1), (to_z ^ z) * 2 + (to_y ^ y)])

    got, pair = {0: cotangent_b}, {}
    got[-1], got[1] = step_ring(cotangent_b, 1), step_ring(cotangent_b, -1)

    both = gates_of(routes_a, gates_a, routes_b, gates_b)
    four = jnp.stack([both] + [xor(both, j) for j in (1, 2, 3)])
    four = lax.dynamic_index_in_dim(four.reshape(4, 4, 4, 2 * tokens), me % 4, 2, False)
    weights, four = tie(weights, four)
    raw1 = raw_forward(0, width // 2, pin(hidden), pin(weights))
    every = jnp.stack([four] + [xor(four, 4 * k) for k in (1, 2, 3)])
    raw1, weights, every, got[-1], got[1] = tie(raw1, weights, every, got[-1], got[1])
    weights = pin(weights)
    every = lax.dynamic_index_in_dim(every, z, 2, False)
    gate = jnp.moveaxis(every.reshape(8, 2, 2, tokens), 2, 0).reshape(2, 8, 2 * tokens)
    gate_a, gate_b = gate[0], gate[1]

    def spread(distances, split, gates):
        return spread_tokens(distances, split, cap, where, gates, (pin(raw1), pin(raw2)))

    def bwd(distances, sides=(0, 1), share=1):
        values = [x for d in distances for x in (got[d], pair[d])]
        return backward(distances, cap, sides, where, pipe, values, gate_b, weights, share)

    got[-2], got[2] = step_ring(got[-1], 1), step_ring(got[1], -1)
    pair[0] = core(got[0])
    raw2 = raw_forward(width // 2, width // 2, pin(hidden), weights)
    raw2, pair[0] = tie(raw2, pair[0])

    keep1, other1, other2 = spread((3, -4, 2, -3), 2, gate_a)
    keep1, other1, other2, got[-2], got[2] = tie(keep1, other1, other2, got[-2], got[2])
    got[-3], got[3] = step_ring(got[-2], 1), step_ring(got[2], -1)
    other1, other2 = core(other1), core(other2)
    for d in (-1, 1, -2):
        pair[d] = core(got[d])
    up = step_ring(add(keep1[:tokens], other1[:tokens]), 1)
    down = step_ring(add(keep1[tokens : 2 * tokens], other1[tokens:]), -1)
    gate_a, pair[-1], pair[1], pair[-2], other2 = tie(
        gate_a, pair[-1], pair[1], pair[-2], other2
    )
    keep2, other3, other4 = spread((1, -2, -1, 0), 2, gate_a)
    keep2, gate_b = tie(keep2, gate_b)
    groups = (0, -1, 1, -2), (2, -3, 3), (-4,)
    send1, hold1 = bwd(groups[0], share=64)

    def mine(i, other, *more):
        at = slice(i * tokens, (i + 1) * tokens)
        other_at = slice(i % 2 * tokens, (i % 2 + 1) * tokens)
        return add(keep2[at], other[other_at], *more)

    send1, got[-3], got[3], up, down, other3, other4 = tie(
        send1, got[-3], got[3], up, down, other3, other4
    )
    got[-4] = step_ring(got[-3], 1)
    down = step_ring(add(keep1[3 * tokens :], other2[tokens:], down), -1)
    recv1 = across(send1)
    pair[2], pair[-3], pair[3] = core(got[2]), core(got[-3]), core(got[3])
    other3, other4 = core(other3), core(other4)
    gate_b, other3, other4 = tie(gate_b, other3, other4)
    send2, hold2 = bwd(groups[1], share=64)

    hold2, send2, up, down, got[-4] = tie(hold2, send2, up, down, got[-4])
    up = step_ring(add(keep1[2 * tokens : 3 * tokens], other2[:tokens], up), 1)
    down = step_ring(mine(1, other3, down), -1)
    pair[-4] = core(got[-4])
    recv2 = across(send2)
    send3, hold3 = bwd(groups[2], share=64)

    send3, hold3, up, down, recv1 = tie(send3, hold3, up, down, recv1)
    up, down = step_ring(mine(0, other3, up), 1), step_ring(mine(2, other4, down), -1)
    recv3 = across(send3)
    hold3, recv2 = tie(hold3, recv2)
    grad = collect(groups[:2], where, (hold1, recv1, hold2, recv2), 8 * rows)
    grad, up, down, recv3 = tie(grad, up, down, recv3)
    mixed_a = mine(3, other4, up, down)
    grad = collect(groups[2:], where, (hold3, recv3), 8 * rows, grad)
    return (mixed_a, grad[None])


def solution(mesh):
    in_specs = (
        P("expert", None, None),
        P("expert", None, "pipe"),
        P("expert", None),
        P("expert", None),
        P("expert", "pipe"),
        P("expert", None),
        P("expert", None),
    )
    out_specs = (P("expert", "pipe"), P("expert", None, "pipe"))
    tailored = mesh.shape["expert"] == 16 and mesh.shape["pipe"] == 2
    return jax.shard_map(
        on_device_16 if tailored else on_device_any,
        mesh=mesh,
        in_specs=in_specs,
        out_specs=out_specs,
        check_vma=False,
    )
```

```python
import functools

import jax
import jax.numpy as jnp
from jax import lax
from jax.experimental import pallas as pl
from jax.experimental.pallas import tpu as pltpu
from jax.sharding import PartitionSpec as P

BF16, F32 = jnp.bfloat16, jnp.float32
TILE = 512
LANES = 128
RAW_TILE = 256


def dense_gates(routes, gates, total):
    experts = jnp.arange(total, dtype=jnp.int32)[:, None, None]
    return jnp.sum(jnp.where(routes[None] == experts, gates[None], 0.0), axis=2)


def ranks_of(gate):
    tokens = gate.shape[-1]
    earlier = jnp.triu(jnp.ones((tokens, tokens), BF16), 1)
    counts = jnp.dot((gate > 0.0).astype(BF16), earlier, preferred_element_type=F32)
    return counts.astype(jnp.int32)


def add(*terms):
    total = terms[0].astype(F32)
    for term in terms[1:]:
        total = total + term.astype(F32)
    return total.astype(BF16)


def on_device_any(hidden_a, expert_weights, routes_a, gates_a, cotangent_b, routes_b, gates_b):
    groups = lax.axis_size("expert")
    me = lax.axis_index("expert")
    total = expert_weights.shape[0] * groups
    rows = hidden_a.shape[1]
    cap = rows // groups
    tokens, width = cotangent_b.shape
    weights = expert_weights[0]

    both = jnp.stack(
        [dense_gates(routes_a, gates_a, total), dense_gates(routes_b, gates_b, total)], axis=1
    )
    every = lax.all_gather(both, "expert", axis=0, tiled=False)
    own = lax.dynamic_index_in_dim(every, me, axis=1, keepdims=False)
    gathered = lax.all_gather(cotangent_b, "expert", axis=0, tiled=True)

    def placement(gate):
        slots = jnp.arange(cap, dtype=jnp.int32)[None, :, None]
        hit = (gate > 0.0)[:, None, :] & (ranks_of(gate)[:, None, :] == slots)
        return hit.astype(BF16), jnp.sum(jnp.where(hit, gate[:, None, :], 0.0), axis=2)

    hit_a, slot_gate_a = placement(own[:, 0])
    hit_b, slot_gate_b = placement(own[:, 1])

    outputs = jnp.einsum("rf,fd->rd", hidden_a[0], weights, preferred_element_type=F32)
    scaled = (outputs * slot_gate_a.reshape(rows, 1)).astype(BF16)
    spread = jnp.einsum(
        "sct,scd->std", hit_a, scaled.reshape(groups, cap, width), preferred_element_type=F32
    ).astype(BF16)
    mixed_a = lax.psum_scatter(
        spread.reshape(groups * tokens, width), "expert", scatter_dimension=0, tiled=True
    )
    picked = jnp.einsum(
        "sct,std->scd",
        hit_b,
        gathered.reshape(groups, tokens, width),
        preferred_element_type=F32,
    ).astype(BF16)
    partial_value = jnp.einsum(
        "rd,fd->rf", picked.reshape(rows, width), weights, preferred_element_type=F32
    )
    partial_value = (partial_value * slot_gate_b.reshape(rows, 1)).astype(BF16)
    grad = lax.psum_scatter(partial_value, "pipe", scatter_dimension=1, tiled=True)
    return (mixed_a, grad[None])


RING = [(0, 0), (1, 0), (2, 0), (3, 0), (3, 1), (2, 1), (1, 1), (0, 1)]


def step_ring(value, way):
    pairs = []
    for place, (z, y) in enumerate(RING):
        to_z, to_y = RING[(place + way) % 8]
        pairs += [(z * 4 + y * 2 + c, to_z * 4 + to_y * 2 + c) for c in range(2)]
    return lax.ppermute(value, "expert", pairs)


def xor(value, bits):
    return lax.ppermute(value, "expert", [(i, i ^ bits) for i in range(16)])


def core(value):
    return xor(value, 1)


def across(value):
    return lax.ppermute(value, "pipe", [(0, 1), (1, 0)])


def pin(value):
    return pltpu.with_memory_space_constraint(value, pltpu.HBM)


def tie(*values):
    return lax.optimization_barrier(values)


SMEM = pl.BlockSpec(memory_space=pltpu.SMEM)
VMEM = pl.BlockSpec(memory_space=pltpu.VMEM)
HBM = pl.BlockSpec(memory_space=pltpu.HBM)
ANY = pl.BlockSpec(memory_space=pl.ANY)


def kernel_call(kernel, name, inputs, out_shape, scratch, flops, moved):
    in_specs, arrays = zip(*inputs)
    return pl.pallas_call(
        kernel,
        in_specs=in_specs,
        out_specs=[VMEM] * len(out_shape),
        out_shape=out_shape,
        scratch_shapes=scratch,
        compiler_params=pltpu.CompilerParams(vmem_limit_bytes=20 * 2**20),
        cost_estimate=pl.CostEstimate(flops=flops, bytes_accessed=moved, transcendentals=0),
        name=name,
    )(*arrays)


def gates_kernel(*refs):
    sources, out, held, sems = refs[:4], refs[4], refs[5:9], refs[9]
    copies = [pltpu.make_async_copy(x, y, sems.at[i]) for i, (x, y) in enumerate(zip(sources, held))]
    for copy in copies:
        copy.start()
    for copy in copies:
        copy.wait()
    top, tokens = held[0].shape
    experts = lax.broadcasted_iota(jnp.int32, (out.shape[0], tokens), 0)
    for i in range(2):
        routes, gates = held[2 * i : 2 * i + 2]
        total = jnp.zeros(experts.shape, F32)
        for k in range(top):
            total += jnp.where(routes[k : k + 1, :] == experts, gates[k : k + 1, :], 0.0)
        out[:, pl.ds(i * tokens, tokens)] = total


def gates_of(*arrays):
    tokens, top = arrays[0].shape
    arrays = [pin(x.T) for x in arrays]
    return kernel_call(
        gates_kernel,
        "gates",
        [(HBM, x) for x in arrays],
        [jax.ShapeDtypeStruct((16, 2 * tokens), F32)],
        [pltpu.VMEM((top, tokens), x.dtype) for x in arrays] + [pltpu.SemaphoreType.DMA((4,))],
        flops=2**20,
        moved=2**17,
    )[0]


def place_slots(distances, where, gates, cap, target, place, slot_gates):
    gate = gates[...]
    tokens = gate.shape[1] // 2
    row = lax.broadcasted_iota(jnp.int32, (2 * tokens, 2 * tokens), 0)
    col = lax.broadcasted_iota(jnp.int32, (2 * tokens, 2 * tokens), 1)
    earlier = ((row < col) & (row // tokens == col // tokens)).astype(F32).astype(BF16)
    chosen = (gate > 0.0).astype(F32).astype(BF16)
    rank = jnp.dot(chosen, earlier, preferred_element_type=F32)
    second = (lax.broadcasted_iota(jnp.int32, gate.shape, 1) // tokens) ^ where[8]
    target[...] = jnp.where(gate > 0.0, rank + (second * cap).astype(F32), -1.0)
    slots = lax.broadcasted_iota(jnp.int32, (2 * cap, 2 * tokens), 0).astype(F32)
    for i, d in enumerate(distances):
        block = pl.ds(where[9 + d % 8], 1)
        hit = target[block, :] == slots
        place[i] = hit.astype(F32).astype(BF16)
        total = jnp.sum(jnp.where(hit, gates[block, :], 0.0), axis=1, keepdims=True)
        slot_gates[pl.ds(i * 2 * cap, 2 * cap), :] = jnp.broadcast_to(total, (2 * cap, LANES))


def place_scratch(count, gates, cap):
    return [
        pltpu.VMEM(gates.shape, F32),
        pltpu.VMEM((count, 2 * cap, gates.shape[1]), BF16),
        pltpu.VMEM((count * 2 * cap, LANES), F32),
    ]


def gated(value, slot_gates):
    factor = jnp.concatenate([slot_gates] * (value.shape[1] // LANES), axis=1)
    return (value * factor).astype(BF16)


class Stream:
    def __init__(self, tile, buffer, sems):
        self.tile, self.buffer, self.sems = tile, buffer, sems
        self.slots, self.parts = sems.shape

    def copies(self, n):
        slot = n % self.slots
        rows = self.buffer.shape[1] // self.parts
        source = self.tile(n)
        for part in range(self.parts):
            at = pl.ds(part * rows, rows)
            yield pltpu.make_async_copy(
                source.at[at, :], self.buffer.at[slot, at, :], self.sems.at[slot, part]
            )

    def start(self, n):
        for copy in self.copies(n):
            copy.start()

    def wait(self, n):
        for copy in self.copies(n):
            copy.wait()


def raw_kernel(first, hidden, weights, out, held, held_sems, buffer, sems, staged, out_sems):
    tiles = out.shape[1] // RAW_TILE
    stream = Stream(
        lambda n: weights.at[:, pl.ds(pl.multiple_of(first + n * RAW_TILE, RAW_TILE), RAW_TILE)], buffer, sems
    )
    rows = held.shape[0] // held_sems.shape[0]
    fetch = []
    for i in range(held_sems.shape[0]):
        at = pl.ds(i * rows, rows)
        fetch.append(pltpu.make_async_copy(hidden.at[at, :], held.at[at, :], held_sems.at[i]))
        fetch[-1].start()
    stream.start(0)

    def put(n):
        cols = pl.ds(pl.multiple_of(n * RAW_TILE, RAW_TILE), RAW_TILE)
        return pltpu.make_async_copy(staged.at[n % 2], out.at[:, cols], out_sems.at[n % 2])

    for copy in fetch:
        copy.wait()
    for n in range(1, stream.slots):
        stream.start(n)

    @pl.loop(0, tiles)
    def _(n):
        stream.wait(n)

        @pl.when(n >= 2)
        def _():
            put(n - 2).wait()

        value = jnp.dot(held[...], buffer[n % stream.slots], preferred_element_type=F32)
        staged[n % 2] = value.astype(BF16)
        put(n).start()

        @pl.when(n + stream.slots < tiles)
        def _():
            stream.start(n + stream.slots)

    put(tiles - 2).wait()
    put(tiles - 1).wait()


def raw_forward(first, width, hidden, weights):
    rows, depth = hidden.shape
    return pl.pallas_call(
        functools.partial(raw_kernel, first),
        in_specs=[HBM, HBM],
        out_specs=HBM,
        out_shape=pltpu.HBM((rows, width), BF16),
        scratch_shapes=[
            pltpu.VMEM(hidden.shape, BF16),
            pltpu.SemaphoreType.DMA((4,)),
            pltpu.VMEM((3, depth, RAW_TILE), BF16),
            pltpu.SemaphoreType.DMA((3, 4)),
            pltpu.VMEM((2, rows, RAW_TILE), BF16),
            pltpu.SemaphoreType.DMA((2,)),
        ],
        compiler_params=pltpu.CompilerParams(vmem_limit_bytes=20 * 2**20),
        cost_estimate=pl.CostEstimate(
            flops=2 * rows * depth * width,
            bytes_accessed=2 * (depth * width + rows * (depth + width)),
            transcendentals=0,
        ),
        name="raw_forward",
    )(hidden, weights)


def spread_kernel(distances, split, cap, where, gates, *refs):
    count = len(distances)
    raws, (keep, *others), scratch = refs[:2], refs[2:-6], refs[-6:]
    target, place, slot_gates, to_tokens, held, sems = scratch
    rows, half = 2 * cap, gates.shape[1] // 2
    width = raws[0].shape[1]

    def fetch(i, start):
        return [
            pltpu.make_async_copy(
                raw.at[pl.ds(start, rows), :],
                held.at[i, :, pl.ds(j * width, width)],
                sems.at[i, j],
            )
            for j, raw in enumerate(raws)
        ]

    for i, d in enumerate(distances):
        for copy in fetch(i, pl.multiple_of(where[d % 8] * rows, rows)):
            copy.start()
    place_slots(distances, where, gates, cap, target, place, slot_gates)
    tokens = 2 * half
    same = lax.broadcasted_iota(jnp.int32, (tokens, tokens), 0) == lax.broadcasted_iota(
        jnp.int32, (tokens, tokens), 1
    )
    same = same.astype(F32).astype(BF16)
    for i in range(count):
        to_tokens[i] = lax.dot_general(
            same, place[i], (((1,), (1,)), ((), ())), preferred_element_type=F32
        ).astype(BF16)
    for g, other in enumerate(others):

        @pl.loop(0, split)
        def _(j):
            i = g * split + j
            for copy in fetch(i, 0):
                copy.wait()
            for n in range(2 * width // TILE):
                cols = pl.ds(n * TILE, TILE)
                part = held[i, :, cols].astype(F32)
                part = gated(part, slot_gates[pl.ds(pl.multiple_of(i * rows, rows), rows), :])
                part = jnp.dot(to_tokens[i], part, preferred_element_type=F32).astype(BF16)
                keep[pl.ds(pl.multiple_of(i * half, half), half), cols] = part[:half]
                other[pl.ds(pl.multiple_of(j * half, half), half), cols] = part[half:]


def spread_tokens(distances, split, cap, where, gates, raws):
    count, half, width = len(distances), gates.shape[1] // 2, 2 * raws[0].shape[1]
    return kernel_call(
        functools.partial(spread_kernel, distances, split, cap),
        "spread_tokens",
        [(SMEM, where), (VMEM, gates), (HBM, raws[0]), (HBM, raws[1])],
        [jax.ShapeDtypeStruct((count * half, width), BF16)]
        + [jax.ShapeDtypeStruct((split * half, width), BF16)] * (count // split),
        [
            *place_scratch(count, gates, cap),
            pltpu.VMEM((count, 2 * half, 2 * cap), BF16),
            pltpu.VMEM((count, 2 * cap, width), BF16),
            pltpu.SemaphoreType.DMA((count, 2)),
        ],
        flops=2**20,
        moved=2**14,
    )


def backward_kernel(distances, cap, sides, where, pipe, gates, weights, *refs):
    count, rows = len(distances), 2 * cap
    tokens, outs = refs[: 2 * count], refs[2 * count : 2 * count + len(sides)]
    block, block_sems, picked, target, place, slot_gates, buffer, sems = refs[
        2 * count + len(sides) :
    ]
    half, tile = tokens[0].shape[0], buffer.shape[1]
    tiles = 4 * len(sides)
    first = (1 - pipe[0] + sides[0]) * 4

    def weight_tile(n):
        return weights.at[pl.ds(pl.multiple_of((first + n) % 8 * tile, tile), tile), :]

    fetch = []
    for i, token in enumerate(tokens):
        to = block.at[i // 2, pl.ds(i % 2 * half, half), :]
        fetch.append(pltpu.make_async_copy(token, to, block_sems.at[i]))
        fetch[-1].start()
    stream = Stream(weight_tile, buffer, sems)
    for n in range(stream.slots):
        stream.start(n)
    place_slots(distances, where, gates, cap, target, place, slot_gates)
    for copy in fetch:
        copy.wait()

    @pl.loop(0, count)
    def _(i):
        for n in range(block.shape[2] // TILE):
            cols = pl.ds(n * TILE, TILE)
            picked[pl.ds(pl.multiple_of(i * rows, rows), rows), cols] = jnp.dot(
                place[i], block[i, :, cols], preferred_element_type=F32
            ).astype(BF16)

    @pl.loop(0, tiles)
    def _(n):
        stream.wait(n)
        value = lax.dot_general(
            picked[...],
            buffer[n % stream.slots],
            (((1,), (1,)), ((), ())),
            preferred_element_type=F32,
        )
        value = gated(value, slot_gates[...])
        cols = pl.ds(pl.multiple_of(n % 4 * tile, tile), tile)
        for i, out in enumerate(outs):

            @pl.when(n // 4 == i)
            def _():
                out[:, cols] = value

        @pl.when(n + stream.slots < tiles)
        def _():
            stream.start(n + stream.slots)


def backward(distances, cap, sides, where, pipe, tokens, gates, weights, share):
    count, rows = len(distances), 2 * cap
    depth, width = weights.shape
    return kernel_call(
        functools.partial(backward_kernel, distances, cap, sides),
        "backward",
        [(SMEM, where), (SMEM, pipe), (VMEM, gates), (HBM, weights)] + [(ANY, x) for x in tokens],
        [jax.ShapeDtypeStruct((count * rows, depth // 2), BF16)] * len(sides),
        [
            pltpu.VMEM((count, gates.shape[1], width), BF16),
            pltpu.SemaphoreType.DMA((2 * count,)),
            pltpu.VMEM((count * rows, width), BF16),
            *place_scratch(count, gates, cap),
            pltpu.VMEM((4, depth // 8, width), BF16),
            pltpu.SemaphoreType.DMA((4, 4)),
        ],
        flops=len(sides) * count * rows * depth * width // share,
        moved=2 * (depth * width + count * rows * (depth + 2 * width)) // share,
    )


def collect_kernel(groups, where, *refs):
    out, held, sems = refs[-3:]
    copies = []
    for g, distances in enumerate(groups):
        hold, recv = refs[2 * g], refs[2 * g + 1]
        rows = hold.shape[0] // len(distances)
        for i, d in enumerate(distances):
            at, n = pl.ds(i * rows, rows), len(copies)
            held[n] = (hold[at, :].astype(F32) + recv[at, :].astype(F32)).astype(BF16)
            to = pl.ds(pl.multiple_of(where[d % 8] * rows, rows), rows)
            copies.append(pltpu.make_async_copy(held.at[n], out.at[to, :], sems.at[n]))
            copies[-1].start()
    for copy in copies:
        copy.wait()


def collect(groups, where, arrays, rows, into=None):
    count = sum(len(distances) for distances in groups)
    out = jax.ShapeDtypeStruct((rows, arrays[0].shape[1]), BF16)
    inputs = [(SMEM, where)] + [(VMEM, x) for x in arrays]
    if into is not None:
        inputs.append((HBM, into))
    in_specs, arrays = zip(*inputs)
    return pl.pallas_call(
        functools.partial(collect_kernel, groups),
        in_specs=in_specs,
        out_specs=HBM,
        out_shape=out,
        scratch_shapes=[
            pltpu.VMEM((count, rows // 8, out.shape[1]), BF16),
            pltpu.SemaphoreType.DMA((count,)),
        ],
        input_output_aliases={} if into is None else {len(inputs) - 1: 0},
        compiler_params=pltpu.CompilerParams(vmem_limit_bytes=20 * 2**20),
        cost_estimate=pl.CostEstimate(
            flops=2**20, bytes_accessed=6 * count * rows * 128, transcendentals=0
        ),
        name="collect",
    )(*arrays)


def on_device_16(hidden_a, expert_weights, routes_a, gates_a, cotangent_b, routes_b, gates_b):
    me = lax.axis_index("expert").astype(jnp.int32)
    z, y, c = me // 4, me // 2 % 2, me % 2
    pipe = lax.axis_index("pipe").astype(jnp.int32).reshape(1)
    rows = hidden_a.shape[1] // 8
    cap = rows // 2
    tokens, width = cotangent_b.shape
    weights, hidden = expert_weights[0], hidden_a[0]

    ring = (jnp.where(y == 0, z, 7 - z) + jnp.arange(8, dtype=jnp.int32)) % 8
    to_z, to_y = jnp.minimum(ring, 7 - ring), (ring > 3).astype(jnp.int32)
    chips = to_z * 2 + to_y
    where = jnp.concatenate([chips, c.reshape(1), (to_z ^ z) * 2 + (to_y ^ y)])

    got, pair = {0: cotangent_b}, {}
    got[-1], got[1] = step_ring(cotangent_b, 1), step_ring(cotangent_b, -1)

    both = gates_of(routes_a, gates_a, routes_b, gates_b)
    four = jnp.stack([both] + [xor(both, j) for j in (1, 2, 3)])
    four = lax.dynamic_index_in_dim(four.reshape(4, 4, 4, 2 * tokens), me % 4, 2, False)
    weights, four = tie(weights, four)
    raw1 = raw_forward(0, width // 2, pin(hidden), pin(weights))
    every = jnp.stack([four] + [xor(four, 4 * k) for k in (1, 2, 3)])
    raw1, weights, every, got[-1], got[1] = tie(raw1, weights, every, got[-1], got[1])
    weights = pin(weights)
    every = lax.dynamic_index_in_dim(every, z, 2, False)
    gate = jnp.moveaxis(every.reshape(8, 2, 2, tokens), 2, 0).reshape(2, 8, 2 * tokens)
    gate_a, gate_b = gate[0], gate[1]

    def spread(distances, split, gates):
        return spread_tokens(distances, split, cap, where, gates, (pin(raw1), pin(raw2)))

    def bwd(distances, sides=(0, 1), share=1):
        values = [x for d in distances for x in (got[d], pair[d])]
        return backward(distances, cap, sides, where, pipe, values, gate_b, weights, share)

    got[-2], got[2] = step_ring(got[-1], 1), step_ring(got[1], -1)
    for d in (0, -1, 1):
        pair[d] = core(got[d])
    raw2 = raw_forward(width // 2, width // 2, pin(hidden), weights)
    raw2, pair[0], pair[-1], pair[1] = tie(raw2, pair[0], pair[-1], pair[1])

    keep1, other1, other2 = spread((3, -4, 2, -3), 2, gate_a)
    keep1, other1, other2, got[-2], got[2] = tie(keep1, other1, other2, got[-2], got[2])
    got[-3], got[3] = step_ring(got[-2], 1), step_ring(got[2], -1)
    other1, other2 = core(other1), core(other2)
    up = step_ring(add(keep1[:tokens], other1[:tokens]), 1)
    down = step_ring(add(keep1[tokens : 2 * tokens], other1[tokens:]), -1)
    pair[-2] = core(got[-2])
    gate_a, pair[-2], other2 = tie(gate_a, pair[-2], other2)
    keep2, other3, other4 = spread((1, -2, -1, 0), 2, gate_a)
    keep2, gate_b = tie(keep2, gate_b)
    groups = (0, -1, 1, -2), (2, -3, 3), (-4,)
    send1, hold1 = bwd(groups[0], share=64)

    def mine(i, other, *more):
        at = slice(i * tokens, (i + 1) * tokens)
        other_at = slice(i % 2 * tokens, (i % 2 + 1) * tokens)
        return add(keep2[at], other[other_at], *more)

    send1, got[-3], got[3], up, down, other3, other4 = tie(
        send1, got[-3], got[3], up, down, other3, other4
    )
    got[-4] = step_ring(got[-3], 1)
    up = add(keep1[2 * tokens : 3 * tokens], other2[:tokens], up)
    down = add(keep1[3 * tokens :], other2[tokens:], down)
    up, down = tie(up, down)
    down = step_ring(down, -1)
    recv1 = across(send1)
    pair[2], pair[-3], pair[3] = core(got[2]), core(got[-3]), core(got[3])
    other3, other4 = core(other3), core(other4)
    gate_b, other3, other4 = tie(gate_b, other3, other4)
    send2, hold2 = bwd(groups[1], share=64)

    hold2, send2, up, down, got[-4] = tie(hold2, send2, up, down, got[-4])
    up, down = step_ring(up, 1), step_ring(mine(1, other3, down), -1)
    pair[-4] = core(got[-4])
    recv2 = across(send2)
    send3, hold3 = bwd(groups[2], share=64)

    send3, hold3, up, down, recv1 = tie(send3, hold3, up, down, recv1)
    up, down = step_ring(mine(0, other3, up), 1), step_ring(mine(2, other4, down), -1)
    recv3 = across(send3)
    hold3, recv2 = tie(hold3, recv2)
    grad = collect(groups[:2], where, (hold1, recv1, hold2, recv2), 8 * rows)
    grad, recv3 = tie(grad, recv3)
    mixed_a = mine(3, other4, up, down)
    grad = collect(groups[2:], where, (hold3, recv3), 8 * rows, grad)
    return (mixed_a, grad[None])


def solution(mesh):
    in_specs = (
        P("expert", None, None),
        P("expert", None, "pipe"),
        P("expert", None),
        P("expert", None),
        P("expert", "pipe"),
        P("expert", None),
        P("expert", None),
    )
    out_specs = (P("expert", "pipe"), P("expert", None, "pipe"))
    tailored = mesh.shape["expert"] == 16 and mesh.shape["pipe"] == 2
    return jax.shard_map(
        on_device_16 if tailored else on_device_any,
        mesh=mesh,
        in_specs=in_specs,
        out_specs=out_specs,
        check_vma=False,
    )
```

```python
import functools

import jax
import jax.numpy as jnp
from jax import lax
from jax.experimental import pallas as pl
from jax.experimental.pallas import tpu as pltpu
from jax.sharding import PartitionSpec as P

BF16, F32 = jnp.bfloat16, jnp.float32
TILE = 512
LANES = 128
RAW_TILE = 256


def dense_gates(routes, gates, total):
    experts = jnp.arange(total, dtype=jnp.int32)[:, None, None]
    return jnp.sum(jnp.where(routes[None] == experts, gates[None], 0.0), axis=2)


def ranks_of(gate):
    tokens = gate.shape[-1]
    earlier = jnp.triu(jnp.ones((tokens, tokens), BF16), 1)
    counts = jnp.dot((gate > 0.0).astype(BF16), earlier, preferred_element_type=F32)
    return counts.astype(jnp.int32)


def add(*terms):
    total = terms[0].astype(F32)
    for term in terms[1:]:
        total = total + term.astype(F32)
    return total.astype(BF16)


def on_device_any(hidden_a, expert_weights, routes_a, gates_a, cotangent_b, routes_b, gates_b):
    groups = lax.axis_size("expert")
    me = lax.axis_index("expert")
    total = expert_weights.shape[0] * groups
    rows = hidden_a.shape[1]
    cap = rows // groups
    tokens, width = cotangent_b.shape
    weights = expert_weights[0]

    both = jnp.stack(
        [dense_gates(routes_a, gates_a, total), dense_gates(routes_b, gates_b, total)], axis=1
    )
    every = lax.all_gather(both, "expert", axis=0, tiled=False)
    own = lax.dynamic_index_in_dim(every, me, axis=1, keepdims=False)
    gathered = lax.all_gather(cotangent_b, "expert", axis=0, tiled=True)

    def placement(gate):
        slots = jnp.arange(cap, dtype=jnp.int32)[None, :, None]
        hit = (gate > 0.0)[:, None, :] & (ranks_of(gate)[:, None, :] == slots)
        return hit.astype(BF16), jnp.sum(jnp.where(hit, gate[:, None, :], 0.0), axis=2)

    hit_a, slot_gate_a = placement(own[:, 0])
    hit_b, slot_gate_b = placement(own[:, 1])

    outputs = jnp.einsum("rf,fd->rd", hidden_a[0], weights, preferred_element_type=F32)
    scaled = (outputs * slot_gate_a.reshape(rows, 1)).astype(BF16)
    spread = jnp.einsum(
        "sct,scd->std", hit_a, scaled.reshape(groups, cap, width), preferred_element_type=F32
    ).astype(BF16)
    mixed_a = lax.psum_scatter(
        spread.reshape(groups * tokens, width), "expert", scatter_dimension=0, tiled=True
    )
    picked = jnp.einsum(
        "sct,std->scd",
        hit_b,
        gathered.reshape(groups, tokens, width),
        preferred_element_type=F32,
    ).astype(BF16)
    partial_value = jnp.einsum(
        "rd,fd->rf", picked.reshape(rows, width), weights, preferred_element_type=F32
    )
    partial_value = (partial_value * slot_gate_b.reshape(rows, 1)).astype(BF16)
    grad = lax.psum_scatter(partial_value, "pipe", scatter_dimension=1, tiled=True)
    return (mixed_a, grad[None])


RING = [(0, 0), (1, 0), (2, 0), (3, 0), (3, 1), (2, 1), (1, 1), (0, 1)]


def step_ring(value, way):
    pairs = []
    for place, (z, y) in enumerate(RING):
        to_z, to_y = RING[(place + way) % 8]
        pairs += [(z * 4 + y * 2 + c, to_z * 4 + to_y * 2 + c) for c in range(2)]
    return lax.ppermute(value, "expert", pairs)


def xor(value, bits):
    return lax.ppermute(value, "expert", [(i, i ^ bits) for i in range(16)])


def core(value):
    return xor(value, 1)


def across(value):
    return lax.ppermute(value, "pipe", [(0, 1), (1, 0)])


def pin(value):
    return pltpu.with_memory_space_constraint(value, pltpu.HBM)


def tie(*values):
    return lax.optimization_barrier(values)


SMEM = pl.BlockSpec(memory_space=pltpu.SMEM)
VMEM = pl.BlockSpec(memory_space=pltpu.VMEM)
HBM = pl.BlockSpec(memory_space=pltpu.HBM)
ANY = pl.BlockSpec(memory_space=pl.ANY)


def kernel_call(kernel, name, inputs, out_shape, scratch, flops, moved, limit=12):
    in_specs, arrays = zip(*inputs)
    return pl.pallas_call(
        kernel,
        in_specs=in_specs,
        out_specs=[VMEM] * len(out_shape),
        out_shape=out_shape,
        scratch_shapes=scratch,
        compiler_params=pltpu.CompilerParams(vmem_limit_bytes=limit * 2**20),
        cost_estimate=pl.CostEstimate(flops=flops, bytes_accessed=moved, transcendentals=0),
        name=name,
    )(*arrays)


def gates_kernel(*refs):
    sources, out, held, sems = refs[:4], refs[4], refs[5:9], refs[9]
    copies = [pltpu.make_async_copy(x, y, sems.at[i]) for i, (x, y) in enumerate(zip(sources, held))]
    for copy in copies:
        copy.start()
    for copy in copies:
        copy.wait()
    top, tokens = held[0].shape
    experts = lax.broadcasted_iota(jnp.int32, (out.shape[0], tokens), 0)
    for i in range(2):
        routes, gates = held[2 * i : 2 * i + 2]
        total = jnp.zeros(experts.shape, F32)
        for k in range(top):
            total += jnp.where(routes[k : k + 1, :] == experts, gates[k : k + 1, :], 0.0)
        out[:, pl.ds(i * tokens, tokens)] = total


def gates_of(*arrays):
    tokens, top = arrays[0].shape
    arrays = [pin(x.T) for x in arrays]
    return kernel_call(
        gates_kernel,
        "gates",
        [(HBM, x) for x in arrays],
        [jax.ShapeDtypeStruct((16, 2 * tokens), F32)],
        [pltpu.VMEM((top, tokens), x.dtype) for x in arrays] + [pltpu.SemaphoreType.DMA((4,))],
        flops=2**20,
        moved=2**17,
    )[0]


def place_slots(distances, where, gates, cap, target, place, slot_gates):
    gate = gates[...]
    tokens = gate.shape[1] // 2
    row = lax.broadcasted_iota(jnp.int32, (2 * tokens, 2 * tokens), 0)
    col = lax.broadcasted_iota(jnp.int32, (2 * tokens, 2 * tokens), 1)
    earlier = ((row < col) & (row // tokens == col // tokens)).astype(F32).astype(BF16)
    chosen = (gate > 0.0).astype(F32).astype(BF16)
    rank = jnp.dot(chosen, earlier, preferred_element_type=F32)
    second = (lax.broadcasted_iota(jnp.int32, gate.shape, 1) // tokens) ^ where[8]
    target[...] = jnp.where(gate > 0.0, rank + (second * cap).astype(F32), -1.0)
    slots = lax.broadcasted_iota(jnp.int32, (2 * cap, 2 * tokens), 0).astype(F32)
    for i, d in enumerate(distances):
        block = pl.ds(where[9 + d % 8], 1)
        hit = target[block, :] == slots
        place[i] = hit.astype(F32).astype(BF16)
        total = jnp.sum(jnp.where(hit, gates[block, :], 0.0), axis=1, keepdims=True)
        slot_gates[pl.ds(i * 2 * cap, 2 * cap), :] = jnp.broadcast_to(total, (2 * cap, LANES))


def place_scratch(count, gates, cap):
    return [
        pltpu.VMEM(gates.shape, F32),
        pltpu.VMEM((count, 2 * cap, gates.shape[1]), BF16),
        pltpu.VMEM((count * 2 * cap, LANES), F32),
    ]


def gated(value, slot_gates):
    factor = jnp.concatenate([slot_gates] * (value.shape[1] // LANES), axis=1)
    return (value * factor).astype(BF16)


class Stream:
    def __init__(self, tile, buffer, sems):
        self.tile, self.buffer, self.sems = tile, buffer, sems
        self.slots, self.parts = sems.shape

    def copies(self, n):
        slot = n % self.slots
        rows = self.buffer.shape[1] // self.parts
        source = self.tile(n)
        for part in range(self.parts):
            at = pl.ds(part * rows, rows)
            yield pltpu.make_async_copy(
                source.at[at, :], self.buffer.at[slot, at, :], self.sems.at[slot, part]
            )

    def start(self, n):
        for copy in self.copies(n):
            copy.start()

    def wait(self, n):
        for copy in self.copies(n):
            copy.wait()


def raw_kernel(first, hidden, weights, out, held, held_sems, buffer, sems, staged, out_sems):
    tiles = out.shape[1] // RAW_TILE
    stream = Stream(
        lambda n: weights.at[:, pl.ds(pl.multiple_of(first + n * RAW_TILE, RAW_TILE), RAW_TILE)], buffer, sems
    )
    rows = held.shape[0] // held_sems.shape[0]
    fetch = []
    for i in range(held_sems.shape[0]):
        at = pl.ds(i * rows, rows)
        fetch.append(pltpu.make_async_copy(hidden.at[at, :], held.at[at, :], held_sems.at[i]))
        fetch[-1].start()
    stream.start(0)

    def put(n):
        cols = pl.ds(pl.multiple_of(n * RAW_TILE, RAW_TILE), RAW_TILE)
        return pltpu.make_async_copy(staged.at[n % 2], out.at[:, cols], out_sems.at[n % 2])

    for copy in fetch:
        copy.wait()
    for n in range(1, stream.slots):
        stream.start(n)

    @pl.loop(0, tiles)
    def _(n):
        stream.wait(n)

        @pl.when(n >= 2)
        def _():
            put(n - 2).wait()

        value = jnp.dot(held[...], buffer[n % stream.slots], preferred_element_type=F32)
        staged[n % 2] = value.astype(BF16)
        put(n).start()

        @pl.when(n + stream.slots < tiles)
        def _():
            stream.start(n + stream.slots)

    put(tiles - 2).wait()
    put(tiles - 1).wait()


def raw_forward(first, width, hidden, weights):
    rows, depth = hidden.shape
    return pl.pallas_call(
        functools.partial(raw_kernel, first),
        in_specs=[HBM, HBM],
        out_specs=HBM,
        out_shape=pltpu.HBM((rows, width), BF16),
        scratch_shapes=[
            pltpu.VMEM(hidden.shape, BF16),
            pltpu.SemaphoreType.DMA((4,)),
            pltpu.VMEM((3, depth, RAW_TILE), BF16),
            pltpu.SemaphoreType.DMA((3, 4)),
            pltpu.VMEM((2, rows, RAW_TILE), BF16),
            pltpu.SemaphoreType.DMA((2,)),
        ],
        compiler_params=pltpu.CompilerParams(vmem_limit_bytes=12 * 2**20),
        cost_estimate=pl.CostEstimate(
            flops=2 * rows * depth * width,
            bytes_accessed=2 * (depth * width + rows * (depth + width)),
            transcendentals=0,
        ),
        name="raw_forward",
    )(hidden, weights)


def spread_kernel(distances, split, cap, where, gates, *refs):
    count = len(distances)
    raws, (keep, *others), scratch = refs[:2], refs[2:-6], refs[-6:]
    target, place, slot_gates, to_tokens, held, sems = scratch
    rows, half = 2 * cap, gates.shape[1] // 2
    width = raws[0].shape[1]

    def fetch(i, start):
        return [
            pltpu.make_async_copy(
                raw.at[pl.ds(start, rows), :],
                held.at[i, :, pl.ds(j * width, width)],
                sems.at[i, j],
            )
            for j, raw in enumerate(raws)
        ]

    for i, d in enumerate(distances):
        for copy in fetch(i, pl.multiple_of(where[d % 8] * rows, rows)):
            copy.start()
    place_slots(distances, where, gates, cap, target, place, slot_gates)
    tokens = 2 * half
    same = lax.broadcasted_iota(jnp.int32, (tokens, tokens), 0) == lax.broadcasted_iota(
        jnp.int32, (tokens, tokens), 1
    )
    same = same.astype(F32).astype(BF16)
    for i in range(count):
        to_tokens[i] = lax.dot_general(
            same, place[i], (((1,), (1,)), ((), ())), preferred_element_type=F32
        ).astype(BF16)
    for g, other in enumerate(others):

        @pl.loop(0, split)
        def _(j):
            i = g * split + j
            for copy in fetch(i, 0):
                copy.wait()
            for n in range(2 * width // TILE):
                cols = pl.ds(n * TILE, TILE)
                part = held[i, :, cols].astype(F32)
                part = gated(part, slot_gates[pl.ds(pl.multiple_of(i * rows, rows), rows), :])
                part = jnp.dot(to_tokens[i], part, preferred_element_type=F32).astype(BF16)
                keep[pl.ds(pl.multiple_of(i * half, half), half), cols] = part[:half]
                other[pl.ds(pl.multiple_of(j * half, half), half), cols] = part[half:]


def spread_tokens(distances, split, cap, where, gates, raws):
    count, half, width = len(distances), gates.shape[1] // 2, 2 * raws[0].shape[1]
    return kernel_call(
        functools.partial(spread_kernel, distances, split, cap),
        "spread_tokens",
        [(SMEM, where), (VMEM, gates), (HBM, raws[0]), (HBM, raws[1])],
        [jax.ShapeDtypeStruct((count * half, width), BF16)]
        + [jax.ShapeDtypeStruct((split * half, width), BF16)] * (count // split),
        [
            *place_scratch(count, gates, cap),
            pltpu.VMEM((count, 2 * half, 2 * cap), BF16),
            pltpu.VMEM((count, 2 * cap, width), BF16),
            pltpu.SemaphoreType.DMA((count, 2)),
        ],
        flops=2**20,
        moved=2**14,
    )


def backward_kernel(distances, cap, sides, where, pipe, gates, weights, *refs):
    count, rows = len(distances), 2 * cap
    tokens, outs = refs[: 2 * count], refs[2 * count : 2 * count + len(sides)]
    block, block_sems, picked, target, place, slot_gates, buffer, sems = refs[
        2 * count + len(sides) :
    ]
    half, tile = tokens[0].shape[0], buffer.shape[1]
    tiles = 4 * len(sides)
    first = (1 - pipe[0] + sides[0]) * 4

    def weight_tile(n):
        return weights.at[pl.ds(pl.multiple_of((first + n) % 8 * tile, tile), tile), :]

    fetch = []
    for i, token in enumerate(tokens):
        to = block.at[i // 2, pl.ds(i % 2 * half, half), :]
        fetch.append(pltpu.make_async_copy(token, to, block_sems.at[i]))
        fetch[-1].start()
    stream = Stream(weight_tile, buffer, sems)
    for n in range(stream.slots):
        stream.start(n)
    place_slots(distances, where, gates, cap, target, place, slot_gates)
    for copy in fetch:
        copy.wait()

    @pl.loop(0, count)
    def _(i):
        for n in range(block.shape[2] // TILE):
            cols = pl.ds(n * TILE, TILE)
            picked[pl.ds(pl.multiple_of(i * rows, rows), rows), cols] = jnp.dot(
                place[i], block[i, :, cols], preferred_element_type=F32
            ).astype(BF16)

    @pl.loop(0, tiles)
    def _(n):
        stream.wait(n)
        value = lax.dot_general(
            picked[...],
            buffer[n % stream.slots],
            (((1,), (1,)), ((), ())),
            preferred_element_type=F32,
        )
        value = gated(value, slot_gates[...])
        cols = pl.ds(pl.multiple_of(n % 4 * tile, tile), tile)
        for i, out in enumerate(outs):

            @pl.when(n // 4 == i)
            def _():
                out[:, cols] = value

        @pl.when(n + stream.slots < tiles)
        def _():
            stream.start(n + stream.slots)


def backward(distances, cap, sides, where, pipe, tokens, gates, weights, share):
    count, rows = len(distances), 2 * cap
    depth, width = weights.shape
    return kernel_call(
        functools.partial(backward_kernel, distances, cap, sides),
        "backward",
        [(SMEM, where), (SMEM, pipe), (VMEM, gates), (HBM, weights)] + [(ANY, x) for x in tokens],
        [jax.ShapeDtypeStruct((count * rows, depth // 2), BF16)] * len(sides),
        [
            pltpu.VMEM((count, gates.shape[1], width), BF16),
            pltpu.SemaphoreType.DMA((2 * count,)),
            pltpu.VMEM((count * rows, width), BF16),
            *place_scratch(count, gates, cap),
            pltpu.VMEM((4, depth // 8, width), BF16),
            pltpu.SemaphoreType.DMA((4, 4)),
        ],
        flops=len(sides) * count * rows * depth * width // share,
        moved=2 * (depth * width + count * rows * (depth + 2 * width)) // share,
        limit=18,
    )


def collect_kernel(groups, where, *refs):
    out, held, sems = refs[-3:]
    copies = []
    for g, distances in enumerate(groups):
        hold, recv = refs[2 * g], refs[2 * g + 1]
        rows = hold.shape[0] // len(distances)
        for i, d in enumerate(distances):
            at, n = pl.ds(i * rows, rows), len(copies)
            held[n] = (hold[at, :].astype(F32) + recv[at, :].astype(F32)).astype(BF16)
            to = pl.ds(pl.multiple_of(where[d % 8] * rows, rows), rows)
            copies.append(pltpu.make_async_copy(held.at[n], out.at[to, :], sems.at[n]))
            copies[-1].start()
    for copy in copies:
        copy.wait()


def collect(groups, where, arrays, rows, into=None):
    count = sum(len(distances) for distances in groups)
    out = jax.ShapeDtypeStruct((rows, arrays[0].shape[1]), BF16)
    inputs = [(SMEM, where)] + [(VMEM, x) for x in arrays]
    if into is not None:
        inputs.append((HBM, into))
    in_specs, arrays = zip(*inputs)
    return pl.pallas_call(
        functools.partial(collect_kernel, groups),
        in_specs=in_specs,
        out_specs=HBM,
        out_shape=out,
        scratch_shapes=[
            pltpu.VMEM((count, rows // 8, out.shape[1]), BF16),
            pltpu.SemaphoreType.DMA((count,)),
        ],
        input_output_aliases={} if into is None else {len(inputs) - 1: 0},
        compiler_params=pltpu.CompilerParams(vmem_limit_bytes=12 * 2**20),
        cost_estimate=pl.CostEstimate(
            flops=2**20, bytes_accessed=6 * count * rows * 128, transcendentals=0
        ),
        name="collect",
    )(*arrays)


def on_device_16(hidden_a, expert_weights, routes_a, gates_a, cotangent_b, routes_b, gates_b):
    me = lax.axis_index("expert").astype(jnp.int32)
    z, y, c = me // 4, me // 2 % 2, me % 2
    pipe = lax.axis_index("pipe").astype(jnp.int32).reshape(1)
    rows = hidden_a.shape[1] // 8
    cap = rows // 2
    tokens, width = cotangent_b.shape
    weights, hidden = expert_weights[0], hidden_a[0]

    ring = (jnp.where(y == 0, z, 7 - z) + jnp.arange(8, dtype=jnp.int32)) % 8
    to_z, to_y = jnp.minimum(ring, 7 - ring), (ring > 3).astype(jnp.int32)
    chips = to_z * 2 + to_y
    where = jnp.concatenate([chips, c.reshape(1), (to_z ^ z) * 2 + (to_y ^ y)])

    got, pair = {0: cotangent_b}, {}
    got[-1], got[1] = step_ring(cotangent_b, 1), step_ring(cotangent_b, -1)

    both = gates_of(routes_a, gates_a, routes_b, gates_b)
    four = jnp.stack([both] + [xor(both, j) for j in (1, 2, 3)])
    four = lax.dynamic_index_in_dim(four.reshape(4, 4, 4, 2 * tokens), me % 4, 2, False)
    weights, four = tie(weights, four)
    raw1 = raw_forward(0, width // 2, pin(hidden), pin(weights))
    every = jnp.stack([four] + [xor(four, 4 * k) for k in (1, 2, 3)])
    raw1, weights, every, got[-1], got[1] = tie(raw1, weights, every, got[-1], got[1])
    weights = pin(weights)
    every = lax.dynamic_index_in_dim(every, z, 2, False)
    gate = jnp.moveaxis(every.reshape(8, 2, 2, tokens), 2, 0).reshape(2, 8, 2 * tokens)
    gate_a, gate_b = gate[0], gate[1]

    def spread(distances, split, gates):
        return spread_tokens(distances, split, cap, where, gates, (pin(raw1), pin(raw2)))

    def bwd(distances, sides=(0, 1), share=1):
        values = [x for d in distances for x in (got[d], pair[d])]
        return backward(distances, cap, sides, where, pipe, values, gate_b, weights, share)

    got[-2], got[2] = step_ring(got[-1], 1), step_ring(got[1], -1)
    for d in (0, -1, 1):
        pair[d] = core(got[d])
    raw2 = raw_forward(width // 2, width // 2, pin(hidden), weights)
    raw2, pair[0], pair[-1], pair[1] = tie(raw2, pair[0], pair[-1], pair[1])

    keep1, other1, other2 = spread((3, -4, 2, -3), 2, gate_a)
    keep1, other1, other2, got[-2], got[2] = tie(keep1, other1, other2, got[-2], got[2])
    got[-3], got[3] = step_ring(got[-2], 1), step_ring(got[2], -1)
    other1, other2 = core(other1), core(other2)
    up = step_ring(add(keep1[:tokens], other1[:tokens]), 1)
    down = step_ring(add(keep1[tokens : 2 * tokens], other1[tokens:]), -1)
    pair[-2] = core(got[-2])
    gate_a, pair[-2], other2 = tie(gate_a, pair[-2], other2)
    keep2, other3, other4 = spread((1, -2, -1, 0), 2, gate_a)
    keep2, gate_b = tie(keep2, gate_b)
    groups = (0, -1, 1, -2), (2, -3, 3), (-4,)
    for d in (0, -1, 1):
        pair[d] = pin(pair[d])
    send1, hold1 = bwd(groups[0], share=64)

    def mine(i, other, *more):
        at = slice(i * tokens, (i + 1) * tokens)
        other_at = slice(i % 2 * tokens, (i % 2 + 1) * tokens)
        return add(keep2[at], other[other_at], *more)

    send1, got[-3], got[3], up, down, other3, other4 = tie(
        send1, got[-3], got[3], up, down, other3, other4
    )
    got[-4] = step_ring(got[-3], 1)
    up = add(keep1[2 * tokens : 3 * tokens], other2[:tokens], up)
    down = add(keep1[3 * tokens :], other2[tokens:], down)
    up, down = tie(up, down)
    down = step_ring(down, -1)
    recv1 = across(send1)
    pair[2], pair[-3], pair[3] = core(got[2]), core(got[-3]), core(got[3])
    other3, other4 = core(other3), core(other4)
    gate_b, other3, other4 = tie(gate_b, other3, other4)
    send2, hold2 = bwd(groups[1], share=64)

    hold2, send2, up, down, got[-4] = tie(hold2, send2, up, down, got[-4])
    up, down = step_ring(up, 1), step_ring(mine(1, other3, down), -1)
    pair[-4] = core(got[-4])
    recv2 = across(send2)
    send3, hold3 = bwd(groups[2], share=64)

    send3, hold3, up, down, recv1 = tie(send3, hold3, up, down, recv1)
    up, down = step_ring(mine(0, other3, up), 1), step_ring(mine(2, other4, down), -1)
    recv3 = across(send3)
    hold3, recv2 = tie(hold3, recv2)
    grad = collect(groups[:2], where, (hold1, recv1, hold2, recv2), 8 * rows)
    grad, recv3 = tie(grad, recv3)
    mixed_a = mine(3, other4, up, down)
    grad = collect(groups[2:], where, (hold3, recv3), 8 * rows, grad)
    return (mixed_a, grad[None])


def solution(mesh):
    in_specs = (
        P("expert", None, None),
        P("expert", None, "pipe"),
        P("expert", None),
        P("expert", None),
        P("expert", "pipe"),
        P("expert", None),
        P("expert", None),
    )
    out_specs = (P("expert", "pipe"), P("expert", None, "pipe"))
    tailored = mesh.shape["expert"] == 16 and mesh.shape["pipe"] == 2
    return jax.shard_map(
        on_device_16 if tailored else on_device_any,
        mesh=mesh,
        in_specs=in_specs,
        out_specs=out_specs,
        check_vma=False,
    )
```

```python
import functools

import jax
import jax.numpy as jnp
from jax import lax
from jax.experimental import pallas as pl
from jax.experimental.pallas import tpu as pltpu
from jax.sharding import PartitionSpec as P

BF16, F32 = jnp.bfloat16, jnp.float32
TILE = 512
LANES = 128
RAW_TILE = 256


def dense_gates(routes, gates, total):
    experts = jnp.arange(total, dtype=jnp.int32)[:, None, None]
    return jnp.sum(jnp.where(routes[None] == experts, gates[None], 0.0), axis=2)


def ranks_of(gate):
    tokens = gate.shape[-1]
    earlier = jnp.triu(jnp.ones((tokens, tokens), BF16), 1)
    counts = jnp.dot((gate > 0.0).astype(BF16), earlier, preferred_element_type=F32)
    return counts.astype(jnp.int32)


def add(*terms):
    total = terms[0].astype(F32)
    for term in terms[1:]:
        total = total + term.astype(F32)
    return total.astype(BF16)


def on_device_any(hidden_a, expert_weights, routes_a, gates_a, cotangent_b, routes_b, gates_b):
    groups = lax.axis_size("expert")
    me = lax.axis_index("expert")
    total = expert_weights.shape[0] * groups
    rows = hidden_a.shape[1]
    cap = rows // groups
    tokens, width = cotangent_b.shape
    weights = expert_weights[0]

    both = jnp.stack(
        [dense_gates(routes_a, gates_a, total), dense_gates(routes_b, gates_b, total)], axis=1
    )
    every = lax.all_gather(both, "expert", axis=0, tiled=False)
    own = lax.dynamic_index_in_dim(every, me, axis=1, keepdims=False)
    gathered = lax.all_gather(cotangent_b, "expert", axis=0, tiled=True)

    def placement(gate):
        slots = jnp.arange(cap, dtype=jnp.int32)[None, :, None]
        hit = (gate > 0.0)[:, None, :] & (ranks_of(gate)[:, None, :] == slots)
        return hit.astype(BF16), jnp.sum(jnp.where(hit, gate[:, None, :], 0.0), axis=2)

    hit_a, slot_gate_a = placement(own[:, 0])
    hit_b, slot_gate_b = placement(own[:, 1])

    outputs = jnp.einsum("rf,fd->rd", hidden_a[0], weights, preferred_element_type=F32)
    scaled = (outputs * slot_gate_a.reshape(rows, 1)).astype(BF16)
    spread = jnp.einsum(
        "sct,scd->std", hit_a, scaled.reshape(groups, cap, width), preferred_element_type=F32
    ).astype(BF16)
    mixed_a = lax.psum_scatter(
        spread.reshape(groups * tokens, width), "expert", scatter_dimension=0, tiled=True
    )
    picked = jnp.einsum(
        "sct,std->scd",
        hit_b,
        gathered.reshape(groups, tokens, width),
        preferred_element_type=F32,
    ).astype(BF16)
    partial_value = jnp.einsum(
        "rd,fd->rf", picked.reshape(rows, width), weights, preferred_element_type=F32
    )
    partial_value = (partial_value * slot_gate_b.reshape(rows, 1)).astype(BF16)
    grad = lax.psum_scatter(partial_value, "pipe", scatter_dimension=1, tiled=True)
    return (mixed_a, grad[None])


RING = [(0, 0), (1, 0), (2, 0), (3, 0), (3, 1), (2, 1), (1, 1), (0, 1)]


def step_ring(value, way):
    pairs = []
    for place, (z, y) in enumerate(RING):
        to_z, to_y = RING[(place + way) % 8]
        pairs += [(z * 4 + y * 2 + c, to_z * 4 + to_y * 2 + c) for c in range(2)]
    return lax.ppermute(value, "expert", pairs)


def xor(value, bits):
    return lax.ppermute(value, "expert", [(i, i ^ bits) for i in range(16)])


def core(value):
    return xor(value, 1)


def across(value):
    return lax.ppermute(value, "pipe", [(0, 1), (1, 0)])


def pin(value):
    return pltpu.with_memory_space_constraint(value, pltpu.HBM)


def tie(*values):
    return lax.optimization_barrier(values)


SMEM = pl.BlockSpec(memory_space=pltpu.SMEM)
VMEM = pl.BlockSpec(memory_space=pltpu.VMEM)
HBM = pl.BlockSpec(memory_space=pltpu.HBM)
ANY = pl.BlockSpec(memory_space=pl.ANY)


def kernel_call(kernel, name, inputs, out_shape, scratch, flops, moved, limit=12):
    in_specs, arrays = zip(*inputs)
    return pl.pallas_call(
        kernel,
        in_specs=in_specs,
        out_specs=[VMEM] * len(out_shape),
        out_shape=out_shape,
        scratch_shapes=scratch,
        compiler_params=pltpu.CompilerParams(vmem_limit_bytes=limit * 2**20),
        cost_estimate=pl.CostEstimate(flops=flops, bytes_accessed=moved, transcendentals=0),
        name=name,
    )(*arrays)


def gates_kernel(*refs):
    sources, out, held, sems = refs[:4], refs[4], refs[5:9], refs[9]
    copies = [pltpu.make_async_copy(x, y, sems.at[i]) for i, (x, y) in enumerate(zip(sources, held))]
    for copy in copies:
        copy.start()
    for copy in copies:
        copy.wait()
    top, tokens = held[0].shape
    experts = lax.broadcasted_iota(jnp.int32, (out.shape[0], tokens), 0)
    for i in range(2):
        routes, gates = held[2 * i : 2 * i + 2]
        total = jnp.zeros(experts.shape, F32)
        for k in range(top):
            total += jnp.where(routes[k : k + 1, :] == experts, gates[k : k + 1, :], 0.0)
        out[:, pl.ds(i * tokens, tokens)] = total


def gates_of(*arrays):
    tokens, top = arrays[0].shape
    arrays = [pin(x.T) for x in arrays]
    return kernel_call(
        gates_kernel,
        "gates",
        [(HBM, x) for x in arrays],
        [jax.ShapeDtypeStruct((16, 2 * tokens), F32)],
        [pltpu.VMEM((top, tokens), x.dtype) for x in arrays] + [pltpu.SemaphoreType.DMA((4,))],
        flops=2**20,
        moved=2**17,
    )[0]


def place_slots(distances, where, gates, cap, target, place, slot_gates):
    gate = gates[...]
    tokens = gate.shape[1] // 2
    row = lax.broadcasted_iota(jnp.int32, (2 * tokens, 2 * tokens), 0)
    col = lax.broadcasted_iota(jnp.int32, (2 * tokens, 2 * tokens), 1)
    earlier = ((row < col) & (row // tokens == col // tokens)).astype(F32).astype(BF16)
    chosen = (gate > 0.0).astype(F32).astype(BF16)
    rank = jnp.dot(chosen, earlier, preferred_element_type=F32)
    second = (lax.broadcasted_iota(jnp.int32, gate.shape, 1) // tokens) ^ where[8]
    target[...] = jnp.where(gate > 0.0, rank + (second * cap).astype(F32), -1.0)
    slots = lax.broadcasted_iota(jnp.int32, (2 * cap, 2 * tokens), 0).astype(F32)
    for i, d in enumerate(distances):
        block = pl.ds(where[9 + d % 8], 1)
        hit = target[block, :] == slots
        place[i] = hit.astype(F32).astype(BF16)
        total = jnp.sum(jnp.where(hit, gates[block, :], 0.0), axis=1, keepdims=True)
        slot_gates[pl.ds(i * 2 * cap, 2 * cap), :] = jnp.broadcast_to(total, (2 * cap, LANES))


def place_scratch(count, gates, cap):
    return [
        pltpu.VMEM(gates.shape, F32),
        pltpu.VMEM((count, 2 * cap, gates.shape[1]), BF16),
        pltpu.VMEM((count * 2 * cap, LANES), F32),
    ]


def gated(value, slot_gates):
    factor = jnp.concatenate([slot_gates] * (value.shape[1] // LANES), axis=1)
    return (value * factor).astype(BF16)


class Stream:
    def __init__(self, tile, buffer, sems):
        self.tile, self.buffer, self.sems = tile, buffer, sems
        self.slots, self.parts = sems.shape

    def copies(self, n):
        slot = n % self.slots
        rows = self.buffer.shape[1] // self.parts
        source = self.tile(n)
        for part in range(self.parts):
            at = pl.ds(part * rows, rows)
            yield pltpu.make_async_copy(
                source.at[at, :], self.buffer.at[slot, at, :], self.sems.at[slot, part]
            )

    def start(self, n):
        for copy in self.copies(n):
            copy.start()

    def wait(self, n):
        for copy in self.copies(n):
            copy.wait()


def raw_kernel(first, hidden, weights, out, held, held_sems, buffer, sems, staged, out_sems):
    tiles = out.shape[1] // RAW_TILE
    stream = Stream(
        lambda n: weights.at[:, pl.ds(pl.multiple_of(first + n * RAW_TILE, RAW_TILE), RAW_TILE)], buffer, sems
    )
    rows = held.shape[0] // held_sems.shape[0]
    fetch = []
    for i in range(held_sems.shape[0]):
        at = pl.ds(i * rows, rows)
        fetch.append(pltpu.make_async_copy(hidden.at[at, :], held.at[at, :], held_sems.at[i]))
        fetch[-1].start()
    stream.start(0)

    def put(n):
        cols = pl.ds(pl.multiple_of(n * RAW_TILE, RAW_TILE), RAW_TILE)
        return pltpu.make_async_copy(staged.at[n % 2], out.at[:, cols], out_sems.at[n % 2])

    for copy in fetch:
        copy.wait()
    for n in range(1, stream.slots):
        stream.start(n)

    @pl.loop(0, tiles)
    def _(n):
        stream.wait(n)

        @pl.when(n >= 2)
        def _():
            put(n - 2).wait()

        value = jnp.dot(held[...], buffer[n % stream.slots], preferred_element_type=F32)
        staged[n % 2] = value.astype(BF16)
        put(n).start()

        @pl.when(n + stream.slots < tiles)
        def _():
            stream.start(n + stream.slots)

    put(tiles - 2).wait()
    put(tiles - 1).wait()


def raw_forward(first, width, hidden, weights):
    rows, depth = hidden.shape
    return pl.pallas_call(
        functools.partial(raw_kernel, first),
        in_specs=[HBM, HBM],
        out_specs=HBM,
        out_shape=pltpu.HBM((rows, width), BF16),
        scratch_shapes=[
            pltpu.VMEM(hidden.shape, BF16),
            pltpu.SemaphoreType.DMA((4,)),
            pltpu.VMEM((3, depth, RAW_TILE), BF16),
            pltpu.SemaphoreType.DMA((3, 4)),
            pltpu.VMEM((2, rows, RAW_TILE), BF16),
            pltpu.SemaphoreType.DMA((2,)),
        ],
        compiler_params=pltpu.CompilerParams(vmem_limit_bytes=12 * 2**20),
        cost_estimate=pl.CostEstimate(
            flops=2 * rows * depth * width,
            bytes_accessed=2 * (depth * width + rows * (depth + width)),
            transcendentals=0,
        ),
        name="raw_forward",
    )(hidden, weights)


def spread_kernel(distances, split, cap, where, gates, *refs):
    count = len(distances)
    raws, (keep, *others), scratch = refs[:2], refs[2:-6], refs[-6:]
    target, place, slot_gates, to_tokens, held, sems = scratch
    rows, half = 2 * cap, gates.shape[1] // 2
    width = raws[0].shape[1]

    def fetch(i, start):
        return [
            pltpu.make_async_copy(
                raw.at[pl.ds(start, rows), :],
                held.at[i, :, pl.ds(j * width, width)],
                sems.at[i, j],
            )
            for j, raw in enumerate(raws)
        ]

    for i, d in enumerate(distances):
        for copy in fetch(i, pl.multiple_of(where[d % 8] * rows, rows)):
            copy.start()
    place_slots(distances, where, gates, cap, target, place, slot_gates)
    tokens = 2 * half
    same = lax.broadcasted_iota(jnp.int32, (tokens, tokens), 0) == lax.broadcasted_iota(
        jnp.int32, (tokens, tokens), 1
    )
    same = same.astype(F32).astype(BF16)
    for i in range(count):
        to_tokens[i] = lax.dot_general(
            same, place[i], (((1,), (1,)), ((), ())), preferred_element_type=F32
        ).astype(BF16)
    for g, other in enumerate(others):

        @pl.loop(0, split)
        def _(j):
            i = g * split + j
            for copy in fetch(i, 0):
                copy.wait()
            for n in range(2 * width // TILE):
                cols = pl.ds(n * TILE, TILE)
                part = held[i, :, cols].astype(F32)
                part = gated(part, slot_gates[pl.ds(pl.multiple_of(i * rows, rows), rows), :])
                part = jnp.dot(to_tokens[i], part, preferred_element_type=F32).astype(BF16)
                keep[pl.ds(pl.multiple_of(i * half, half), half), cols] = part[:half]
                other[pl.ds(pl.multiple_of(j * half, half), half), cols] = part[half:]


def spread_tokens(distances, split, cap, where, gates, raws):
    count, half, width = len(distances), gates.shape[1] // 2, 2 * raws[0].shape[1]
    return kernel_call(
        functools.partial(spread_kernel, distances, split, cap),
        "spread_tokens",
        [(SMEM, where), (VMEM, gates), (HBM, raws[0]), (HBM, raws[1])],
        [jax.ShapeDtypeStruct((count * half, width), BF16)]
        + [jax.ShapeDtypeStruct((split * half, width), BF16)] * (count // split),
        [
            *place_scratch(count, gates, cap),
            pltpu.VMEM((count, 2 * half, 2 * cap), BF16),
            pltpu.VMEM((count, 2 * cap, width), BF16),
            pltpu.SemaphoreType.DMA((count, 2)),
        ],
        flops=2**20,
        moved=2**14,
    )


def backward_kernel(distances, cap, sides, where, pipe, gates, weights, *refs):
    count, rows = len(distances), 2 * cap
    tokens, outs = refs[: 2 * count], refs[2 * count : 2 * count + len(sides)]
    block, block_sems, picked, target, place, slot_gates, buffer, sems = refs[
        2 * count + len(sides) :
    ]
    half, tile = tokens[0].shape[0], buffer.shape[1]
    tiles = 4 * len(sides)
    first = (1 - pipe[0] + sides[0]) * 4

    def weight_tile(n):
        return weights.at[pl.ds(pl.multiple_of((first + n) % 8 * tile, tile), tile), :]

    fetch = []
    for i, token in enumerate(tokens):
        to = block.at[i // 2, pl.ds(i % 2 * half, half), :]
        fetch.append(pltpu.make_async_copy(token, to, block_sems.at[i]))
        fetch[-1].start()
    stream = Stream(weight_tile, buffer, sems)
    for n in range(stream.slots):
        stream.start(n)
    place_slots(distances, where, gates, cap, target, place, slot_gates)
    for copy in fetch:
        copy.wait()

    @pl.loop(0, count)
    def _(i):
        for n in range(block.shape[2] // TILE):
            cols = pl.ds(n * TILE, TILE)
            picked[pl.ds(pl.multiple_of(i * rows, rows), rows), cols] = jnp.dot(
                place[i], block[i, :, cols], preferred_element_type=F32
            ).astype(BF16)

    @pl.loop(0, tiles)
    def _(n):
        stream.wait(n)
        value = lax.dot_general(
            picked[...],
            buffer[n % stream.slots],
            (((1,), (1,)), ((), ())),
            preferred_element_type=F32,
        )
        value = gated(value, slot_gates[...])
        cols = pl.ds(pl.multiple_of(n % 4 * tile, tile), tile)
        for i, out in enumerate(outs):

            @pl.when(n // 4 == i)
            def _():
                out[:, cols] = value

        @pl.when(n + stream.slots < tiles)
        def _():
            stream.start(n + stream.slots)


def backward(distances, cap, sides, where, pipe, tokens, gates, weights, share):
    count, rows = len(distances), 2 * cap
    depth, width = weights.shape
    return kernel_call(
        functools.partial(backward_kernel, distances, cap, sides),
        "backward",
        [(SMEM, where), (SMEM, pipe), (VMEM, gates), (HBM, weights)] + [(ANY, x) for x in tokens],
        [jax.ShapeDtypeStruct((count * rows, depth // 2), BF16)] * len(sides),
        [
            pltpu.VMEM((count, gates.shape[1], width), BF16),
            pltpu.SemaphoreType.DMA((2 * count,)),
            pltpu.VMEM((count * rows, width), BF16),
            *place_scratch(count, gates, cap),
            pltpu.VMEM((4, depth // 8, width), BF16),
            pltpu.SemaphoreType.DMA((4, 4)),
        ],
        flops=len(sides) * count * rows * depth * width // share,
        moved=2 * (depth * width + count * rows * (depth + 2 * width)) // share,
        limit=18,
    )


def collect_kernel(groups, where, *refs):
    out, held, sems = refs[-3:]
    copies = []
    for g, distances in enumerate(groups):
        hold, recv = refs[2 * g], refs[2 * g + 1]
        rows = hold.shape[0] // len(distances)
        for i, d in enumerate(distances):
            at, n = pl.ds(i * rows, rows), len(copies)
            held[n] = (hold[at, :].astype(F32) + recv[at, :].astype(F32)).astype(BF16)
            to = pl.ds(pl.multiple_of(where[d % 8] * rows, rows), rows)
            copies.append(pltpu.make_async_copy(held.at[n], out.at[to, :], sems.at[n]))
            copies[-1].start()
    for copy in copies:
        copy.wait()


def collect(groups, where, arrays, rows, into=None):
    count = sum(len(distances) for distances in groups)
    out = jax.ShapeDtypeStruct((rows, arrays[0].shape[1]), BF16)
    inputs = [(SMEM, where)] + [(VMEM, x) for x in arrays]
    if into is not None:
        inputs.append((HBM, into))
    in_specs, arrays = zip(*inputs)
    return pl.pallas_call(
        functools.partial(collect_kernel, groups),
        in_specs=in_specs,
        out_specs=HBM,
        out_shape=out,
        scratch_shapes=[
            pltpu.VMEM((count, rows // 8, out.shape[1]), BF16),
            pltpu.SemaphoreType.DMA((count,)),
        ],
        input_output_aliases={} if into is None else {len(inputs) - 1: 0},
        compiler_params=pltpu.CompilerParams(vmem_limit_bytes=12 * 2**20),
        cost_estimate=pl.CostEstimate(
            flops=2**20, bytes_accessed=6 * count * rows * 128, transcendentals=0
        ),
        name="collect",
    )(*arrays)


def on_device_16(hidden_a, expert_weights, routes_a, gates_a, cotangent_b, routes_b, gates_b):
    me = lax.axis_index("expert").astype(jnp.int32)
    z, y, c = me // 4, me // 2 % 2, me % 2
    pipe = lax.axis_index("pipe").astype(jnp.int32).reshape(1)
    rows = hidden_a.shape[1] // 8
    cap = rows // 2
    tokens, width = cotangent_b.shape
    weights, hidden = expert_weights[0], hidden_a[0]

    ring = (jnp.where(y == 0, z, 7 - z) + jnp.arange(8, dtype=jnp.int32)) % 8
    to_z, to_y = jnp.minimum(ring, 7 - ring), (ring > 3).astype(jnp.int32)
    chips = to_z * 2 + to_y
    where = jnp.concatenate([chips, c.reshape(1), (to_z ^ z) * 2 + (to_y ^ y)])

    got, pair = {0: cotangent_b}, {}
    got[-1], got[1] = step_ring(cotangent_b, 1), step_ring(cotangent_b, -1)

    both = gates_of(routes_a, gates_a, routes_b, gates_b)
    four = jnp.stack([both] + [xor(both, j) for j in (1, 2, 3)])
    four = lax.dynamic_index_in_dim(four.reshape(4, 4, 4, 2 * tokens), me % 4, 2, False)
    weights, four = tie(weights, four)
    raw1 = raw_forward(0, width // 2, pin(hidden), pin(weights))
    every = jnp.stack([four] + [xor(four, 4 * k) for k in (1, 2, 3)])
    raw1, weights, every, got[-1], got[1] = tie(raw1, weights, every, got[-1], got[1])
    weights = pin(weights)
    every = lax.dynamic_index_in_dim(every, z, 2, False)
    gate = jnp.moveaxis(every.reshape(8, 2, 2, tokens), 2, 0).reshape(2, 8, 2 * tokens)
    gate_a, gate_b = gate[0], gate[1]

    def spread(distances, split, gates):
        return spread_tokens(distances, split, cap, where, gates, (pin(raw1), pin(raw2)))

    def bwd(distances, sides=(0, 1), share=1):
        values = [x for d in distances for x in (got[d], pair[d])]
        return backward(distances, cap, sides, where, pipe, values, gate_b, weights, share)

    got[-2], got[2] = step_ring(got[-1], 1), step_ring(got[1], -1)
    for d in (0, -1, 1):
        pair[d] = core(got[d])
    raw2 = raw_forward(width // 2, width // 2, pin(hidden), weights)
    raw2, pair[0], pair[-1], pair[1] = tie(raw2, pair[0], pair[-1], pair[1])

    keep1, other1, other2 = spread((3, -4, 2, -3), 2, gate_a)
    keep1, other1, other2, got[-2], got[2] = tie(keep1, other1, other2, got[-2], got[2])
    got[-3], got[3] = step_ring(got[-2], 1), step_ring(got[2], -1)
    other1, other2 = core(other1), core(other2)
    up = step_ring(add(keep1[:tokens], other1[:tokens]), 1)
    down = step_ring(add(keep1[tokens : 2 * tokens], other1[tokens:]), -1)
    pair[-2] = core(got[-2])
    gate_a, pair[-2], other2 = tie(gate_a, pair[-2], other2)
    keep2, other3, other4 = spread((1, -2, -1, 0), 2, gate_a)
    keep2, gate_b = tie(keep2, gate_b)
    groups = (0, -1, 1, -2), (2, -3), (3, -4)
    for d in (0, -1, 1):
        pair[d] = pin(pair[d])
    send1, hold1 = bwd(groups[0], share=64)

    def mine(i, other, *more):
        at = slice(i * tokens, (i + 1) * tokens)
        other_at = slice(i % 2 * tokens, (i % 2 + 1) * tokens)
        return add(keep2[at], other[other_at], *more)

    send1, got[-3], got[3], up, down, other3, other4 = tie(
        send1, got[-3], got[3], up, down, other3, other4
    )
    got[-4] = step_ring(got[-3], 1)
    up = add(keep1[2 * tokens : 3 * tokens], other2[:tokens], up)
    down = add(keep1[3 * tokens :], other2[tokens:], down)
    up, down = tie(up, down)
    down = step_ring(down, -1)
    recv1 = across(send1)
    pair[2], pair[-3] = core(got[2]), core(got[-3])
    other3, other4 = core(other3), core(other4)
    gate_b, other3, other4 = tie(gate_b, other3, other4)
    send2, hold2 = bwd(groups[1], share=64)

    hold2, send2, up, down, got[3], got[-4] = tie(hold2, send2, up, down, got[3], got[-4])
    up, down = step_ring(up, 1), step_ring(mine(1, other3, down), -1)
    pair[3], pair[-4] = core(got[3]), core(got[-4])
    recv2 = across(send2)
    send3, hold3 = bwd(groups[2], share=64)

    send3, hold3, up, down, recv1, recv2 = tie(send3, hold3, up, down, recv1, recv2)
    up, down = step_ring(mine(0, other3, up), 1), step_ring(mine(2, other4, down), -1)
    recv3 = across(send3)
    grad = collect(groups[:2], where, (hold1, recv1, hold2, recv2), 8 * rows)
    grad, recv3 = tie(grad, recv3)
    mixed_a = mine(3, other4, up, down)
    grad = collect(groups[2:], where, (hold3, recv3), 8 * rows, grad)
    return (mixed_a, grad[None])


def solution(mesh):
    in_specs = (
        P("expert", None, None),
        P("expert", None, "pipe"),
        P("expert", None),
        P("expert", None),
        P("expert", "pipe"),
        P("expert", None),
        P("expert", None),
    )
    out_specs = (P("expert", "pipe"), P("expert", None, "pipe"))
    tailored = mesh.shape["expert"] == 16 and mesh.shape["pipe"] == 2
    return jax.shard_map(
        on_device_16 if tailored else on_device_any,
        mesh=mesh,
        in_specs=in_specs,
        out_specs=out_specs,
        check_vma=False,
    )
```

```python
import functools

import jax
import jax.numpy as jnp
from jax import lax
from jax.experimental import pallas as pl
from jax.experimental.pallas import tpu as pltpu
from jax.sharding import PartitionSpec as P

BF16, F32 = jnp.bfloat16, jnp.float32
TILE = 512
LANES = 128
RAW_TILE = 256


def dense_gates(routes, gates, total):
    experts = jnp.arange(total, dtype=jnp.int32)[:, None, None]
    return jnp.sum(jnp.where(routes[None] == experts, gates[None], 0.0), axis=2)


def ranks_of(gate):
    tokens = gate.shape[-1]
    earlier = jnp.triu(jnp.ones((tokens, tokens), BF16), 1)
    counts = jnp.dot((gate > 0.0).astype(BF16), earlier, preferred_element_type=F32)
    return counts.astype(jnp.int32)


def add(*terms):
    total = terms[0].astype(F32)
    for term in terms[1:]:
        total = total + term.astype(F32)
    return total.astype(BF16)


def on_device_any(hidden_a, expert_weights, routes_a, gates_a, cotangent_b, routes_b, gates_b):
    groups = lax.axis_size("expert")
    me = lax.axis_index("expert")
    total = expert_weights.shape[0] * groups
    rows = hidden_a.shape[1]
    cap = rows // groups
    tokens, width = cotangent_b.shape
    weights = expert_weights[0]

    both = jnp.stack(
        [dense_gates(routes_a, gates_a, total), dense_gates(routes_b, gates_b, total)], axis=1
    )
    every = lax.all_gather(both, "expert", axis=0, tiled=False)
    own = lax.dynamic_index_in_dim(every, me, axis=1, keepdims=False)
    gathered = lax.all_gather(cotangent_b, "expert", axis=0, tiled=True)

    def placement(gate):
        slots = jnp.arange(cap, dtype=jnp.int32)[None, :, None]
        hit = (gate > 0.0)[:, None, :] & (ranks_of(gate)[:, None, :] == slots)
        return hit.astype(BF16), jnp.sum(jnp.where(hit, gate[:, None, :], 0.0), axis=2)

    hit_a, slot_gate_a = placement(own[:, 0])
    hit_b, slot_gate_b = placement(own[:, 1])

    outputs = jnp.einsum("rf,fd->rd", hidden_a[0], weights, preferred_element_type=F32)
    scaled = (outputs * slot_gate_a.reshape(rows, 1)).astype(BF16)
    spread = jnp.einsum(
        "sct,scd->std", hit_a, scaled.reshape(groups, cap, width), preferred_element_type=F32
    ).astype(BF16)
    mixed_a = lax.psum_scatter(
        spread.reshape(groups * tokens, width), "expert", scatter_dimension=0, tiled=True
    )
    picked = jnp.einsum(
        "sct,std->scd",
        hit_b,
        gathered.reshape(groups, tokens, width),
        preferred_element_type=F32,
    ).astype(BF16)
    partial_value = jnp.einsum(
        "rd,fd->rf", picked.reshape(rows, width), weights, preferred_element_type=F32
    )
    partial_value = (partial_value * slot_gate_b.reshape(rows, 1)).astype(BF16)
    grad = lax.psum_scatter(partial_value, "pipe", scatter_dimension=1, tiled=True)
    return (mixed_a, grad[None])


RING = [(0, 0), (1, 0), (2, 0), (3, 0), (3, 1), (2, 1), (1, 1), (0, 1)]


def step_ring(value, way):
    pairs = []
    for place, (z, y) in enumerate(RING):
        to_z, to_y = RING[(place + way) % 8]
        pairs += [(z * 4 + y * 2 + c, to_z * 4 + to_y * 2 + c) for c in range(2)]
    return lax.ppermute(value, "expert", pairs)


def xor(value, bits):
    return lax.ppermute(value, "expert", [(i, i ^ bits) for i in range(16)])


def core(value):
    return xor(value, 1)


def across(value):
    return lax.ppermute(value, "pipe", [(0, 1), (1, 0)])


def pin(value):
    return pltpu.with_memory_space_constraint(value, pltpu.HBM)


def tie(*values):
    return lax.optimization_barrier(values)


SMEM = pl.BlockSpec(memory_space=pltpu.SMEM)
VMEM = pl.BlockSpec(memory_space=pltpu.VMEM)
HBM = pl.BlockSpec(memory_space=pltpu.HBM)
ANY = pl.BlockSpec(memory_space=pl.ANY)


def kernel_call(kernel, name, inputs, out_shape, scratch, flops, moved, limit=12):
    in_specs, arrays = zip(*inputs)
    return pl.pallas_call(
        kernel,
        in_specs=in_specs,
        out_specs=[VMEM] * len(out_shape),
        out_shape=out_shape,
        scratch_shapes=scratch,
        compiler_params=pltpu.CompilerParams(vmem_limit_bytes=limit * 2**20),
        cost_estimate=pl.CostEstimate(flops=flops, bytes_accessed=moved, transcendentals=0),
        name=name,
    )(*arrays)


def gates_kernel(*refs):
    sources, out, held, sems = refs[:4], refs[4], refs[5:9], refs[9]
    copies = [pltpu.make_async_copy(x, y, sems.at[i]) for i, (x, y) in enumerate(zip(sources, held))]
    for copy in copies:
        copy.start()
    for copy in copies:
        copy.wait()
    top, tokens = held[0].shape
    experts = lax.broadcasted_iota(jnp.int32, (out.shape[0], tokens), 0)
    for i in range(2):
        routes, gates = held[2 * i : 2 * i + 2]
        total = jnp.zeros(experts.shape, F32)
        for k in range(top):
            total += jnp.where(routes[k : k + 1, :] == experts, gates[k : k + 1, :], 0.0)
        out[:, pl.ds(i * tokens, tokens)] = total


def gates_of(*arrays):
    tokens, top = arrays[0].shape
    arrays = [pin(x.T) for x in arrays]
    return kernel_call(
        gates_kernel,
        "gates",
        [(HBM, x) for x in arrays],
        [jax.ShapeDtypeStruct((16, 2 * tokens), F32)],
        [pltpu.VMEM((top, tokens), x.dtype) for x in arrays] + [pltpu.SemaphoreType.DMA((4,))],
        flops=2**20,
        moved=2**17,
    )[0]


def place_slots(distances, where, gates, cap, target, place, slot_gates):
    gate = gates[...]
    tokens = gate.shape[1] // 2
    row = lax.broadcasted_iota(jnp.int32, (2 * tokens, 2 * tokens), 0)
    col = lax.broadcasted_iota(jnp.int32, (2 * tokens, 2 * tokens), 1)
    earlier = ((row < col) & (row // tokens == col // tokens)).astype(F32).astype(BF16)
    chosen = (gate > 0.0).astype(F32).astype(BF16)
    rank = jnp.dot(chosen, earlier, preferred_element_type=F32)
    second = (lax.broadcasted_iota(jnp.int32, gate.shape, 1) // tokens) ^ where[8]
    target[...] = jnp.where(gate > 0.0, rank + (second * cap).astype(F32), -1.0)
    slots = lax.broadcasted_iota(jnp.int32, (2 * cap, 2 * tokens), 0).astype(F32)
    for i, d in enumerate(distances):
        block = pl.ds(where[9 + d % 8], 1)
        hit = target[block, :] == slots
        place[i] = hit.astype(F32).astype(BF16)
        total = jnp.sum(jnp.where(hit, gates[block, :], 0.0), axis=1, keepdims=True)
        slot_gates[pl.ds(i * 2 * cap, 2 * cap), :] = jnp.broadcast_to(total, (2 * cap, LANES))


def place_scratch(count, gates, cap):
    return [
        pltpu.VMEM(gates.shape, F32),
        pltpu.VMEM((count, 2 * cap, gates.shape[1]), BF16),
        pltpu.VMEM((count * 2 * cap, LANES), F32),
    ]


def gated(value, slot_gates):
    factor = jnp.concatenate([slot_gates] * (value.shape[1] // LANES), axis=1)
    return (value * factor).astype(BF16)


class Stream:
    def __init__(self, tile, buffer, sems):
        self.tile, self.buffer, self.sems = tile, buffer, sems
        self.slots, self.parts = sems.shape

    def copies(self, n):
        slot = n % self.slots
        rows = self.buffer.shape[1] // self.parts
        source = self.tile(n)
        for part in range(self.parts):
            at = pl.ds(part * rows, rows)
            yield pltpu.make_async_copy(
                source.at[at, :], self.buffer.at[slot, at, :], self.sems.at[slot, part]
            )

    def start(self, n):
        for copy in self.copies(n):
            copy.start()

    def wait(self, n):
        for copy in self.copies(n):
            copy.wait()


def raw_kernel(first, hidden, weights, out, held, held_sems, buffer, sems, staged, out_sems):
    tiles = out.shape[1] // RAW_TILE
    stream = Stream(
        lambda n: weights.at[:, pl.ds(pl.multiple_of(first + n * RAW_TILE, RAW_TILE), RAW_TILE)], buffer, sems
    )
    rows = held.shape[0] // held_sems.shape[0]
    fetch = []
    for i in range(held_sems.shape[0]):
        at = pl.ds(i * rows, rows)
        fetch.append(pltpu.make_async_copy(hidden.at[at, :], held.at[at, :], held_sems.at[i]))
        fetch[-1].start()
    stream.start(0)

    def put(n):
        cols = pl.ds(pl.multiple_of(n * RAW_TILE, RAW_TILE), RAW_TILE)
        return pltpu.make_async_copy(staged.at[n % 2], out.at[:, cols], out_sems.at[n % 2])

    for copy in fetch:
        copy.wait()
    for n in range(1, stream.slots):
        stream.start(n)

    @pl.loop(0, tiles)
    def _(n):
        stream.wait(n)

        @pl.when(n >= 2)
        def _():
            put(n - 2).wait()

        value = jnp.dot(held[...], buffer[n % stream.slots], preferred_element_type=F32)
        staged[n % 2] = value.astype(BF16)
        put(n).start()

        @pl.when(n + stream.slots < tiles)
        def _():
            stream.start(n + stream.slots)

    put(tiles - 2).wait()
    put(tiles - 1).wait()


def raw_forward(first, width, hidden, weights):
    rows, depth = hidden.shape
    return pl.pallas_call(
        functools.partial(raw_kernel, first),
        in_specs=[HBM, HBM],
        out_specs=HBM,
        out_shape=pltpu.HBM((rows, width), BF16),
        scratch_shapes=[
            pltpu.VMEM(hidden.shape, BF16),
            pltpu.SemaphoreType.DMA((4,)),
            pltpu.VMEM((3, depth, RAW_TILE), BF16),
            pltpu.SemaphoreType.DMA((3, 4)),
            pltpu.VMEM((2, rows, RAW_TILE), BF16),
            pltpu.SemaphoreType.DMA((2,)),
        ],
        compiler_params=pltpu.CompilerParams(vmem_limit_bytes=12 * 2**20),
        cost_estimate=pl.CostEstimate(
            flops=2 * rows * depth * width,
            bytes_accessed=2 * (depth * width + rows * (depth + width)),
            transcendentals=0,
        ),
        name="raw_forward",
    )(hidden, weights)


def spread_kernel(distances, split, cap, where, gates, *refs):
    count = len(distances)
    raws, (keep, *others), scratch = refs[:2], refs[2:-6], refs[-6:]
    target, place, slot_gates, to_tokens, held, sems = scratch
    rows, half = 2 * cap, gates.shape[1] // 2
    width = raws[0].shape[1]

    def fetch(i, start):
        return [
            pltpu.make_async_copy(
                raw.at[pl.ds(start, rows), :],
                held.at[i, :, pl.ds(j * width, width)],
                sems.at[i, j],
            )
            for j, raw in enumerate(raws)
        ]

    for i, d in enumerate(distances):
        for copy in fetch(i, pl.multiple_of(where[d % 8] * rows, rows)):
            copy.start()
    place_slots(distances, where, gates, cap, target, place, slot_gates)
    tokens = 2 * half
    same = lax.broadcasted_iota(jnp.int32, (tokens, tokens), 0) == lax.broadcasted_iota(
        jnp.int32, (tokens, tokens), 1
    )
    same = same.astype(F32).astype(BF16)
    for i in range(count):
        to_tokens[i] = lax.dot_general(
            same, place[i], (((1,), (1,)), ((), ())), preferred_element_type=F32
        ).astype(BF16)
    for g, other in enumerate(others):

        @pl.loop(0, split)
        def _(j):
            i = g * split + j
            for copy in fetch(i, 0):
                copy.wait()
            for n in range(2 * width // TILE):
                cols = pl.ds(n * TILE, TILE)
                part = held[i, :, cols].astype(F32)
                part = gated(part, slot_gates[pl.ds(pl.multiple_of(i * rows, rows), rows), :])
                part = jnp.dot(to_tokens[i], part, preferred_element_type=F32).astype(BF16)
                keep[pl.ds(pl.multiple_of(i * half, half), half), cols] = part[:half]
                other[pl.ds(pl.multiple_of(j * half, half), half), cols] = part[half:]


def spread_tokens(distances, split, cap, where, gates, raws):
    count, half, width = len(distances), gates.shape[1] // 2, 2 * raws[0].shape[1]
    return kernel_call(
        functools.partial(spread_kernel, distances, split, cap),
        "spread_tokens",
        [(SMEM, where), (VMEM, gates), (HBM, raws[0]), (HBM, raws[1])],
        [jax.ShapeDtypeStruct((count * half, width), BF16)]
        + [jax.ShapeDtypeStruct((split * half, width), BF16)] * (count // split),
        [
            *place_scratch(count, gates, cap),
            pltpu.VMEM((count, 2 * half, 2 * cap), BF16),
            pltpu.VMEM((count, 2 * cap, width), BF16),
            pltpu.SemaphoreType.DMA((count, 2)),
        ],
        flops=2**20,
        moved=2**14,
    )


def backward_kernel(distances, cap, sides, where, pipe, gates, weights, *refs):
    count, rows = len(distances), 2 * cap
    tokens, outs = refs[: 2 * count], refs[2 * count : 2 * count + len(sides)]
    block, block_sems, picked, target, place, slot_gates, buffer, sems = refs[
        2 * count + len(sides) :
    ]
    half, tile = tokens[0].shape[0], buffer.shape[1]
    tiles = 4 * len(sides)
    first = (1 - pipe[0] + sides[0]) * 4

    def weight_tile(n):
        return weights.at[pl.ds(pl.multiple_of((first + n) % 8 * tile, tile), tile), :]

    fetch = []
    for i, token in enumerate(tokens):
        to = block.at[i // 2, pl.ds(i % 2 * half, half), :]
        fetch.append(pltpu.make_async_copy(token, to, block_sems.at[i]))
        fetch[-1].start()
    stream = Stream(weight_tile, buffer, sems)
    for n in range(stream.slots):
        stream.start(n)
    place_slots(distances, where, gates, cap, target, place, slot_gates)
    for copy in fetch:
        copy.wait()

    @pl.loop(0, count)
    def _(i):
        for n in range(block.shape[2] // TILE):
            cols = pl.ds(n * TILE, TILE)
            picked[pl.ds(pl.multiple_of(i * rows, rows), rows), cols] = jnp.dot(
                place[i], block[i, :, cols], preferred_element_type=F32
            ).astype(BF16)

    @pl.loop(0, tiles)
    def _(n):
        stream.wait(n)
        value = lax.dot_general(
            picked[...],
            buffer[n % stream.slots],
            (((1,), (1,)), ((), ())),
            preferred_element_type=F32,
        )
        value = gated(value, slot_gates[...])
        cols = pl.ds(pl.multiple_of(n % 4 * tile, tile), tile)
        for i, out in enumerate(outs):

            @pl.when(n // 4 == i)
            def _():
                out[:, cols] = value

        @pl.when(n + stream.slots < tiles)
        def _():
            stream.start(n + stream.slots)


def backward(distances, cap, sides, where, pipe, tokens, gates, weights, share):
    count, rows = len(distances), 2 * cap
    depth, width = weights.shape
    return kernel_call(
        functools.partial(backward_kernel, distances, cap, sides),
        "backward",
        [(SMEM, where), (SMEM, pipe), (VMEM, gates), (HBM, weights)] + [(ANY, x) for x in tokens],
        [jax.ShapeDtypeStruct((count * rows, depth // 2), BF16)] * len(sides),
        [
            pltpu.VMEM((count, gates.shape[1], width), BF16),
            pltpu.SemaphoreType.DMA((2 * count,)),
            pltpu.VMEM((count * rows, width), BF16),
            *place_scratch(count, gates, cap),
            pltpu.VMEM((4, depth // 8, width), BF16),
            pltpu.SemaphoreType.DMA((4, 4)),
        ],
        flops=len(sides) * count * rows * depth * width // share,
        moved=2 * (depth * width + count * rows * (depth + 2 * width)) // share,
        limit=18,
    )


def collect_kernel(groups, where, *refs):
    out, held, sems = refs[-3:]
    copies = []
    for g, distances in enumerate(groups):
        hold, recv = refs[2 * g], refs[2 * g + 1]
        rows = hold.shape[0] // len(distances)
        for i, d in enumerate(distances):
            at, n = pl.ds(i * rows, rows), len(copies)
            held[n] = (hold[at, :].astype(F32) + recv[at, :].astype(F32)).astype(BF16)
            to = pl.ds(pl.multiple_of(where[d % 8] * rows, rows), rows)
            copies.append(pltpu.make_async_copy(held.at[n], out.at[to, :], sems.at[n]))
            copies[-1].start()
    for copy in copies:
        copy.wait()


def collect(groups, where, arrays, rows, into=None):
    count = sum(len(distances) for distances in groups)
    out = jax.ShapeDtypeStruct((rows, arrays[0].shape[1]), BF16)
    inputs = [(SMEM, where)] + [(VMEM, x) for x in arrays]
    if into is not None:
        inputs.append((HBM, into))
    in_specs, arrays = zip(*inputs)
    return pl.pallas_call(
        functools.partial(collect_kernel, groups),
        in_specs=in_specs,
        out_specs=HBM,
        out_shape=out,
        scratch_shapes=[
            pltpu.VMEM((count, rows // 8, out.shape[1]), BF16),
            pltpu.SemaphoreType.DMA((count,)),
        ],
        input_output_aliases={} if into is None else {len(inputs) - 1: 0},
        compiler_params=pltpu.CompilerParams(vmem_limit_bytes=12 * 2**20),
        cost_estimate=pl.CostEstimate(
            flops=2**20, bytes_accessed=6 * count * rows * 128, transcendentals=0
        ),
        name="collect",
    )(*arrays)


def on_device_16(hidden_a, expert_weights, routes_a, gates_a, cotangent_b, routes_b, gates_b):
    me = lax.axis_index("expert").astype(jnp.int32)
    z, y, c = me // 4, me // 2 % 2, me % 2
    pipe = lax.axis_index("pipe").astype(jnp.int32).reshape(1)
    rows = hidden_a.shape[1] // 8
    cap = rows // 2
    tokens, width = cotangent_b.shape
    weights, hidden = expert_weights[0], hidden_a[0]

    ring = (jnp.where(y == 0, z, 7 - z) + jnp.arange(8, dtype=jnp.int32)) % 8
    to_z, to_y = jnp.minimum(ring, 7 - ring), (ring > 3).astype(jnp.int32)
    chips = to_z * 2 + to_y
    where = jnp.concatenate([chips, c.reshape(1), (to_z ^ z) * 2 + (to_y ^ y)])

    got, pair = {0: cotangent_b}, {}
    got[-1], got[1] = step_ring(cotangent_b, 1), step_ring(cotangent_b, -1)

    both = gates_of(routes_a, gates_a, routes_b, gates_b)
    four = jnp.stack([both] + [xor(both, j) for j in (1, 2, 3)])
    four = lax.dynamic_index_in_dim(four.reshape(4, 4, 4, 2 * tokens), me % 4, 2, False)
    weights, four = tie(weights, four)
    raw1 = raw_forward(0, width // 2, pin(hidden), pin(weights))
    every = jnp.stack([four] + [xor(four, 4 * k) for k in (1, 2, 3)])
    raw1, weights, every, got[-1], got[1] = tie(raw1, weights, every, got[-1], got[1])
    weights = pin(weights)
    every = lax.dynamic_index_in_dim(every, z, 2, False)
    gate = jnp.moveaxis(every.reshape(8, 2, 2, tokens), 2, 0).reshape(2, 8, 2 * tokens)
    gate_a, gate_b = gate[0], gate[1]

    def spread(distances, split, gates):
        return spread_tokens(distances, split, cap, where, gates, (pin(raw1), pin(raw2)))

    def bwd(distances, sides=(0, 1), share=1):
        values = [x for d in distances for x in (got[d], pair[d])]
        return backward(distances, cap, sides, where, pipe, values, gate_b, weights, share)

    got[-2], got[2] = step_ring(got[-1], 1), step_ring(got[1], -1)
    for d in (0, -1, 1):
        pair[d] = core(got[d])
    raw2 = raw_forward(width // 2, width // 2, pin(hidden), weights)
    raw2, pair[0], pair[-1], pair[1] = tie(raw2, pair[0], pair[-1], pair[1])

    keep1, other1, other2 = spread((3, -4, 2, -3), 2, gate_a)
    keep1, other1, other2, got[-2], got[2] = tie(keep1, other1, other2, got[-2], got[2])
    got[-3], got[3] = step_ring(got[-2], 1), step_ring(got[2], -1)
    other1, other2 = core(other1), core(other2)
    up = step_ring(add(keep1[:tokens], other1[:tokens]), 1)
    down = step_ring(add(keep1[tokens : 2 * tokens], other1[tokens:]), -1)
    pair[-2] = core(got[-2])
    gate_a, pair[-2], other2 = tie(gate_a, pair[-2], other2)
    keep2, other3 = spread((1, -2, -1, 0), 4, gate_a)
    keep2, gate_b = tie(keep2, gate_b)
    groups = (0, -1, 1, -2), (2, -3, 3), (-4,)
    for d in (0, -1, 1):
        pair[d] = pin(pair[d])
    send1, hold1 = bwd(groups[0], share=64)

    def mine(i, *more):
        at = slice(i * tokens, (i + 1) * tokens)
        return add(keep2[at], other3[at], *more)

    send1, got[-3], got[3], up, down, other3 = tie(send1, got[-3], got[3], up, down, other3)
    got[-4] = step_ring(got[-3], 1)
    up = add(keep1[2 * tokens : 3 * tokens], other2[:tokens], up)
    down = add(keep1[3 * tokens :], other2[tokens:], down)
    up, down = tie(up, down)
    down = step_ring(down, -1)
    recv1 = across(send1)
    pair[2], pair[-3], pair[3] = core(got[2]), core(got[-3]), core(got[3])
    other3 = core(other3)
    gate_b, other3 = tie(gate_b, other3)
    send2, hold2 = bwd(groups[1], share=64)

    hold2, send2, up, down, got[-4] = tie(hold2, send2, up, down, got[-4])
    up, down = step_ring(up, 1), step_ring(mine(1, down), -1)
    pair[-4] = core(got[-4])
    recv2 = across(send2)
    send3, hold3 = bwd(groups[2], share=64)

    send3, hold3, up, down, recv1 = tie(send3, hold3, up, down, recv1)
    up, down = step_ring(mine(0, up), 1), step_ring(mine(2, down), -1)
    recv3 = across(send3)
    hold3, recv2 = tie(hold3, recv2)
    grad = collect(groups[:2], where, (hold1, recv1, hold2, recv2), 8 * rows)
    grad, recv3 = tie(grad, recv3)
    mixed_a = mine(3, up, down)
    grad = collect(groups[2:], where, (hold3, recv3), 8 * rows, grad)
    return (mixed_a, grad[None])


def solution(mesh):
    in_specs = (
        P("expert", None, None),
        P("expert", None, "pipe"),
        P("expert", None),
        P("expert", None),
        P("expert", "pipe"),
        P("expert", None),
        P("expert", None),
    )
    out_specs = (P("expert", "pipe"), P("expert", None, "pipe"))
    tailored = mesh.shape["expert"] == 16 and mesh.shape["pipe"] == 2
    return jax.shard_map(
        on_device_16 if tailored else on_device_any,
        mesh=mesh,
        in_specs=in_specs,
        out_specs=out_specs,
        check_vma=False,
    )
```

```python
import functools

import jax
import jax.numpy as jnp
from jax import lax
from jax.experimental import pallas as pl
from jax.experimental.pallas import tpu as pltpu
from jax.sharding import PartitionSpec as P

BF16, F32 = jnp.bfloat16, jnp.float32
TILE = 512
LANES = 128
RAW_TILE = 256


def dense_gates(routes, gates, total):
    experts = jnp.arange(total, dtype=jnp.int32)[:, None, None]
    return jnp.sum(jnp.where(routes[None] == experts, gates[None], 0.0), axis=2)


def ranks_of(gate):
    tokens = gate.shape[-1]
    earlier = jnp.triu(jnp.ones((tokens, tokens), BF16), 1)
    counts = jnp.dot((gate > 0.0).astype(BF16), earlier, preferred_element_type=F32)
    return counts.astype(jnp.int32)


def add(*terms):
    total = terms[0].astype(F32)
    for term in terms[1:]:
        total = total + term.astype(F32)
    return total.astype(BF16)


def on_device_any(hidden_a, expert_weights, routes_a, gates_a, cotangent_b, routes_b, gates_b):
    groups = lax.axis_size("expert")
    me = lax.axis_index("expert")
    total = expert_weights.shape[0] * groups
    rows = hidden_a.shape[1]
    cap = rows // groups
    tokens, width = cotangent_b.shape
    weights = expert_weights[0]

    both = jnp.stack(
        [dense_gates(routes_a, gates_a, total), dense_gates(routes_b, gates_b, total)], axis=1
    )
    every = lax.all_gather(both, "expert", axis=0, tiled=False)
    own = lax.dynamic_index_in_dim(every, me, axis=1, keepdims=False)
    gathered = lax.all_gather(cotangent_b, "expert", axis=0, tiled=True)

    def placement(gate):
        slots = jnp.arange(cap, dtype=jnp.int32)[None, :, None]
        hit = (gate > 0.0)[:, None, :] & (ranks_of(gate)[:, None, :] == slots)
        return hit.astype(BF16), jnp.sum(jnp.where(hit, gate[:, None, :], 0.0), axis=2)

    hit_a, slot_gate_a = placement(own[:, 0])
    hit_b, slot_gate_b = placement(own[:, 1])

    outputs = jnp.einsum("rf,fd->rd", hidden_a[0], weights, preferred_element_type=F32)
    scaled = (outputs * slot_gate_a.reshape(rows, 1)).astype(BF16)
    spread = jnp.einsum(
        "sct,scd->std", hit_a, scaled.reshape(groups, cap, width), preferred_element_type=F32
    ).astype(BF16)
    mixed_a = lax.psum_scatter(
        spread.reshape(groups * tokens, width), "expert", scatter_dimension=0, tiled=True
    )
    picked = jnp.einsum(
        "sct,std->scd",
        hit_b,
        gathered.reshape(groups, tokens, width),
        preferred_element_type=F32,
    ).astype(BF16)
    partial_value = jnp.einsum(
        "rd,fd->rf", picked.reshape(rows, width), weights, preferred_element_type=F32
    )
    partial_value = (partial_value * slot_gate_b.reshape(rows, 1)).astype(BF16)
    grad = lax.psum_scatter(partial_value, "pipe", scatter_dimension=1, tiled=True)
    return (mixed_a, grad[None])


RING = [(0, 0), (1, 0), (2, 0), (3, 0), (3, 1), (2, 1), (1, 1), (0, 1)]


def step_ring(value, way):
    pairs = []
    for place, (z, y) in enumerate(RING):
        to_z, to_y = RING[(place + way) % 8]
        pairs += [(z * 4 + y * 2 + c, to_z * 4 + to_y * 2 + c) for c in range(2)]
    return lax.ppermute(value, "expert", pairs)


def xor(value, bits):
    return lax.ppermute(value, "expert", [(i, i ^ bits) for i in range(16)])


def core(value):
    return xor(value, 1)


def across(value):
    return lax.ppermute(value, "pipe", [(0, 1), (1, 0)])


def pin(value):
    return pltpu.with_memory_space_constraint(value, pltpu.HBM)


def tie(*values):
    return lax.optimization_barrier(values)


SMEM = pl.BlockSpec(memory_space=pltpu.SMEM)
VMEM = pl.BlockSpec(memory_space=pltpu.VMEM)
HBM = pl.BlockSpec(memory_space=pltpu.HBM)
ANY = pl.BlockSpec(memory_space=pl.ANY)


def kernel_call(kernel, name, inputs, out_shape, scratch, flops, moved, limit=9):
    in_specs, arrays = zip(*inputs)
    return pl.pallas_call(
        kernel,
        in_specs=in_specs,
        out_specs=[VMEM] * len(out_shape),
        out_shape=out_shape,
        scratch_shapes=scratch,
        compiler_params=pltpu.CompilerParams(vmem_limit_bytes=limit * 2**20),
        cost_estimate=pl.CostEstimate(flops=flops, bytes_accessed=moved, transcendentals=0),
        name=name,
    )(*arrays)


def gates_kernel(*refs):
    sources, out, held, sems = refs[:4], refs[4], refs[5:9], refs[9]
    copies = [pltpu.make_async_copy(x, y, sems.at[i]) for i, (x, y) in enumerate(zip(sources, held))]
    for copy in copies:
        copy.start()
    for copy in copies:
        copy.wait()
    top, tokens = held[0].shape
    experts = lax.broadcasted_iota(jnp.int32, (out.shape[0], tokens), 0)
    for i in range(2):
        routes, gates = held[2 * i : 2 * i + 2]
        total = jnp.zeros(experts.shape, F32)
        for k in range(top):
            total += jnp.where(routes[k : k + 1, :] == experts, gates[k : k + 1, :], 0.0)
        out[:, pl.ds(i * tokens, tokens)] = total


def gates_of(*arrays):
    tokens, top = arrays[0].shape
    arrays = [pin(x.T) for x in arrays]
    return kernel_call(
        gates_kernel,
        "gates",
        [(HBM, x) for x in arrays],
        [jax.ShapeDtypeStruct((16, 2 * tokens), F32)],
        [pltpu.VMEM((top, tokens), x.dtype) for x in arrays] + [pltpu.SemaphoreType.DMA((4,))],
        flops=2**20,
        moved=2**17,
    )[0]


def place_slots(distances, where, gates, cap, target, place, slot_gates):
    gate = gates[...]
    tokens = gate.shape[1] // 2
    row = lax.broadcasted_iota(jnp.int32, (2 * tokens, 2 * tokens), 0)
    col = lax.broadcasted_iota(jnp.int32, (2 * tokens, 2 * tokens), 1)
    earlier = ((row < col) & (row // tokens == col // tokens)).astype(F32).astype(BF16)
    chosen = (gate > 0.0).astype(F32).astype(BF16)
    rank = jnp.dot(chosen, earlier, preferred_element_type=F32)
    second = (lax.broadcasted_iota(jnp.int32, gate.shape, 1) // tokens) ^ where[8]
    target[...] = jnp.where(gate > 0.0, rank + (second * cap).astype(F32), -1.0)
    slots = lax.broadcasted_iota(jnp.int32, (2 * cap, 2 * tokens), 0).astype(F32)
    for i, d in enumerate(distances):
        block = pl.ds(where[9 + d % 8], 1)
        hit = target[block, :] == slots
        place[i] = hit.astype(F32).astype(BF16)
        total = jnp.sum(jnp.where(hit, gates[block, :], 0.0), axis=1, keepdims=True)
        slot_gates[pl.ds(i * 2 * cap, 2 * cap), :] = jnp.broadcast_to(total, (2 * cap, LANES))


def place_scratch(count, gates, cap):
    return [
        pltpu.VMEM(gates.shape, F32),
        pltpu.VMEM((count, 2 * cap, gates.shape[1]), BF16),
        pltpu.VMEM((count * 2 * cap, LANES), F32),
    ]


def gated(value, slot_gates):
    factor = jnp.concatenate([slot_gates] * (value.shape[1] // LANES), axis=1)
    return (value * factor).astype(BF16)


class Stream:
    def __init__(self, tile, buffer, sems):
        self.tile, self.buffer, self.sems = tile, buffer, sems
        self.slots, self.parts = sems.shape

    def copies(self, n):
        slot = n % self.slots
        rows = self.buffer.shape[1] // self.parts
        source = self.tile(n)
        for part in range(self.parts):
            at = pl.ds(part * rows, rows)
            yield pltpu.make_async_copy(
                source.at[at, :], self.buffer.at[slot, at, :], self.sems.at[slot, part]
            )

    def start(self, n):
        for copy in self.copies(n):
            copy.start()

    def wait(self, n):
        for copy in self.copies(n):
            copy.wait()


def raw_kernel(first, hidden, weights, out, held, held_sems, buffer, sems, staged, out_sems):
    tiles = out.shape[1] // RAW_TILE
    stream = Stream(
        lambda n: weights.at[:, pl.ds(pl.multiple_of(first + n * RAW_TILE, RAW_TILE), RAW_TILE)], buffer, sems
    )
    rows = held.shape[0] // held_sems.shape[0]
    fetch = []
    for i in range(held_sems.shape[0]):
        at = pl.ds(i * rows, rows)
        fetch.append(pltpu.make_async_copy(hidden.at[at, :], held.at[at, :], held_sems.at[i]))
        fetch[-1].start()
    stream.start(0)

    def put(n):
        cols = pl.ds(pl.multiple_of(n * RAW_TILE, RAW_TILE), RAW_TILE)
        return pltpu.make_async_copy(staged.at[n % 2], out.at[:, cols], out_sems.at[n % 2])

    for copy in fetch:
        copy.wait()
    for n in range(1, stream.slots):
        stream.start(n)

    @pl.loop(0, tiles)
    def _(n):
        stream.wait(n)

        @pl.when(n >= 2)
        def _():
            put(n - 2).wait()

        value = jnp.dot(held[...], buffer[n % stream.slots], preferred_element_type=F32)
        staged[n % 2] = value.astype(BF16)
        put(n).start()

        @pl.when(n + stream.slots < tiles)
        def _():
            stream.start(n + stream.slots)

    put(tiles - 2).wait()
    put(tiles - 1).wait()


def raw_forward(first, width, hidden, weights):
    rows, depth = hidden.shape
    return pl.pallas_call(
        functools.partial(raw_kernel, first),
        in_specs=[HBM, HBM],
        out_specs=HBM,
        out_shape=pltpu.HBM((rows, width), BF16),
        scratch_shapes=[
            pltpu.VMEM(hidden.shape, BF16),
            pltpu.SemaphoreType.DMA((4,)),
            pltpu.VMEM((3, depth, RAW_TILE), BF16),
            pltpu.SemaphoreType.DMA((3, 4)),
            pltpu.VMEM((2, rows, RAW_TILE), BF16),
            pltpu.SemaphoreType.DMA((2,)),
        ],
        compiler_params=pltpu.CompilerParams(vmem_limit_bytes=9 * 2**20),
        cost_estimate=pl.CostEstimate(
            flops=2 * rows * depth * width,
            bytes_accessed=2 * (depth * width + rows * (depth + width)),
            transcendentals=0,
        ),
        name="raw_forward",
    )(hidden, weights)


def spread_kernel(distances, split, cap, where, gates, *refs):
    count = len(distances)
    raws, (keep, *others), scratch = refs[:2], refs[2:-6], refs[-6:]
    target, place, slot_gates, to_tokens, held, sems = scratch
    rows, half = 2 * cap, gates.shape[1] // 2
    width = raws[0].shape[1]

    def fetch(i, start):
        return [
            pltpu.make_async_copy(
                raw.at[pl.ds(start, rows), :],
                held.at[i, :, pl.ds(j * width, width)],
                sems.at[i, j],
            )
            for j, raw in enumerate(raws)
        ]

    for i, d in enumerate(distances):
        for copy in fetch(i, pl.multiple_of(where[d % 8] * rows, rows)):
            copy.start()
    place_slots(distances, where, gates, cap, target, place, slot_gates)
    tokens = 2 * half
    same = lax.broadcasted_iota(jnp.int32, (tokens, tokens), 0) == lax.broadcasted_iota(
        jnp.int32, (tokens, tokens), 1
    )
    same = same.astype(F32).astype(BF16)
    for i in range(count):
        to_tokens[i] = lax.dot_general(
            same, place[i], (((1,), (1,)), ((), ())), preferred_element_type=F32
        ).astype(BF16)
    for g, other in enumerate(others):

        @pl.loop(0, split)
        def _(j):
            i = g * split + j
            for copy in fetch(i, 0):
                copy.wait()
            for n in range(2 * width // TILE):
                cols = pl.ds(n * TILE, TILE)
                part = held[i, :, cols].astype(F32)
                part = gated(part, slot_gates[pl.ds(pl.multiple_of(i * rows, rows), rows), :])
                part = jnp.dot(to_tokens[i], part, preferred_element_type=F32).astype(BF16)
                keep[pl.ds(pl.multiple_of(i * half, half), half), cols] = part[:half]
                other[pl.ds(pl.multiple_of(j * half, half), half), cols] = part[half:]


def spread_tokens(distances, split, cap, where, gates, raws):
    count, half, width = len(distances), gates.shape[1] // 2, 2 * raws[0].shape[1]
    return kernel_call(
        functools.partial(spread_kernel, distances, split, cap),
        "spread_tokens",
        [(SMEM, where), (VMEM, gates), (HBM, raws[0]), (HBM, raws[1])],
        [jax.ShapeDtypeStruct((count * half, width), BF16)]
        + [jax.ShapeDtypeStruct((split * half, width), BF16)] * (count // split),
        [
            *place_scratch(count, gates, cap),
            pltpu.VMEM((count, 2 * half, 2 * cap), BF16),
            pltpu.VMEM((count, 2 * cap, width), BF16),
            pltpu.SemaphoreType.DMA((count, 2)),
        ],
        flops=2**20,
        moved=2**14,
    )


def backward_kernel(distances, cap, sides, where, pipe, gates, weights, *refs):
    count, rows = len(distances), 2 * cap
    tokens, outs = refs[: 2 * count], refs[2 * count : 2 * count + len(sides)]
    block, block_sems, picked, target, place, slot_gates, buffer, sems = refs[
        2 * count + len(sides) :
    ]
    half, tile = tokens[0].shape[0], buffer.shape[1]
    tiles = 4 * len(sides)
    first = (1 - pipe[0] + sides[0]) * 4

    def weight_tile(n):
        return weights.at[pl.ds(pl.multiple_of((first + n) % 8 * tile, tile), tile), :]

    fetch = []
    for i, token in enumerate(tokens):
        to = block.at[i // 2, pl.ds(i % 2 * half, half), :]
        fetch.append(pltpu.make_async_copy(token, to, block_sems.at[i]))
        fetch[-1].start()
    stream = Stream(weight_tile, buffer, sems)
    for n in range(stream.slots):
        stream.start(n)
    place_slots(distances, where, gates, cap, target, place, slot_gates)
    for copy in fetch:
        copy.wait()

    @pl.loop(0, count)
    def _(i):
        for n in range(block.shape[2] // TILE):
            cols = pl.ds(n * TILE, TILE)
            picked[pl.ds(pl.multiple_of(i * rows, rows), rows), cols] = jnp.dot(
                place[i], block[i, :, cols], preferred_element_type=F32
            ).astype(BF16)

    @pl.loop(0, tiles)
    def _(n):
        stream.wait(n)
        value = lax.dot_general(
            picked[...],
            buffer[n % stream.slots],
            (((1,), (1,)), ((), ())),
            preferred_element_type=F32,
        )
        value = gated(value, slot_gates[...])
        cols = pl.ds(pl.multiple_of(n % 4 * tile, tile), tile)
        for i, out in enumerate(outs):

            @pl.when(n // 4 == i)
            def _():
                out[:, cols] = value

        @pl.when(n + stream.slots < tiles)
        def _():
            stream.start(n + stream.slots)


def backward(distances, cap, sides, where, pipe, tokens, gates, weights, share):
    count, rows = len(distances), 2 * cap
    depth, width = weights.shape
    return kernel_call(
        functools.partial(backward_kernel, distances, cap, sides),
        "backward",
        [(SMEM, where), (SMEM, pipe), (VMEM, gates), (HBM, weights)] + [(ANY, x) for x in tokens],
        [jax.ShapeDtypeStruct((count * rows, depth // 2), BF16)] * len(sides),
        [
            pltpu.VMEM((count, gates.shape[1], width), BF16),
            pltpu.SemaphoreType.DMA((2 * count,)),
            pltpu.VMEM((count * rows, width), BF16),
            *place_scratch(count, gates, cap),
            pltpu.VMEM((4, depth // 8, width), BF16),
            pltpu.SemaphoreType.DMA((4, 4)),
        ],
        flops=len(sides) * count * rows * depth * width // share,
        moved=2 * (depth * width + count * rows * (depth + 2 * width)) // share,
        limit=16,
    )


def collect_kernel(groups, where, *refs):
    out, held, sems = refs[-3:]
    copies = []
    for g, distances in enumerate(groups):
        hold, recv = refs[2 * g], refs[2 * g + 1]
        rows = hold.shape[0] // len(distances)
        for i, d in enumerate(distances):
            at, n = pl.ds(i * rows, rows), len(copies)
            held[n] = (hold[at, :].astype(F32) + recv[at, :].astype(F32)).astype(BF16)
            to = pl.ds(pl.multiple_of(where[d % 8] * rows, rows), rows)
            copies.append(pltpu.make_async_copy(held.at[n], out.at[to, :], sems.at[n]))
            copies[-1].start()
    for copy in copies:
        copy.wait()


def collect(groups, where, arrays, rows, into=None):
    count = sum(len(distances) for distances in groups)
    out = jax.ShapeDtypeStruct((rows, arrays[0].shape[1]), BF16)
    inputs = [(SMEM, where)] + [(VMEM, x) for x in arrays]
    if into is not None:
        inputs.append((HBM, into))
    in_specs, arrays = zip(*inputs)
    return pl.pallas_call(
        functools.partial(collect_kernel, groups),
        in_specs=in_specs,
        out_specs=HBM,
        out_shape=out,
        scratch_shapes=[
            pltpu.VMEM((count, rows // 8, out.shape[1]), BF16),
            pltpu.SemaphoreType.DMA((count,)),
        ],
        input_output_aliases={} if into is None else {len(inputs) - 1: 0},
        compiler_params=pltpu.CompilerParams(vmem_limit_bytes=9 * 2**20),
        cost_estimate=pl.CostEstimate(
            flops=2**20, bytes_accessed=6 * count * rows * 128, transcendentals=0
        ),
        name="collect",
    )(*arrays)


def on_device_16(hidden_a, expert_weights, routes_a, gates_a, cotangent_b, routes_b, gates_b):
    me = lax.axis_index("expert").astype(jnp.int32)
    z, y, c = me // 4, me // 2 % 2, me % 2
    pipe = lax.axis_index("pipe").astype(jnp.int32).reshape(1)
    rows = hidden_a.shape[1] // 8
    cap = rows // 2
    tokens, width = cotangent_b.shape
    weights, hidden = expert_weights[0], hidden_a[0]

    ring = (jnp.where(y == 0, z, 7 - z) + jnp.arange(8, dtype=jnp.int32)) % 8
    to_z, to_y = jnp.minimum(ring, 7 - ring), (ring > 3).astype(jnp.int32)
    chips = to_z * 2 + to_y
    where = jnp.concatenate([chips, c.reshape(1), (to_z ^ z) * 2 + (to_y ^ y)])

    got, pair = {0: cotangent_b}, {}
    got[-1], got[1] = step_ring(cotangent_b, 1), step_ring(cotangent_b, -1)

    both = gates_of(routes_a, gates_a, routes_b, gates_b)
    four = jnp.stack([both] + [xor(both, j) for j in (1, 2, 3)])
    four = lax.dynamic_index_in_dim(four.reshape(4, 4, 4, 2 * tokens), me % 4, 2, False)
    weights, four = tie(weights, four)
    raw1 = raw_forward(0, width // 2, pin(hidden), pin(weights))
    every = jnp.stack([four] + [xor(four, 4 * k) for k in (1, 2, 3)])
    raw1, weights, every, got[-1], got[1] = tie(raw1, weights, every, got[-1], got[1])
    weights = pin(weights)
    every = lax.dynamic_index_in_dim(every, z, 2, False)
    gate = jnp.moveaxis(every.reshape(8, 2, 2, tokens), 2, 0).reshape(2, 8, 2 * tokens)
    gate_a, gate_b = gate[0], gate[1]

    def spread(distances, split, gates):
        return spread_tokens(distances, split, cap, where, gates, (pin(raw1), pin(raw2)))

    def bwd(distances, sides=(0, 1), share=1):
        values = [x for d in distances for x in (got[d], pair[d])]
        return backward(distances, cap, sides, where, pipe, values, gate_b, weights, share)

    got[-2], got[2] = step_ring(got[-1], 1), step_ring(got[1], -1)
    for d in (0, -1, 1):
        pair[d] = core(got[d])
    raw2 = raw_forward(width // 2, width // 2, pin(hidden), weights)
    raw2, pair[0], pair[-1], pair[1] = tie(raw2, pair[0], pair[-1], pair[1])

    keep1, other1, other2 = spread((3, -4, 2, -3), 2, gate_a)
    keep1, other1, other2, got[-2], got[2] = tie(keep1, other1, other2, got[-2], got[2])
    got[-3], got[3] = step_ring(got[-2], 1), step_ring(got[2], -1)
    other1, other2 = core(other1), core(other2)
    up = step_ring(add(keep1[:tokens], other1[:tokens]), 1)
    down = step_ring(add(keep1[tokens : 2 * tokens], other1[tokens:]), -1)
    pair[-2] = core(got[-2])
    gate_a, pair[-2], other2 = tie(gate_a, pair[-2], other2)
    keep2, other3 = spread((1, -2, -1, 0), 4, gate_a)
    keep2, gate_b = tie(keep2, gate_b)
    groups = (0, -1, 1, -2), (2, -3, 3), (-4,)
    for d in (0, -1, 1):
        pair[d] = pin(pair[d])
    send1, hold1 = bwd(groups[0], share=64)

    def mine(i, *more):
        at = slice(i * tokens, (i + 1) * tokens)
        return add(keep2[at], other3[at], *more)

    send1, got[-3], got[3], up, down, other3 = tie(send1, got[-3], got[3], up, down, other3)
    got[-4] = step_ring(got[-3], 1)
    up = add(keep1[2 * tokens : 3 * tokens], other2[:tokens], up)
    down = add(keep1[3 * tokens :], other2[tokens:], down)
    up, down = tie(up, down)
    down = step_ring(down, -1)
    recv1 = across(send1)
    pair[2], pair[-3], pair[3] = core(got[2]), core(got[-3]), core(got[3])
    other3 = core(other3)
    gate_b, other3 = tie(gate_b, other3)
    send2, hold2 = bwd(groups[1], share=64)

    hold2, send2, up, down, got[-4] = tie(hold2, send2, up, down, got[-4])
    up, down = step_ring(up, 1), step_ring(mine(1, down), -1)
    pair[-4] = core(got[-4])
    recv2 = across(send2)
    send3, hold3 = bwd(groups[2], share=64)

    send3, hold3, up, down, recv1 = tie(send3, hold3, up, down, recv1)
    up, down = step_ring(mine(0, up), 1), step_ring(mine(2, down), -1)
    recv3 = across(send3)
    hold3, recv2 = tie(hold3, recv2)
    grad = collect(groups[:2], where, (hold1, recv1, hold2, recv2), 8 * rows)
    grad, recv3 = tie(grad, recv3)
    mixed_a = mine(3, up, down)
    grad = collect(groups[2:], where, (hold3, recv3), 8 * rows, grad)
    return (mixed_a, grad[None])


def solution(mesh):
    in_specs = (
        P("expert", None, None),
        P("expert", None, "pipe"),
        P("expert", None),
        P("expert", None),
        P("expert", "pipe"),
        P("expert", None),
        P("expert", None),
    )
    out_specs = (P("expert", "pipe"), P("expert", None, "pipe"))
    tailored = mesh.shape["expert"] == 16 and mesh.shape["pipe"] == 2
    return jax.shard_map(
        on_device_16 if tailored else on_device_any,
        mesh=mesh,
        in_specs=in_specs,
        out_specs=out_specs,
        check_vma=False,
    )
```

```python
import functools

import jax
import jax.numpy as jnp
from jax import lax
from jax.experimental import pallas as pl
from jax.experimental.pallas import tpu as pltpu
from jax.sharding import PartitionSpec as P

BF16, F32 = jnp.bfloat16, jnp.float32
TILE = 512
LANES = 128
RAW_TILE = 256


def dense_gates(routes, gates, total):
    experts = jnp.arange(total, dtype=jnp.int32)[:, None, None]
    return jnp.sum(jnp.where(routes[None] == experts, gates[None], 0.0), axis=2)


def ranks_of(gate):
    tokens = gate.shape[-1]
    earlier = jnp.triu(jnp.ones((tokens, tokens), BF16), 1)
    counts = jnp.dot((gate > 0.0).astype(BF16), earlier, preferred_element_type=F32)
    return counts.astype(jnp.int32)


def add(*terms):
    total = terms[0].astype(F32)
    for term in terms[1:]:
        total = total + term.astype(F32)
    return total.astype(BF16)


def on_device_any(hidden_a, expert_weights, routes_a, gates_a, cotangent_b, routes_b, gates_b):
    groups = lax.axis_size("expert")
    me = lax.axis_index("expert")
    total = expert_weights.shape[0] * groups
    rows = hidden_a.shape[1]
    cap = rows // groups
    tokens, width = cotangent_b.shape
    weights = expert_weights[0]

    both = jnp.stack(
        [dense_gates(routes_a, gates_a, total), dense_gates(routes_b, gates_b, total)], axis=1
    )
    every = lax.all_gather(both, "expert", axis=0, tiled=False)
    own = lax.dynamic_index_in_dim(every, me, axis=1, keepdims=False)
    gathered = lax.all_gather(cotangent_b, "expert", axis=0, tiled=True)

    def placement(gate):
        slots = jnp.arange(cap, dtype=jnp.int32)[None, :, None]
        hit = (gate > 0.0)[:, None, :] & (ranks_of(gate)[:, None, :] == slots)
        return hit.astype(BF16), jnp.sum(jnp.where(hit, gate[:, None, :], 0.0), axis=2)

    hit_a, slot_gate_a = placement(own[:, 0])
    hit_b, slot_gate_b = placement(own[:, 1])

    outputs = jnp.einsum("rf,fd->rd", hidden_a[0], weights, preferred_element_type=F32)
    scaled = (outputs * slot_gate_a.reshape(rows, 1)).astype(BF16)
    spread = jnp.einsum(
        "sct,scd->std", hit_a, scaled.reshape(groups, cap, width), preferred_element_type=F32
    ).astype(BF16)
    mixed_a = lax.psum_scatter(
        spread.reshape(groups * tokens, width), "expert", scatter_dimension=0, tiled=True
    )
    picked = jnp.einsum(
        "sct,std->scd",
        hit_b,
        gathered.reshape(groups, tokens, width),
        preferred_element_type=F32,
    ).astype(BF16)
    partial_value = jnp.einsum(
        "rd,fd->rf", picked.reshape(rows, width), weights, preferred_element_type=F32
    )
    partial_value = (partial_value * slot_gate_b.reshape(rows, 1)).astype(BF16)
    grad = lax.psum_scatter(partial_value, "pipe", scatter_dimension=1, tiled=True)
    return (mixed_a, grad[None])


RING = [(0, 0), (1, 0), (2, 0), (3, 0), (3, 1), (2, 1), (1, 1), (0, 1)]


def step_ring(value, way):
    pairs = []
    for place, (z, y) in enumerate(RING):
        to_z, to_y = RING[(place + way) % 8]
        pairs += [(z * 4 + y * 2 + c, to_z * 4 + to_y * 2 + c) for c in range(2)]
    return lax.ppermute(value, "expert", pairs)


def xor(value, bits):
    return lax.ppermute(value, "expert", [(i, i ^ bits) for i in range(16)])


def core(value):
    return xor(value, 1)


def across(value):
    return lax.ppermute(value, "pipe", [(0, 1), (1, 0)])


def pin(value):
    return pltpu.with_memory_space_constraint(value, pltpu.HBM)


def tie(*values):
    return lax.optimization_barrier(values)


SMEM = pl.BlockSpec(memory_space=pltpu.SMEM)
VMEM = pl.BlockSpec(memory_space=pltpu.VMEM)
HBM = pl.BlockSpec(memory_space=pltpu.HBM)
ANY = pl.BlockSpec(memory_space=pl.ANY)


def kernel_call(kernel, name, inputs, out_shape, scratch, flops, moved, limit=9):
    in_specs, arrays = zip(*inputs)
    return pl.pallas_call(
        kernel,
        in_specs=in_specs,
        out_specs=[VMEM] * len(out_shape),
        out_shape=out_shape,
        scratch_shapes=scratch,
        compiler_params=pltpu.CompilerParams(vmem_limit_bytes=limit * 2**20),
        cost_estimate=pl.CostEstimate(flops=flops, bytes_accessed=moved, transcendentals=0),
        name=name,
    )(*arrays)


def gates_kernel(*refs):
    sources, out, held, sems = refs[:4], refs[4], refs[5:9], refs[9]
    copies = [pltpu.make_async_copy(x, y, sems.at[i]) for i, (x, y) in enumerate(zip(sources, held))]
    for copy in copies:
        copy.start()
    for copy in copies:
        copy.wait()
    top, tokens = held[0].shape
    experts = lax.broadcasted_iota(jnp.int32, (out.shape[0], tokens), 0)
    for i in range(2):
        routes, gates = held[2 * i : 2 * i + 2]
        total = jnp.zeros(experts.shape, F32)
        for k in range(top):
            total += jnp.where(routes[k : k + 1, :] == experts, gates[k : k + 1, :], 0.0)
        out[:, pl.ds(i * tokens, tokens)] = total


def gates_of(*arrays):
    tokens, top = arrays[0].shape
    arrays = [pin(x.T) for x in arrays]
    return kernel_call(
        gates_kernel,
        "gates",
        [(HBM, x) for x in arrays],
        [jax.ShapeDtypeStruct((16, 2 * tokens), F32)],
        [pltpu.VMEM((top, tokens), x.dtype) for x in arrays] + [pltpu.SemaphoreType.DMA((4,))],
        flops=2**20,
        moved=2**17,
    )[0]


def place_slots(distances, where, gates, cap, target, place, slot_gates):
    gate = gates[...]
    tokens = gate.shape[1] // 2
    row = lax.broadcasted_iota(jnp.int32, (2 * tokens, 2 * tokens), 0)
    col = lax.broadcasted_iota(jnp.int32, (2 * tokens, 2 * tokens), 1)
    earlier = ((row < col) & (row // tokens == col // tokens)).astype(F32).astype(BF16)
    chosen = (gate > 0.0).astype(F32).astype(BF16)
    rank = jnp.dot(chosen, earlier, preferred_element_type=F32)
    second = (lax.broadcasted_iota(jnp.int32, gate.shape, 1) // tokens) ^ where[8]
    target[...] = jnp.where(gate > 0.0, rank + (second * cap).astype(F32), -1.0)
    slots = lax.broadcasted_iota(jnp.int32, (2 * cap, 2 * tokens), 0).astype(F32)
    for i, d in enumerate(distances):
        block = pl.ds(where[9 + d % 8], 1)
        hit = target[block, :] == slots
        place[i] = hit.astype(F32).astype(BF16)
        total = jnp.sum(jnp.where(hit, gates[block, :], 0.0), axis=1, keepdims=True)
        slot_gates[pl.ds(i * 2 * cap, 2 * cap), :] = jnp.broadcast_to(total, (2 * cap, LANES))


def place_scratch(count, gates, cap):
    return [
        pltpu.VMEM(gates.shape, F32),
        pltpu.VMEM((count, 2 * cap, gates.shape[1]), BF16),
        pltpu.VMEM((count * 2 * cap, LANES), F32),
    ]


def gated(value, slot_gates):
    factor = jnp.concatenate([slot_gates] * (value.shape[1] // LANES), axis=1)
    return (value * factor).astype(BF16)


class Stream:
    def __init__(self, tile, buffer, sems):
        self.tile, self.buffer, self.sems = tile, buffer, sems
        self.slots, self.parts = sems.shape

    def copies(self, n):
        slot = n % self.slots
        rows = self.buffer.shape[1] // self.parts
        source = self.tile(n)
        for part in range(self.parts):
            at = pl.ds(part * rows, rows)
            yield pltpu.make_async_copy(
                source.at[at, :], self.buffer.at[slot, at, :], self.sems.at[slot, part]
            )

    def start(self, n):
        for copy in self.copies(n):
            copy.start()

    def wait(self, n):
        for copy in self.copies(n):
            copy.wait()


def raw_kernel(first, hidden, weights, out, held, held_sems, buffer, sems, staged, out_sems):
    tiles = out.shape[1] // RAW_TILE
    stream = Stream(
        lambda n: weights.at[:, pl.ds(pl.multiple_of(first + n * RAW_TILE, RAW_TILE), RAW_TILE)], buffer, sems
    )
    rows = held.shape[0] // held_sems.shape[0]
    fetch = []
    for i in range(held_sems.shape[0]):
        at = pl.ds(i * rows, rows)
        fetch.append(pltpu.make_async_copy(hidden.at[at, :], held.at[at, :], held_sems.at[i]))
        fetch[-1].start()
    stream.start(0)

    def put(n):
        cols = pl.ds(pl.multiple_of(n * RAW_TILE, RAW_TILE), RAW_TILE)
        return pltpu.make_async_copy(staged.at[n % 2], out.at[:, cols], out_sems.at[n % 2])

    for copy in fetch:
        copy.wait()
    for n in range(1, stream.slots):
        stream.start(n)

    @pl.loop(0, tiles)
    def _(n):
        stream.wait(n)

        @pl.when(n >= 2)
        def _():
            put(n - 2).wait()

        value = jnp.dot(held[...], buffer[n % stream.slots], preferred_element_type=F32)
        staged[n % 2] = value.astype(BF16)
        put(n).start()

        @pl.when(n + stream.slots < tiles)
        def _():
            stream.start(n + stream.slots)

    put(tiles - 2).wait()
    put(tiles - 1).wait()


def raw_forward(first, width, hidden, weights):
    rows, depth = hidden.shape
    return pl.pallas_call(
        functools.partial(raw_kernel, first),
        in_specs=[HBM, HBM],
        out_specs=HBM,
        out_shape=pltpu.HBM((rows, width), BF16),
        scratch_shapes=[
            pltpu.VMEM(hidden.shape, BF16),
            pltpu.SemaphoreType.DMA((4,)),
            pltpu.VMEM((3, depth, RAW_TILE), BF16),
            pltpu.SemaphoreType.DMA((3, 4)),
            pltpu.VMEM((2, rows, RAW_TILE), BF16),
            pltpu.SemaphoreType.DMA((2,)),
        ],
        compiler_params=pltpu.CompilerParams(vmem_limit_bytes=9 * 2**20),
        cost_estimate=pl.CostEstimate(
            flops=2 * rows * depth * width,
            bytes_accessed=2 * (depth * width + rows * (depth + width)),
            transcendentals=0,
        ),
        name="raw_forward",
    )(hidden, weights)


def spread_kernel(distances, split, cap, where, gates, *refs):
    count = len(distances)
    raws, (keep, *others), scratch = refs[:2], refs[2:-6], refs[-6:]
    target, place, slot_gates, to_tokens, held, sems = scratch
    rows, half = 2 * cap, gates.shape[1] // 2
    width = raws[0].shape[1]

    def fetch(i, start):
        return [
            pltpu.make_async_copy(
                raw.at[pl.ds(start, rows), :],
                held.at[i, :, pl.ds(j * width, width)],
                sems.at[i, j],
            )
            for j, raw in enumerate(raws)
        ]

    for i, d in enumerate(distances):
        for copy in fetch(i, pl.multiple_of(where[d % 8] * rows, rows)):
            copy.start()
    place_slots(distances, where, gates, cap, target, place, slot_gates)
    tokens = 2 * half
    same = lax.broadcasted_iota(jnp.int32, (tokens, tokens), 0) == lax.broadcasted_iota(
        jnp.int32, (tokens, tokens), 1
    )
    same = same.astype(F32).astype(BF16)
    for i in range(count):
        to_tokens[i] = lax.dot_general(
            same, place[i], (((1,), (1,)), ((), ())), preferred_element_type=F32
        ).astype(BF16)
    for g, other in enumerate(others):

        @pl.loop(0, split)
        def _(j):
            i = g * split + j
            for copy in fetch(i, 0):
                copy.wait()
            for n in range(2 * width // TILE):
                cols = pl.ds(n * TILE, TILE)
                part = held[i, :, cols].astype(F32)
                part = gated(part, slot_gates[pl.ds(pl.multiple_of(i * rows, rows), rows), :])
                part = jnp.dot(to_tokens[i], part, preferred_element_type=F32).astype(BF16)
                keep[pl.ds(pl.multiple_of(i * half, half), half), cols] = part[:half]
                other[pl.ds(pl.multiple_of(j * half, half), half), cols] = part[half:]


def spread_tokens(distances, split, cap, where, gates, raws):
    count, half, width = len(distances), gates.shape[1] // 2, 2 * raws[0].shape[1]
    return kernel_call(
        functools.partial(spread_kernel, distances, split, cap),
        "spread_tokens",
        [(SMEM, where), (VMEM, gates), (HBM, raws[0]), (HBM, raws[1])],
        [jax.ShapeDtypeStruct((count * half, width), BF16)]
        + [jax.ShapeDtypeStruct((split * half, width), BF16)] * (count // split),
        [
            *place_scratch(count, gates, cap),
            pltpu.VMEM((count, 2 * half, 2 * cap), BF16),
            pltpu.VMEM((count, 2 * cap, width), BF16),
            pltpu.SemaphoreType.DMA((count, 2)),
        ],
        flops=2**20,
        moved=2**14,
    )


def backward_kernel(distances, cap, sides, where, pipe, gates, weights, *refs):
    count, rows = len(distances), 2 * cap
    tokens, outs = refs[: 2 * count], refs[2 * count : 2 * count + len(sides)]
    block, block_sems, picked, target, place, slot_gates, buffer, sems = refs[
        2 * count + len(sides) :
    ]
    half, tile = tokens[0].shape[0], buffer.shape[1]
    tiles = 4 * len(sides)
    first = (1 - pipe[0] + sides[0]) * 4

    def weight_tile(n):
        return weights.at[pl.ds(pl.multiple_of((first + n) % 8 * tile, tile), tile), :]

    fetch = []
    for i, token in enumerate(tokens):
        to = block.at[i // 2, pl.ds(i % 2 * half, half), :]
        fetch.append(pltpu.make_async_copy(token, to, block_sems.at[i]))
        fetch[-1].start()
    stream = Stream(weight_tile, buffer, sems)
    for n in range(stream.slots):
        stream.start(n)
    place_slots(distances, where, gates, cap, target, place, slot_gates)
    for copy in fetch:
        copy.wait()

    @pl.loop(0, count)
    def _(i):
        for n in range(block.shape[2] // TILE):
            cols = pl.ds(n * TILE, TILE)
            picked[pl.ds(pl.multiple_of(i * rows, rows), rows), cols] = jnp.dot(
                place[i], block[i, :, cols], preferred_element_type=F32
            ).astype(BF16)

    @pl.loop(0, tiles)
    def _(n):
        stream.wait(n)
        value = lax.dot_general(
            picked[...],
            buffer[n % stream.slots],
            (((1,), (1,)), ((), ())),
            preferred_element_type=F32,
        )
        value = gated(value, slot_gates[...])
        cols = pl.ds(pl.multiple_of(n % 4 * tile, tile), tile)
        for i, out in enumerate(outs):

            @pl.when(n // 4 == i)
            def _():
                out[:, cols] = value

        @pl.when(n + stream.slots < tiles)
        def _():
            stream.start(n + stream.slots)


def backward(distances, cap, sides, where, pipe, tokens, gates, weights, share):
    count, rows = len(distances), 2 * cap
    depth, width = weights.shape
    return kernel_call(
        functools.partial(backward_kernel, distances, cap, sides),
        "backward",
        [(SMEM, where), (SMEM, pipe), (VMEM, gates), (HBM, weights)] + [(ANY, x) for x in tokens],
        [jax.ShapeDtypeStruct((count * rows, depth // 2), BF16)] * len(sides),
        [
            pltpu.VMEM((count, gates.shape[1], width), BF16),
            pltpu.SemaphoreType.DMA((2 * count,)),
            pltpu.VMEM((count * rows, width), BF16),
            *place_scratch(count, gates, cap),
            pltpu.VMEM((4, depth // 8, width), BF16),
            pltpu.SemaphoreType.DMA((4, 4)),
        ],
        flops=len(sides) * count * rows * depth * width // share,
        moved=2 * (depth * width + count * rows * (depth + 2 * width)) // share,
        limit=16,
    )


def collect_kernel(groups, where, *refs):
    out, held, sems = refs[-3:]
    copies = []
    for g, distances in enumerate(groups):
        hold, recv = refs[2 * g], refs[2 * g + 1]
        rows = hold.shape[0] // len(distances)
        for i, d in enumerate(distances):
            at, n = pl.ds(i * rows, rows), len(copies)
            held[n] = (hold[at, :].astype(F32) + recv[at, :].astype(F32)).astype(BF16)
            to = pl.ds(pl.multiple_of(where[d % 8] * rows, rows), rows)
            copies.append(pltpu.make_async_copy(held.at[n], out.at[to, :], sems.at[n]))
            copies[-1].start()
    for copy in copies:
        copy.wait()


def collect(groups, where, arrays, rows, into=None):
    count = sum(len(distances) for distances in groups)
    out = jax.ShapeDtypeStruct((rows, arrays[0].shape[1]), BF16)
    inputs = [(SMEM, where)] + [(VMEM, x) for x in arrays]
    if into is not None:
        inputs.append((HBM, into))
    in_specs, arrays = zip(*inputs)
    return pl.pallas_call(
        functools.partial(collect_kernel, groups),
        in_specs=in_specs,
        out_specs=HBM,
        out_shape=out,
        scratch_shapes=[
            pltpu.VMEM((count, rows // 8, out.shape[1]), BF16),
            pltpu.SemaphoreType.DMA((count,)),
        ],
        input_output_aliases={} if into is None else {len(inputs) - 1: 0},
        compiler_params=pltpu.CompilerParams(vmem_limit_bytes=9 * 2**20),
        cost_estimate=pl.CostEstimate(
            flops=2**20, bytes_accessed=6 * count * rows * 128, transcendentals=0
        ),
        name="collect",
    )(*arrays)


def on_device_16(hidden_a, expert_weights, routes_a, gates_a, cotangent_b, routes_b, gates_b):
    me = lax.axis_index("expert").astype(jnp.int32)
    z, y, c = me // 4, me // 2 % 2, me % 2
    pipe = lax.axis_index("pipe").astype(jnp.int32).reshape(1)
    rows = hidden_a.shape[1] // 8
    cap = rows // 2
    tokens, width = cotangent_b.shape
    weights, hidden = expert_weights[0], hidden_a[0]

    ring = (jnp.where(y == 0, z, 7 - z) + jnp.arange(8, dtype=jnp.int32)) % 8
    to_z, to_y = jnp.minimum(ring, 7 - ring), (ring > 3).astype(jnp.int32)
    chips = to_z * 2 + to_y
    where = jnp.concatenate([chips, c.reshape(1), (to_z ^ z) * 2 + (to_y ^ y)])

    got, pair = {0: cotangent_b}, {}
    got[-1], got[1] = step_ring(cotangent_b, 1), step_ring(cotangent_b, -1)

    both = gates_of(routes_a, gates_a, routes_b, gates_b)
    four = jnp.stack([both] + [xor(both, j) for j in (1, 2, 3)])
    four = lax.dynamic_index_in_dim(four.reshape(4, 4, 4, 2 * tokens), me % 4, 2, False)
    weights, four = tie(weights, four)
    raw1 = raw_forward(0, width // 2, pin(hidden), pin(weights))
    every = jnp.stack([four] + [xor(four, 4 * k) for k in (1, 2, 3)])
    raw1, weights, every, got[-1], got[1] = tie(raw1, weights, every, got[-1], got[1])
    weights = pin(weights)
    every = lax.dynamic_index_in_dim(every, z, 2, False)
    gate = jnp.moveaxis(every.reshape(8, 2, 2, tokens), 2, 0).reshape(2, 8, 2 * tokens)
    gate_a, gate_b = gate[0], gate[1]

    def spread(distances, split, gates):
        return spread_tokens(distances, split, cap, where, gates, (pin(raw1), pin(raw2)))

    def bwd(distances, sides=(0, 1), share=1):
        values = [x for d in distances for x in (got[d], pair[d])]
        return backward(distances, cap, sides, where, pipe, values, gate_b, weights, share)

    got[-2], got[2] = step_ring(got[-1], 1), step_ring(got[1], -1)
    for d in (0, -1, 1):
        pair[d] = core(got[d])
    raw2 = raw_forward(width // 2, width // 2, pin(hidden), weights)
    raw2, pair[0], pair[-1], pair[1] = tie(raw2, pair[0], pair[-1], pair[1])

    keep1, other1, other2 = spread((3, -4, 2, -3), 2, gate_a)
    keep1, other1, other2, got[-2], got[2] = tie(keep1, other1, other2, got[-2], got[2])
    got[-3], got[3] = step_ring(got[-2], 1), step_ring(got[2], -1)
    other1, other2 = core(other1), core(other2)
    up = step_ring(add(keep1[:tokens], other1[:tokens]), 1)
    down = step_ring(add(keep1[tokens : 2 * tokens], other1[tokens:]), -1)
    pair[-2] = core(got[-2])
    gate_a, pair[-2], other2 = tie(gate_a, pair[-2], other2)
    keep2, other3 = spread((1, -2, -1, 0), 4, gate_a)
    keep2, gate_b = tie(keep2, gate_b)
    groups = (0, -1, 1, -2), (2, -3, 3), (-4,)
    send1, hold1 = bwd(groups[0], share=64)

    def mine(i, *more):
        at = slice(i * tokens, (i + 1) * tokens)
        return add(keep2[at], other3[at], *more)

    send1, got[-3], got[3], up, down, other3 = tie(send1, got[-3], got[3], up, down, other3)
    got[-4] = step_ring(got[-3], 1)
    up = add(keep1[2 * tokens : 3 * tokens], other2[:tokens], up)
    down = add(keep1[3 * tokens :], other2[tokens:], down)
    up, down = tie(up, down)
    down = step_ring(down, -1)
    recv1 = across(send1)
    pair[2], pair[-3], pair[3] = core(got[2]), core(got[-3]), core(got[3])
    other3 = core(other3)
    gate_b, other3 = tie(gate_b, other3)
    send2, hold2 = bwd(groups[1], share=64)

    hold2, send2, up, down, got[-4] = tie(hold2, send2, up, down, got[-4])
    up, down = step_ring(up, 1), step_ring(mine(1, down), -1)
    pair[-4] = core(got[-4])
    recv2 = across(send2)
    send3, hold3 = bwd(groups[2], share=64)

    send3, hold3, up, down, recv1 = tie(send3, hold3, up, down, recv1)
    up, down = step_ring(mine(0, up), 1), step_ring(mine(2, down), -1)
    recv3 = across(send3)
    hold3, recv2 = tie(hold3, recv2)
    grad = collect(groups[:2], where, (hold1, recv1, hold2, recv2), 8 * rows)
    grad, recv3 = tie(grad, recv3)
    mixed_a = mine(3, up, down)
    grad = collect(groups[2:], where, (hold3, recv3), 8 * rows, grad)
    return (mixed_a, grad[None])


def solution(mesh):
    in_specs = (
        P("expert", None, None),
        P("expert", None, "pipe"),
        P("expert", None),
        P("expert", None),
        P("expert", "pipe"),
        P("expert", None),
        P("expert", None),
    )
    out_specs = (P("expert", "pipe"), P("expert", None, "pipe"))
    tailored = mesh.shape["expert"] == 16 and mesh.shape["pipe"] == 2
    return jax.shard_map(
        on_device_16 if tailored else on_device_any,
        mesh=mesh,
        in_specs=in_specs,
        out_specs=out_specs,
        check_vma=False,
    )
```
